32 devices in a mesh: grp: 2 (over y), blk: 16 (over z, x, core).
Axes of the slice: x: 2, y: 2, z: 4, core: 2. Of those that a mesh axis runs over, the one named last changes fastest.
Arguments:
- activations: bfloat16 [2, 4096, 256], P(None, ('grp', 'blk')), parts along dimension 1, may hold values from -6 to 6
- out_grads: bfloat16 [2, 4096, 256], P(None, ('grp', 'blk')), parts along dimension 1, may hold values from -6 to 6
- lengths: int32 [64], P(('grp', 'blk')), parts along dimension 0, may hold values from 8 to 64
- layer_ids: int32 [4], P('grp'), parts along dimension 0, may hold values from 0 to 15, as said below
- flagged: int32 [64], P('grp'), parts along dimension 0, may hold values from 0 to 31, each once
- act_factor: float32 [16, 256, 256], replicated, as said below
- grad_factor: float32 [16, 256, 256], replicated, as said below
Outputs:
- influence: float32 [64, 32], P(('grp', 'blk')), parts along dimension 0
The draws below stay inside these ranges and needn't reach their ends.
There are 2 independent parts, one for each index of `grp`. The reference program is written for one: setup_inputs(seed, part) draws one part's arguments, and reference() takes and returns one part's arrays. A program takes and returns all parts, laid end to end along the dimension named above; an argument that names none is the same for every part. Nothing has to cross between parts.
Inputs may be any that keep to these rules, and one draw needn't show every extreme that they name: `act_factor`: each stored factor is symmetric. `grad_factor`: each stored factor is symmetric. `layer_ids`: indices of stored layers.
All inputs are finite; a program needn't handle non-finite values.
Results may differ from the reference program's by a relative error of at most 0.0007.
Values may be sent and summed in bfloat16 or wider, within the bound.
No kernel may reach another device: no remote copies, remote signals or barrier semaphores. Data moves between devices by JAX's collectives and lax.ppermute only.
A program may use at most 128 MiB of HBM per device.

```python
import jax
import jax.numpy as jnp
from jax import lax

RANK = 256
SEQ_LEN = 64
LAYERS = 2
LAYERS_ALL = 16
SEQS = 32
TOKENS = 2048


def factor_draw(key, lower, upper, spread):
    first, second = jax.random.split(key)
    diagonal = jnp.exp(jax.random.uniform(first, (LAYERS_ALL, RANK), jnp.float32, jnp.log(lower), jnp.log(upper)))
    noise = jax.random.normal(second, (LAYERS_ALL, RANK, RANK), jnp.float32) * spread
    symmetric = 0.5 * (noise + jnp.transpose(noise, (0, 2, 1)))
    identity = jnp.eye(RANK, dtype=jnp.float32)
    return symmetric * (1.0 - identity) + identity * diagonal[:, :, None]


def draw_act_factor(key, part):
    key = jax.random.fold_in(key, 11)
    return factor_draw(key, 0.5, 2.0, 0.016)


def draw_grad_factor(key, part):
    key = jax.random.fold_in(key, 23)
    return factor_draw(key, 0.5, 2.0, 0.016)


def draw_layer_ids(key, part):
    key = jax.random.fold_in(key, 37)
    halves = jax.random.randint(key, (LAYERS,), 0, LAYERS_ALL // 2, jnp.int32)
    parity = (jnp.asarray(part).astype(jnp.int32) + jnp.arange(LAYERS, dtype=jnp.int32)) % 2
    return (2 * halves + parity).astype(jnp.int32)


def place_ends(drawn, stream_key, smallest, largest):
    longest = drawn.shape.index(max(drawn.shape))
    spots = []
    for shift in (0, 1):
        where = [jax.random.randint(jax.random.fold_in(stream_key, axis), (), 0, length) for axis, length in enumerate(drawn.shape)]
        where[longest] = (where[longest] + shift) % drawn.shape[longest]
        spots.append(tuple(where))
    return drawn.at[spots[0]].set(smallest).at[spots[1]].set(largest)


def block_scale(key, shape, pieces, least, high):
    def one(axis_at, shards_of):
        heights = jax.random.uniform(jax.random.fold_in(jax.random.fold_in(key, 6), axis_at), (shards_of,), jnp.float32, least / len(pieces), high / len(pieces))
        return jnp.repeat(jnp.exp(heights), shape[axis_at] // shards_of).reshape((-1,) + (1,) * (len(shape) - axis_at - 1))

    factor_of = one(*pieces[0])
    for cut in pieces[1:]:
        factor_of = factor_of * one(*cut)
    return factor_of


def normal_values(rng, extent, width, reach, shards=(), held_as=jnp.bfloat16):
    entries = width * jax.random.normal(rng, extent, jnp.float32)
    if shards:
        entries = entries * block_scale(rng, extent, shards, -0.22, 0.18)
    return jnp.clip(entries, -reach, reach).astype(held_as)


def setup_inputs(seed: int = 0, part: int = 0) -> dict:
    splits = jax.random.split(jax.random.key(seed), 8)
    own_keys = jax.random.split(jax.random.fold_in(splits[7], part), 8)
    activations = normal_values(own_keys[0], (LAYERS, TOKENS, RANK), 1.0, 6.0, ((1, 16),))
    out_grads = normal_values(own_keys[1], (LAYERS, TOKENS, RANK), 1.0, 6.0, ((1, 16),))
    lengths = place_ends(jax.random.randint(own_keys[2], (SEQS,), SEQ_LEN // 8, SEQ_LEN + 1), jax.random.fold_in(own_keys[2], 1), SEQ_LEN // 8, SEQ_LEN).astype(jnp.int32)
    layer_ids = draw_layer_ids(jax.random.fold_in(jax.random.fold_in(splits[7], part), 71), part)
    flagged = jax.random.permutation(own_keys[4], SEQS).astype(jnp.int32)
    act_factor = draw_act_factor(jax.random.fold_in(splits[7], 71), part)
    grad_factor = draw_grad_factor(jax.random.fold_in(splits[7], 71), part)
    return {"activations": activations, "out_grads": out_grads, "lengths": lengths, "layer_ids": layer_ids, "flagged": flagged, "act_factor": act_factor, "grad_factor": grad_factor}


def reference(activations, out_grads, lengths, layer_ids, flagged, act_factor, grad_factor):
    slots = jnp.arange(TOKENS) % SEQ_LEN
    keep = (slots < jnp.repeat(lengths, SEQ_LEN)).astype(jnp.bfloat16)
    masked_acts = activations * keep[None, :, None]
    masked_grads = out_grads * keep[None, :, None]
    picked_act = act_factor[layer_ids]
    picked_grad = grad_factor[layer_ids]
    white_acts = jnp.einsum("ltr,lrs->lts", masked_acts.astype(jnp.float32), picked_act, precision=lax.Precision.HIGHEST).astype(jnp.bfloat16)
    white_grads = jnp.einsum("ltr,lrs->lts", masked_grads.astype(jnp.float32), picked_grad, precision=lax.Precision.HIGHEST).astype(jnp.bfloat16)
    block_seqs = 8
    block_rows = block_seqs * SEQ_LEN
    all_acts = masked_acts.astype(jnp.float32)
    all_grads = masked_grads.astype(jnp.float32)
    scale = 1.0 / (RANK * SEQ_LEN)

    def row_block(index):
        start = (index * block_rows).astype(jnp.int32)
        query_acts = lax.dynamic_slice_in_dim(white_acts, start, block_rows, 1).astype(jnp.float32)
        query_grads = lax.dynamic_slice_in_dim(white_grads, start, block_rows, 1).astype(jnp.float32)
        gram_acts = jnp.einsum("lqr,lkr->lqk", query_acts, all_acts)
        gram_grads = jnp.einsum("lqr,lkr->lqk", query_grads, all_grads)
        pair = jnp.sum(gram_acts * gram_grads, axis=0)
        return pair.reshape(block_seqs, SEQ_LEN, SEQS, SEQ_LEN).sum(axis=(1, 3)) * scale

    scores = lax.map(row_block, jnp.arange(SEQS // block_seqs, dtype=jnp.int32))
    scores = scores.reshape(SEQS, SEQS)
    return jnp.take(scores, flagged, axis=1)
```

```python
import functools

import jax
import jax.numpy as jnp
from jax import lax
from jax.experimental import pallas as pl
from jax.experimental.pallas import tpu as pltpu
from jax.sharding import PartitionSpec as P

HIGHEST = lax.Precision.HIGHEST


def tile_scores(white_acts, white_grads, remote_acts, remote_grads, seq_len):
    gram_acts = jnp.einsum(
        "lqr,lkr->lqk", white_acts, remote_acts, preferred_element_type=jnp.float32
    )
    gram_grads = jnp.einsum(
        "lqr,lkr->lqk", white_grads, remote_grads, preferred_element_type=jnp.float32
    )
    pair = jnp.sum(gram_acts * gram_grads, axis=0)
    rows = pair.shape[0] // seq_len
    columns = pair.shape[1] // seq_len
    width = white_acts.shape[2]
    return pair.reshape(rows, seq_len, columns, seq_len).sum(axis=(1, 3)) * (
        1.0 / (width * seq_len)
    )


def gathered(activations, out_grads, lengths, layer_ids, flagged, act_factor, grad_factor):
    tok_rows = activations.shape[1]
    seq_count = lengths.shape[0]
    seq_len = tok_rows // seq_count
    slots = jnp.arange(tok_rows) % seq_len
    keep = (slots < jnp.repeat(lengths, seq_len)).astype(jnp.bfloat16)
    masked_acts = activations * keep[None, :, None]
    masked_grads = out_grads * keep[None, :, None]
    picked_act = jnp.take(act_factor, layer_ids, axis=0)
    picked_grad = jnp.take(grad_factor, layer_ids, axis=0)
    white_acts = jnp.einsum(
        "ltr,lrs->lts", masked_acts.astype(jnp.float32), picked_act, precision=HIGHEST
    ).astype(jnp.bfloat16)
    white_grads = jnp.einsum(
        "ltr,lrs->lts", masked_grads.astype(jnp.float32), picked_grad, precision=HIGHEST
    ).astype(jnp.bfloat16)
    part_scores = tile_scores(
        white_acts,
        white_grads,
        lax.all_gather(masked_acts, "blk", axis=1, tiled=True),
        lax.all_gather(masked_grads, "blk", axis=1, tiled=True),
        seq_len,
    )
    return jnp.take(part_scores, flagged, axis=1)


def z_near(d):
    return d ^ 4 ^ ((d >> 1) & 1)


def prep_kernel(seq_len, lens, acts, grads, own, away):
    half = lax.axis_index("blk") // 8
    row = lax.broadcasted_iota(jnp.int32, (acts.shape[1], 1), 0)
    bound = jnp.zeros_like(row)
    for s in range(lens.shape[0]):
        bound = jnp.where(row // seq_len == s, lens[s] + s * seq_len, bound)
    keep = row < bound
    for index, src in enumerate((acts, grads)):
        for layer, dst in ((half, own), (1 - half, away)):
            x = src[layer]
            dst[index] = jnp.where(keep, x, jnp.zeros_like(x))


def prep(activations, out_grads, lengths, seq_len):
    unit = jax.ShapeDtypeStruct((2,) + activations.shape[1:], activations.dtype)
    vmem = pl.BlockSpec(memory_space=pltpu.VMEM)
    return pl.pallas_call(
        functools.partial(prep_kernel, seq_len),
        out_shape=(unit, unit),
        in_specs=[pl.BlockSpec(memory_space=pltpu.SMEM), vmem, vmem],
        out_specs=(vmem, vmem),
        name="mask_units",
    )(lengths, activations, out_grads)


def whiten(x, factor):
    total = None
    rest = factor
    for _ in range(3):
        term = rest.astype(jnp.bfloat16)
        rest = rest - term.astype(jnp.float32)
        part = jnp.dot(x, term, preferred_element_type=jnp.float32)
        total = part if total is None else total + part
    return total.astype(jnp.bfloat16)


def score_kernel(seq_len, layer_ids, flagged, act_f, grad_f, *refs):
    units, out = refs[:8], refs[8]
    rank = units[0].shape[2]
    d = lax.axis_index("blk")
    f32 = jnp.float32
    toks = [
        [jnp.concatenate([units[2 * i][w], units[2 * i + 1][w]], axis=0) for w in range(2)]
        for i in range(4)
    ]
    factors = (act_f[0], grad_f[0])
    white = [[whiten(toks[i][w], factors[w]) for w in range(2)] for i in range(3)]
    rows = toks[0][0].shape[0]
    seqs = rows // seq_len
    zeros = jnp.zeros((seqs, rows), f32)
    sums = []
    for i in range(4):
        line = []
        for j in range(4):
            if i < 3 and (j > i or i == 0) and not (i == 1 and j < 2):
                grams = [
                    lax.dot_general(
                        white[i][w], toks[j][w], (((1,), (1,)), ((), ())), preferred_element_type=f32
                    )
                    for w in range(2)
                ]
                pair = grams[0] * grams[1]
                line.append(pair.reshape(seqs, seq_len, rows).sum(axis=1))
            else:
                line.append(zeros)
        sums.append(jnp.concatenate(line, axis=1))
    sums = jnp.concatenate(sums, axis=0)
    n = 4 * seqs
    tok = lax.broadcasted_iota(jnp.int32, (4 * rows, n), 0)
    col = lax.broadcasted_iota(jnp.int32, (4 * rows, n), 1)
    fold = jnp.where(tok // seq_len == col, 1.0 / (rank * seq_len), 0.0).astype(f32)
    local = jnp.dot(sums, fold, precision=HIGHEST, preferred_element_type=f32)
    r = lax.broadcasted_iota(jnp.int32, (n, n), 0) // seqs
    c = lax.broadcasted_iota(jnp.int32, (n, n), 1) // seqs
    diagonal = jnp.where((r == 2) & (c == 3), local, 0.0)
    place = lax.broadcasted_iota(jnp.int32, (n, flagged.shape[1]), 0)
    per = seqs // 2
    spot = place // per
    slot = spot // 2
    owner = jnp.where(slot == 0, d, jnp.where(slot == 1, d ^ 1, jnp.where(slot == 2, d ^ 2, z_near(d))))
    owner = owner ^ (8 * (spot % 2))
    seq = owner * per + place % per
    pick = jnp.where(seq == flagged[...], 1.0, 0.0).astype(f32)
    picked = jnp.dot(local, pick, precision=HIGHEST, preferred_element_type=f32)
    picked = picked + lax.dot_general(
        diagonal, pick, (((0,), (0,)), ((), ())), precision=HIGHEST, preferred_element_type=f32
    )
    out[...] = jnp.zeros_like(out)
    for i, base in enumerate((d, d ^ 1, d ^ 2, z_near(d))):
        for j in range(2):
            at = (2 * i + j) * per
            out[base ^ (8 * j)] = picked[at : at + per]


def score(units, layer_ids, flagged, act_factor, grad_factor, seq_len, size):
    rank = units[0].shape[2]
    per = units[0].shape[1] // seq_len
    vmem = pl.BlockSpec(memory_space=pltpu.VMEM)
    factor = pl.BlockSpec(
        (1, rank, rank), lambda i, ids: (ids[lax.axis_index("blk") // 8], 0, 0)
    )
    return pl.pallas_call(
        functools.partial(score_kernel, seq_len),
        out_shape=jax.ShapeDtypeStruct((size, per, flagged.shape[0]), jnp.float32),
        grid_spec=pltpu.PrefetchScalarGridSpec(
            num_scalar_prefetch=1,
            grid=(1,),
            in_specs=[pl.BlockSpec((1, flagged.shape[0]), lambda i, ids: (0, 0)), factor, factor] + [vmem] * 8,
            out_specs=vmem,
        ),
        compiler_params=pltpu.CompilerParams(vmem_limit_bytes=48 * 1024 * 1024),
        name="pair_scores",
    )(layer_ids, flagged.reshape(1, -1), act_factor, grad_factor, *units)


def paired(activations, out_grads, lengths, layer_ids, flagged, act_factor, grad_factor):
    size = 16
    seq_len = activations.shape[1] // lengths.shape[0]
    own, away = prep(activations, out_grads, lengths, seq_len)

    def send(x, to):
        return lax.ppermute(x, "blk", [(d, to(d)) for d in range(size)])

    ways = (lambda d: d ^ 1, lambda d: d ^ 2, z_near)
    opposite = send(away, lambda d: d ^ 8)
    near = [send(own, to) for to in ways]
    far = [send(opposite, to) for to in ways]
    units = [own, opposite]
    for a, b in zip(near, far):
        units += [a, b]
    parts = score(units, layer_ids, flagged, act_factor, grad_factor, seq_len, size)
    back = lax.all_to_all(parts, "blk", 0, 0, tiled=True)
    return jnp.sum(back, axis=0)


def solution(mesh):
    in_specs = (
        P(None, ("grp", "blk"), None),
        P(None, ("grp", "blk"), None),
        P(("grp", "blk")),
        P("grp"),
        P("grp"),
        P(),
        P(),
    )
    out_specs = P(("grp", "blk"), None)
    shards = paired if mesh.shape["blk"] == 16 else gathered
    return jax.shard_map(shards, mesh=mesh, in_specs=in_specs, out_specs=out_specs, check_vma=False)
```

```python
import functools

import jax
import jax.numpy as jnp
from jax import lax
from jax.experimental import pallas as pl
from jax.experimental.pallas import tpu as pltpu
from jax.sharding import PartitionSpec as P

HIGHEST = lax.Precision.HIGHEST


def tile_scores(white_acts, white_grads, remote_acts, remote_grads, seq_len):
    gram_acts = jnp.einsum(
        "lqr,lkr->lqk", white_acts, remote_acts, preferred_element_type=jnp.float32
    )
    gram_grads = jnp.einsum(
        "lqr,lkr->lqk", white_grads, remote_grads, preferred_element_type=jnp.float32
    )
    pair = jnp.sum(gram_acts * gram_grads, axis=0)
    rows = pair.shape[0] // seq_len
    columns = pair.shape[1] // seq_len
    width = white_acts.shape[2]
    return pair.reshape(rows, seq_len, columns, seq_len).sum(axis=(1, 3)) * (
        1.0 / (width * seq_len)
    )


def gathered(activations, out_grads, lengths, layer_ids, flagged, act_factor, grad_factor):
    tok_rows = activations.shape[1]
    seq_count = lengths.shape[0]
    seq_len = tok_rows // seq_count
    slots = jnp.arange(tok_rows) % seq_len
    keep = (slots < jnp.repeat(lengths, seq_len)).astype(jnp.bfloat16)
    masked_acts = activations * keep[None, :, None]
    masked_grads = out_grads * keep[None, :, None]
    picked_act = jnp.take(act_factor, layer_ids, axis=0)
    picked_grad = jnp.take(grad_factor, layer_ids, axis=0)
    white_acts = jnp.einsum(
        "ltr,lrs->lts", masked_acts.astype(jnp.float32), picked_act, precision=HIGHEST
    ).astype(jnp.bfloat16)
    white_grads = jnp.einsum(
        "ltr,lrs->lts", masked_grads.astype(jnp.float32), picked_grad, precision=HIGHEST
    ).astype(jnp.bfloat16)
    part_scores = tile_scores(
        white_acts,
        white_grads,
        lax.all_gather(masked_acts, "blk", axis=1, tiled=True),
        lax.all_gather(masked_grads, "blk", axis=1, tiled=True),
        seq_len,
    )
    return jnp.take(part_scores, flagged, axis=1)


def z_near(d):
    return d ^ 4 ^ ((d >> 1) & 1)


def prep_kernel(seq_len, lens, acts, grads, own, away):
    half = lax.axis_index("blk") // 8
    row = lax.broadcasted_iota(jnp.int32, (acts.shape[1], 1), 0)
    bound = jnp.zeros_like(row)
    for s in range(lens.shape[0]):
        bound = jnp.where(row // seq_len == s, lens[s] + s * seq_len, bound)
    keep = row < bound
    for index, src in enumerate((acts, grads)):
        for layer, dst in ((half, own), (1 - half, away)):
            x = src[layer]
            dst[index] = jnp.where(keep, x, jnp.zeros_like(x))


def prep(activations, out_grads, lengths, seq_len):
    unit = jax.ShapeDtypeStruct((2,) + activations.shape[1:], activations.dtype)
    vmem = pl.BlockSpec(memory_space=pltpu.VMEM)
    return pl.pallas_call(
        functools.partial(prep_kernel, seq_len),
        out_shape=(unit, unit),
        in_specs=[pl.BlockSpec(memory_space=pltpu.SMEM), vmem, vmem],
        out_specs=(vmem, vmem),
        compiler_params=pltpu.CompilerParams(vmem_limit_bytes=59 * 1024 * 1024),
        name="mask_units",
    )(lengths, activations, out_grads)


def setup_kernel(seq_len, per, layer_ids, flagged, act_f, grad_f, terms, pick, factor, sems):
    d = lax.axis_index("blk")
    layer = layer_ids[d // 8]
    copies = [
        pltpu.make_async_copy(src.at[layer], factor.at[i], sems.at[i])
        for i, src in enumerate((act_f, grad_f))
    ]
    for copy in copies:
        copy.start()
    token = lax.broadcasted_iota(jnp.int32, pick.shape, 0)
    spot = token // (seq_len * per)
    slot = spot // 2
    owner = jnp.where(
        slot == 0, d, jnp.where(slot == 1, d ^ 1, jnp.where(slot == 2, d ^ 2, z_near(d)))
    )
    owner = owner ^ (8 * (spot % 2))
    seq = owner * per + token // seq_len % per
    scale = 1.0 / (factor.shape[1] * seq_len)
    pick[...] = jnp.where(seq == flagged[...], scale, 0.0).astype(pick.dtype)
    for i, copy in enumerate(copies):
        copy.wait()
        rest = factor[i]
        for n in range(3):
            term = rest.astype(jnp.bfloat16)
            terms[i, n] = term
            rest = rest - term.astype(jnp.float32)


def setup(layer_ids, flagged, act_factor, grad_factor, seq_len, per):
    rank = act_factor.shape[1]
    vmem = pl.BlockSpec(memory_space=pltpu.VMEM)
    hbm = pl.BlockSpec(memory_space=pltpu.HBM)
    return pl.pallas_call(
        functools.partial(setup_kernel, seq_len, per),
        out_shape=(
            jax.ShapeDtypeStruct((2, 3, rank, rank), jnp.bfloat16),
            jax.ShapeDtypeStruct((8 * per * seq_len, flagged.shape[0]), jnp.bfloat16),
        ),
        in_specs=[pl.BlockSpec(memory_space=pltpu.SMEM), vmem, hbm, hbm],
        out_specs=(vmem, vmem),
        scratch_shapes=[pltpu.VMEM((2, rank, rank), jnp.float32), pltpu.SemaphoreType.DMA((2,))],
        compiler_params=pltpu.CompilerParams(vmem_limit_bytes=59 * 1024 * 1024),
        cost_estimate=pl.CostEstimate(flops=10**9, bytes_accessed=2 * 10**6, transcendentals=0),
        name="factor_terms",
    )(layer_ids, flagged.reshape(1, -1), act_factor, grad_factor)


def whiten(x, terms):
    total = jnp.dot(x, terms[0], preferred_element_type=jnp.float32)
    for n in (1, 2):
        total = total + jnp.dot(x, terms[n], preferred_element_type=jnp.float32)
    return total.astype(jnp.bfloat16)


def score_kernel(seq_len, terms, pick, *refs):
    units, outs = refs[:8], refs[8:]
    f32 = jnp.float32
    toks = [
        [jnp.concatenate([units[2 * i][w], units[2 * i + 1][w]], axis=0) for w in range(2)]
        for i in range(4)
    ]
    white = [[whiten(toks[i][w], terms.at[w]) for w in range(2)] for i in range(3)]
    rows = toks[0][0].shape[0]
    seqs = rows // seq_len

    def block(left, right):
        grams = [
            lax.dot_general(a, b, (((1,), (1,)), ((), ())), preferred_element_type=f32)
            for a, b in zip(left, right)
        ]
        return (grams[0] * grams[1]).reshape(seqs, seq_len, rows).sum(axis=1)

    zeros = jnp.zeros((seqs, rows), f32)
    lines = [
        [block(white[0], toks[j]) for j in range(4)],
        [zeros, zeros] + [block(white[1], toks[j]) for j in (2, 3)],
        [zeros, zeros, zeros, block(white[2], toks[3])],
        [zeros, zeros, block(toks[3], white[2]), zeros],
    ]
    rest = jnp.concatenate([jnp.concatenate(line, axis=1) for line in lines], axis=0)
    n = rest.shape[0]
    parts = []
    for _ in range(3):
        part = rest.astype(jnp.bfloat16)
        parts.append(part)
        rest = rest - part.astype(f32)
    picked = jnp.dot(jnp.concatenate(parts, axis=0), pick[...], preferred_element_type=f32)
    picked = picked[:n] + picked[n : 2 * n] + picked[2 * n :]
    per = n // 8
    for i, out in enumerate(outs):
        out[...] = picked[i * per : (i + 1) * per]


def score(units, terms, pick, seq_len):
    per = units[0].shape[1] // seq_len
    vmem = pl.BlockSpec(memory_space=pltpu.VMEM)
    return pl.pallas_call(
        functools.partial(score_kernel, seq_len),
        out_shape=[jax.ShapeDtypeStruct((per, pick.shape[1]), jnp.float32)] * 8,
        in_specs=[vmem] * 10,
        out_specs=[vmem] * 8,
        compiler_params=pltpu.CompilerParams(vmem_limit_bytes=40 * 1024 * 1024),
        cost_estimate=pl.CostEstimate(flops=2 * 10**9, bytes_accessed=2 * 10**6, transcendentals=0),
        name="pair_scores",
    )(terms, pick, *units)


def paired(activations, out_grads, lengths, layer_ids, flagged, act_factor, grad_factor):
    size = 16
    per = lengths.shape[0]
    seq_len = activations.shape[1] // per
    own, away = prep(activations, out_grads, lengths, seq_len)

    def send(x, to):
        return lax.ppermute(x, "blk", [(d, to(d)) for d in range(size)])

    ways = (lambda d: d ^ 1, lambda d: d ^ 2, z_near)
    opposite = send(away, lambda d: d ^ 8)
    near = [send(own, to) for to in ways]
    terms, pick = setup(layer_ids, flagged, act_factor, grad_factor, seq_len, per)
    opposite, terms, pick = lax.optimization_barrier((opposite, terms, pick))
    far = [send(opposite, to) for to in ways]
    units = [own, opposite]
    for a, b in zip(near, far):
        units += [a, b]
    parts = score(units, terms, pick, seq_len)
    total = parts[0] + send(parts[1], lambda d: d ^ 8)
    for i, to in enumerate(ways):
        total = total + send(parts[2 * i + 2], to)
        total = total + send(parts[2 * i + 3], lambda d, to=to: to(d) ^ 8)
    return total


def solution(mesh):
    in_specs = (
        P(None, ("grp", "blk"), None),
        P(None, ("grp", "blk"), None),
        P(("grp", "blk")),
        P("grp"),
        P("grp"),
        P(),
        P(),
    )
    out_specs = P(("grp", "blk"), None)
    shards = paired if mesh.shape["blk"] == 16 else gathered
    return jax.shard_map(shards, mesh=mesh, in_specs=in_specs, out_specs=out_specs, check_vma=False)
```

```python
import functools

import jax
import jax.numpy as jnp
from jax import lax
from jax.experimental import pallas as pl
from jax.experimental.pallas import tpu as pltpu
from jax.sharding import PartitionSpec as P

HIGHEST = lax.Precision.HIGHEST


def tile_scores(white_acts, white_grads, remote_acts, remote_grads, seq_len):
    gram_acts = jnp.einsum(
        "lqr,lkr->lqk", white_acts, remote_acts, preferred_element_type=jnp.float32
    )
    gram_grads = jnp.einsum(
        "lqr,lkr->lqk", white_grads, remote_grads, preferred_element_type=jnp.float32
    )
    pair = jnp.sum(gram_acts * gram_grads, axis=0)
    rows = pair.shape[0] // seq_len
    columns = pair.shape[1] // seq_len
    width = white_acts.shape[2]
    return pair.reshape(rows, seq_len, columns, seq_len).sum(axis=(1, 3)) * (
        1.0 / (width * seq_len)
    )


def gathered(activations, out_grads, lengths, layer_ids, flagged, act_factor, grad_factor):
    tok_rows = activations.shape[1]
    seq_count = lengths.shape[0]
    seq_len = tok_rows // seq_count
    slots = jnp.arange(tok_rows) % seq_len
    keep = (slots < jnp.repeat(lengths, seq_len)).astype(jnp.bfloat16)
    masked_acts = activations * keep[None, :, None]
    masked_grads = out_grads * keep[None, :, None]
    picked_act = jnp.take(act_factor, layer_ids, axis=0)
    picked_grad = jnp.take(grad_factor, layer_ids, axis=0)
    white_acts = jnp.einsum(
        "ltr,lrs->lts", masked_acts.astype(jnp.float32), picked_act, precision=HIGHEST
    ).astype(jnp.bfloat16)
    white_grads = jnp.einsum(
        "ltr,lrs->lts", masked_grads.astype(jnp.float32), picked_grad, precision=HIGHEST
    ).astype(jnp.bfloat16)
    part_scores = tile_scores(
        white_acts,
        white_grads,
        lax.all_gather(masked_acts, "blk", axis=1, tiled=True),
        lax.all_gather(masked_grads, "blk", axis=1, tiled=True),
        seq_len,
    )
    return jnp.take(part_scores, flagged, axis=1)


def z_near(d):
    return d ^ 4 ^ ((d >> 1) & 1)


def prep_kernel(seq_len, lens, acts, grads, own, away):
    half = lax.axis_index("blk") // 8
    row = lax.broadcasted_iota(jnp.int32, (acts.shape[1], 1), 0)
    bound = jnp.zeros_like(row)
    for s in range(lens.shape[0]):
        bound = jnp.where(row // seq_len == s, lens[s] + s * seq_len, bound)
    keep = row < bound
    for index, src in enumerate((acts, grads)):
        for layer, dst in ((half, own), (1 - half, away)):
            x = src[layer]
            dst[index] = jnp.where(keep, x, jnp.zeros_like(x))


def prep(activations, out_grads, lengths, seq_len):
    unit = jax.ShapeDtypeStruct((2,) + activations.shape[1:], activations.dtype)
    vmem = pl.BlockSpec(memory_space=pltpu.VMEM)
    return pl.pallas_call(
        functools.partial(prep_kernel, seq_len),
        out_shape=(unit, unit),
        in_specs=[pl.BlockSpec(memory_space=pltpu.SMEM), vmem, vmem],
        out_specs=(vmem, vmem),
        compiler_params=pltpu.CompilerParams(vmem_limit_bytes=59 * 1024 * 1024),
        name="mask_units",
    )(lengths, activations, out_grads)


def setup_kernel(seq_len, per, layer_ids, flagged, act_f, grad_f, terms, pick, factor, sems):
    d = lax.axis_index("blk")
    layer = layer_ids[d // 8]
    copies = [
        pltpu.make_async_copy(src.at[layer], factor.at[i], sems.at[i])
        for i, src in enumerate((act_f, grad_f))
    ]
    for copy in copies:
        copy.start()
    token = lax.broadcasted_iota(jnp.int32, pick.shape, 0)
    spot = token // (seq_len * per)
    slot = spot // 2
    owner = jnp.where(
        slot == 0, d, jnp.where(slot == 1, d ^ 1, jnp.where(slot == 2, d ^ 2, z_near(d)))
    )
    owner = owner ^ (8 * (spot % 2))
    seq = owner * per + token // seq_len % per
    scale = 1.0 / (factor.shape[1] * seq_len)
    pick[...] = jnp.where(seq == flagged[...], scale, 0.0).astype(pick.dtype)
    for i, copy in enumerate(copies):
        copy.wait()
        rest = factor[i]
        for n in range(3):
            term = rest.astype(jnp.bfloat16)
            terms[i, n] = term
            rest = rest - term.astype(jnp.float32)


def setup(layer_ids, flagged, act_factor, grad_factor, seq_len, per):
    rank = act_factor.shape[1]
    vmem = pl.BlockSpec(memory_space=pltpu.VMEM)
    hbm = pl.BlockSpec(memory_space=pltpu.HBM)
    return pl.pallas_call(
        functools.partial(setup_kernel, seq_len, per),
        out_shape=(
            jax.ShapeDtypeStruct((2, 3, rank, rank), jnp.bfloat16),
            jax.ShapeDtypeStruct((8 * per * seq_len, flagged.shape[0]), jnp.bfloat16),
        ),
        in_specs=[pl.BlockSpec(memory_space=pltpu.SMEM), vmem, hbm, hbm],
        out_specs=(vmem, vmem),
        scratch_shapes=[pltpu.VMEM((2, rank, rank), jnp.float32), pltpu.SemaphoreType.DMA((2,))],
        compiler_params=pltpu.CompilerParams(vmem_limit_bytes=51 * 1024 * 1024),
        cost_estimate=pl.CostEstimate(flops=10**9, bytes_accessed=2 * 10**6, transcendentals=0),
        name="factor_terms",
    )(layer_ids, flagged.reshape(1, -1), act_factor, grad_factor)


def whiten(x, terms):
    total = jnp.dot(x, terms[0], preferred_element_type=jnp.float32)
    for n in (1, 2):
        total = total + jnp.dot(x, terms[n], preferred_element_type=jnp.float32)
    return total.astype(jnp.bfloat16)


def score_kernel(seq_len, terms, pick, *refs):
    units, outs = refs[:8], refs[8:]
    f32 = jnp.float32
    toks = [
        [jnp.concatenate([units[2 * i][w], units[2 * i + 1][w]], axis=0) for w in range(2)]
        for i in range(4)
    ]
    white = {i: [whiten(toks[i][w], terms.at[w]) for w in range(2)] for i in (0, 2, 3)}
    rows = toks[0][0].shape[0]
    seqs = rows // seq_len

    def block(left, right):
        grams = [
            lax.dot_general(a, b, (((1,), (1,)), ((), ())), preferred_element_type=f32)
            for a, b in zip(left, right)
        ]
        return (grams[0] * grams[1]).reshape(seqs, seq_len, rows).sum(axis=1)

    zeros = jnp.zeros((seqs, rows), f32)
    lines = [
        [block(white[0], toks[j]) for j in range(4)],
        [zeros, block(white[2], toks[1]), zeros, block(white[2], toks[3])],
        [zeros, block(white[3], toks[1]), block(white[3], toks[2]), zeros],
    ]
    rest = jnp.concatenate([jnp.concatenate(line, axis=1) for line in lines], axis=0)
    n = rest.shape[0]
    parts = []
    for _ in range(3):
        part = rest.astype(jnp.bfloat16)
        parts.append(part)
        rest = rest - part.astype(f32)
    picked = jnp.dot(jnp.concatenate(parts, axis=0), pick[...], preferred_element_type=f32)
    picked = picked[:n] + picked[n : 2 * n] + picked[2 * n :]
    for i, out in enumerate(outs):
        out[...] = picked[i * seqs : (i + 1) * seqs]


def score(units, terms, pick, seq_len):
    seqs = 2 * units[0].shape[1] // seq_len
    vmem = pl.BlockSpec(memory_space=pltpu.VMEM)
    return pl.pallas_call(
        functools.partial(score_kernel, seq_len),
        out_shape=[jax.ShapeDtypeStruct((seqs, pick.shape[1]), jnp.float32)] * 3,
        in_specs=[vmem] * 10,
        out_specs=[vmem] * 3,
        compiler_params=pltpu.CompilerParams(vmem_limit_bytes=40 * 1024 * 1024),
        cost_estimate=pl.CostEstimate(flops=2 * 10**9, bytes_accessed=2 * 10**6, transcendentals=0),
        name="pair_scores",
    )(terms, pick, *units)


def paired(activations, out_grads, lengths, layer_ids, flagged, act_factor, grad_factor):
    size = 16
    per = lengths.shape[0]
    seq_len = activations.shape[1] // per
    own, away = prep(activations, out_grads, lengths, seq_len)

    def send(x, to):
        return lax.ppermute(x, "blk", [(d, to(d)) for d in range(size)])

    ways = (lambda d: d ^ 1, lambda d: d ^ 2, z_near)
    opposite = send(away, lambda d: d ^ 8)
    near = [send(own, to) for to in ways]
    terms, pick = setup(layer_ids, flagged, act_factor, grad_factor, seq_len, per)
    opposite, terms, pick = lax.optimization_barrier((opposite, terms, pick))
    far = [send(opposite, to) for to in ways]
    units = [own, opposite]
    for a, b in zip(near, far):
        units += [a, b]
    mine, by_x, by_z = score(units, terms, pick, seq_len)
    half_sum = mine + send(by_x, lambda d: d ^ 2) + send(by_z, z_near)
    return half_sum[:per] + send(half_sum[per:], lambda d: d ^ 8)


def solution(mesh):
    in_specs = (
        P(None, ("grp", "blk"), None),
        P(None, ("grp", "blk"), None),
        P(("grp", "blk")),
        P("grp"),
        P("grp"),
        P(),
        P(),
    )
    out_specs = P(("grp", "blk"), None)
    shards = paired if mesh.shape["blk"] == 16 else gathered
    return jax.shard_map(shards, mesh=mesh, in_specs=in_specs, out_specs=out_specs, check_vma=False)
```

```python
import functools

import jax
import jax.numpy as jnp
from jax import lax
from jax.experimental import pallas as pl
from jax.experimental.pallas import tpu as pltpu
from jax.sharding import PartitionSpec as P

HIGHEST = lax.Precision.HIGHEST


def tile_scores(white_acts, white_grads, remote_acts, remote_grads, seq_len):
    gram_acts = jnp.einsum(
        "lqr,lkr->lqk", white_acts, remote_acts, preferred_element_type=jnp.float32
    )
    gram_grads = jnp.einsum(
        "lqr,lkr->lqk", white_grads, remote_grads, preferred_element_type=jnp.float32
    )
    pair = jnp.sum(gram_acts * gram_grads, axis=0)
    rows = pair.shape[0] // seq_len
    columns = pair.shape[1] // seq_len
    width = white_acts.shape[2]
    return pair.reshape(rows, seq_len, columns, seq_len).sum(axis=(1, 3)) * (
        1.0 / (width * seq_len)
    )


def gathered(activations, out_grads, lengths, layer_ids, flagged, act_factor, grad_factor):
    tok_rows = activations.shape[1]
    seq_count = lengths.shape[0]
    seq_len = tok_rows // seq_count
    slots = jnp.arange(tok_rows) % seq_len
    keep = (slots < jnp.repeat(lengths, seq_len)).astype(jnp.bfloat16)
    masked_acts = activations * keep[None, :, None]
    masked_grads = out_grads * keep[None, :, None]
    picked_act = jnp.take(act_factor, layer_ids, axis=0)
    picked_grad = jnp.take(grad_factor, layer_ids, axis=0)
    white_acts = jnp.einsum(
        "ltr,lrs->lts", masked_acts.astype(jnp.float32), picked_act, precision=HIGHEST
    ).astype(jnp.bfloat16)
    white_grads = jnp.einsum(
        "ltr,lrs->lts", masked_grads.astype(jnp.float32), picked_grad, precision=HIGHEST
    ).astype(jnp.bfloat16)
    part_scores = tile_scores(
        white_acts,
        white_grads,
        lax.all_gather(masked_acts, "blk", axis=1, tiled=True),
        lax.all_gather(masked_grads, "blk", axis=1, tiled=True),
        seq_len,
    )
    return jnp.take(part_scores, flagged, axis=1)


def z_near(d):
    return d ^ 4 ^ ((d >> 1) & 1)


def prep_kernel(seq_len, lens, acts, grads, own, away):
    half = lax.axis_index("blk") // 8
    row = lax.broadcasted_iota(jnp.int32, (acts.shape[1], 1), 0)
    bound = jnp.zeros_like(row)
    for s in range(lens.shape[0]):
        bound = jnp.where(row // seq_len == s, lens[s] + s * seq_len, bound)
    keep = row < bound
    for index, src in enumerate((acts, grads)):
        for layer, dst in ((half, own), (1 - half, away)):
            x = src[layer]
            dst[index] = jnp.where(keep, x, jnp.zeros_like(x))


def prep(activations, out_grads, lengths, seq_len):
    unit = jax.ShapeDtypeStruct((2,) + activations.shape[1:], activations.dtype)
    vmem = pl.BlockSpec(memory_space=pltpu.VMEM)
    return pl.pallas_call(
        functools.partial(prep_kernel, seq_len),
        out_shape=(unit, unit),
        in_specs=[pl.BlockSpec(memory_space=pltpu.SMEM), vmem, vmem],
        out_specs=(vmem, vmem),
        compiler_params=pltpu.CompilerParams(vmem_limit_bytes=59 * 1024 * 1024),
        name="mask_units",
    )(lengths, activations, out_grads)


def setup_kernel(seq_len, per, layer_ids, flagged, act_f, grad_f, terms, pick, factor, sems):
    d = lax.axis_index("blk")
    layer = layer_ids[d // 8]
    copies = [
        pltpu.make_async_copy(src.at[layer], factor.at[i], sems.at[i])
        for i, src in enumerate((act_f, grad_f))
    ]
    for copy in copies:
        copy.start()
    token = lax.broadcasted_iota(jnp.int32, pick.shape, 0)
    spot = token // (seq_len * per)
    slot = spot // 2
    owner = jnp.where(
        slot == 0, d, jnp.where(slot == 1, d ^ 1, jnp.where(slot == 2, d ^ 2, z_near(d)))
    )
    owner = owner ^ (8 * (spot % 2))
    seq = owner * per + token // seq_len % per
    scale = 1.0 / (factor.shape[1] * seq_len)
    pick[...] = jnp.where(seq == flagged[...], scale, 0.0).astype(pick.dtype)
    for i, copy in enumerate(copies):
        copy.wait()
        rest = factor[i]
        for n in range(3):
            term = rest.astype(jnp.bfloat16)
            terms[i, n] = term
            rest = rest - term.astype(jnp.float32)


def setup(layer_ids, flagged, act_factor, grad_factor, seq_len, per):
    rank = act_factor.shape[1]
    vmem = pl.BlockSpec(memory_space=pltpu.VMEM)
    hbm = pl.BlockSpec(memory_space=pltpu.HBM)
    return pl.pallas_call(
        functools.partial(setup_kernel, seq_len, per),
        out_shape=(
            jax.ShapeDtypeStruct((2, 3, rank, rank), jnp.bfloat16),
            jax.ShapeDtypeStruct((8 * per * seq_len, flagged.shape[0]), jnp.bfloat16),
        ),
        in_specs=[pl.BlockSpec(memory_space=pltpu.SMEM), vmem, hbm, hbm],
        out_specs=(vmem, vmem),
        scratch_shapes=[pltpu.VMEM((2, rank, rank), jnp.float32), pltpu.SemaphoreType.DMA((2,))],
        compiler_params=pltpu.CompilerParams(vmem_limit_bytes=51 * 1024 * 1024),
        cost_estimate=pl.CostEstimate(flops=10**9, bytes_accessed=2 * 10**6, transcendentals=0),
        name="factor_terms",
    )(layer_ids, flagged.reshape(1, -1), act_factor, grad_factor)


def whiten(x, terms):
    total = jnp.dot(x, terms[0], preferred_element_type=jnp.float32)
    for n in (1, 2):
        total = total + jnp.dot(x, terms[n], preferred_element_type=jnp.float32)
    return total.astype(jnp.bfloat16)


def score_kernel(seq_len, terms, pick, *refs):
    units, out = refs[:8], refs[8]
    f32 = jnp.float32
    toks = [
        [jnp.concatenate([units[2 * i][w], units[2 * i + 1][w]], axis=0) for w in range(2)]
        for i in range(4)
    ]
    white = {i: [whiten(toks[i][w], terms.at[w]) for w in range(2)] for i in (0, 2, 3)}
    rows = toks[0][0].shape[0]
    seqs = rows // seq_len

    def block(left, right):
        grams = [
            lax.dot_general(a, b, (((1,), (1,)), ((), ())), preferred_element_type=f32)
            for a, b in zip(left, right)
        ]
        return (grams[0] * grams[1]).reshape(seqs, seq_len, rows).sum(axis=1)

    zeros = jnp.zeros((seqs, rows), f32)
    lines = [
        [block(white[0], toks[j]) for j in range(4)],
        [zeros, block(white[2], toks[1]), zeros, block(white[2], toks[3])],
        [zeros, block(white[3], toks[1]), block(white[3], toks[2]), zeros],
    ]
    rest = jnp.concatenate([jnp.concatenate(line, axis=1) for line in lines], axis=0)
    n = rest.shape[0]
    parts = []
    for _ in range(3):
        part = rest.astype(jnp.bfloat16)
        parts.append(part)
        rest = rest - part.astype(f32)
    picked = jnp.dot(jnp.concatenate(parts, axis=0), pick[...], preferred_element_type=f32)
    picked = picked[:n] + picked[n : 2 * n] + picked[2 * n :]
    d = lax.axis_index("blk")
    per = seqs // 2
    out[...] = jnp.zeros_like(out)
    for i, owner in enumerate((d, d ^ 2, z_near(d))):
        at = i * seqs
        out[owner] = picked[at : at + per]
        out[owner ^ 8] = picked[at + per : at + seqs]


def score(units, terms, pick, seq_len, size):
    per = units[0].shape[1] // seq_len
    vmem = pl.BlockSpec(memory_space=pltpu.VMEM)
    return pl.pallas_call(
        functools.partial(score_kernel, seq_len),
        out_shape=jax.ShapeDtypeStruct((size, per, pick.shape[1]), jnp.float32),
        in_specs=[vmem] * 10,
        out_specs=vmem,
        compiler_params=pltpu.CompilerParams(vmem_limit_bytes=40 * 1024 * 1024),
        cost_estimate=pl.CostEstimate(flops=2 * 10**9, bytes_accessed=2 * 10**6, transcendentals=0),
        name="pair_scores",
    )(terms, pick, *units)


def paired(activations, out_grads, lengths, layer_ids, flagged, act_factor, grad_factor):
    size = 16
    per = lengths.shape[0]
    seq_len = activations.shape[1] // per
    own, away = prep(activations, out_grads, lengths, seq_len)

    def send(x, to):
        return lax.ppermute(x, "blk", [(d, to(d)) for d in range(size)])

    ways = (lambda d: d ^ 1, lambda d: d ^ 2, z_near)
    opposite = send(away, lambda d: d ^ 8)
    near = [send(own, to) for to in ways]
    terms, pick = setup(layer_ids, flagged, act_factor, grad_factor, seq_len, per)
    opposite, terms, pick = lax.optimization_barrier((opposite, terms, pick))
    far = [send(opposite, to) for to in ways]
    units = [own, opposite]
    for a, b in zip(near, far):
        units += [a, b]
    total = lax.psum(score(units, terms, pick, seq_len, size), "blk")
    return lax.dynamic_index_in_dim(total, lax.axis_index("blk"), 0, keepdims=False)


def solution(mesh):
    in_specs = (
        P(None, ("grp", "blk"), None),
        P(None, ("grp", "blk"), None),
        P(("grp", "blk")),
        P("grp"),
        P("grp"),
        P(),
        P(),
    )
    out_specs = P(("grp", "blk"), None)
    shards = paired if mesh.shape["blk"] == 16 else gathered
    return jax.shard_map(shards, mesh=mesh, in_specs=in_specs, out_specs=out_specs, check_vma=False)
```

```python
import functools

import jax
import jax.numpy as jnp
from jax import lax
from jax.experimental import pallas as pl
from jax.experimental.pallas import tpu as pltpu
from jax.sharding import PartitionSpec as P

HIGHEST = lax.Precision.HIGHEST


def tile_scores(white_acts, white_grads, remote_acts, remote_grads, seq_len):
    gram_acts = jnp.einsum(
        "lqr,lkr->lqk", white_acts, remote_acts, preferred_element_type=jnp.float32
    )
    gram_grads = jnp.einsum(
        "lqr,lkr->lqk", white_grads, remote_grads, preferred_element_type=jnp.float32
    )
    pair = jnp.sum(gram_acts * gram_grads, axis=0)
    rows = pair.shape[0] // seq_len
    columns = pair.shape[1] // seq_len
    width = white_acts.shape[2]
    return pair.reshape(rows, seq_len, columns, seq_len).sum(axis=(1, 3)) * (
        1.0 / (width * seq_len)
    )


def gathered(activations, out_grads, lengths, layer_ids, flagged, act_factor, grad_factor):
    tok_rows = activations.shape[1]
    seq_count = lengths.shape[0]
    seq_len = tok_rows // seq_count
    slots = jnp.arange(tok_rows) % seq_len
    keep = (slots < jnp.repeat(lengths, seq_len)).astype(jnp.bfloat16)
    masked_acts = activations * keep[None, :, None]
    masked_grads = out_grads * keep[None, :, None]
    picked_act = jnp.take(act_factor, layer_ids, axis=0)
    picked_grad = jnp.take(grad_factor, layer_ids, axis=0)
    white_acts = jnp.einsum(
        "ltr,lrs->lts", masked_acts.astype(jnp.float32), picked_act, precision=HIGHEST
    ).astype(jnp.bfloat16)
    white_grads = jnp.einsum(
        "ltr,lrs->lts", masked_grads.astype(jnp.float32), picked_grad, precision=HIGHEST
    ).astype(jnp.bfloat16)
    part_scores = tile_scores(
        white_acts,
        white_grads,
        lax.all_gather(masked_acts, "blk", axis=1, tiled=True),
        lax.all_gather(masked_grads, "blk", axis=1, tiled=True),
        seq_len,
    )
    return jnp.take(part_scores, flagged, axis=1)


def z_near(d):
    return d ^ 4 ^ ((d >> 1) & 1)


def mask_kernel(seq_len, pieces, lens, acts, grads, *refs):
    outs, bufs, sems = refs[: len(pieces)], refs[len(pieces) : -1], refs[-1]
    half = lax.axis_index("blk") // 8
    copies = []
    for n, (kept, first, buf) in enumerate(zip(*zip(*pieces), bufs)):
        layer = half if kept else 1 - half
        for w, src in enumerate((acts, grads)):
            rows = pl.ds(first, buf.shape[1])
            copies.append(pltpu.make_async_copy(src.at[layer, rows], buf.at[w], sems.at[n, w]))
            copies[-1].start()
    for n, (piece, buf, out) in enumerate(zip(pieces, bufs, outs)):
        row = lax.broadcasted_iota(jnp.int32, (buf.shape[1], 1), 0)
        bound = jnp.zeros_like(row)
        for s in range(buf.shape[1] // seq_len):
            bound = jnp.where(row // seq_len == s, lens[piece[1] // seq_len + s] + s * seq_len, bound)
        for w in range(2):
            copies[2 * n + w].wait()
            x = buf[w]
            out[w] = jnp.where(row < bound, x, jnp.zeros_like(x))


def masked(activations, out_grads, lengths, seq_len, pieces):
    rank = activations.shape[2]
    shapes = [(2, rows, rank) for _, _, rows in pieces]
    vmem = pl.BlockSpec(memory_space=pltpu.VMEM)
    hbm = pl.BlockSpec(memory_space=pltpu.HBM)
    return pl.pallas_call(
        functools.partial(mask_kernel, seq_len, [piece[:2] for piece in pieces]),
        out_shape=[jax.ShapeDtypeStruct(shape, activations.dtype) for shape in shapes],
        in_specs=[pl.BlockSpec(memory_space=pltpu.SMEM), hbm, hbm],
        out_specs=[vmem] * len(pieces),
        scratch_shapes=[pltpu.VMEM(shape, activations.dtype) for shape in shapes]
        + [pltpu.SemaphoreType.DMA((len(pieces), 2))],
        compiler_params=pltpu.CompilerParams(vmem_limit_bytes=59 * 1024 * 1024),
        cost_estimate=pl.CostEstimate(flops=10**9, bytes_accessed=10**6, transcendentals=0),
        name="masked",
    )(lengths, activations, out_grads)


def whiten(x, terms):
    total = jnp.dot(x, terms[0], preferred_element_type=jnp.float32)
    for n in (1, 2):
        total = total + jnp.dot(x, terms[n], preferred_element_type=jnp.float32)
    return total.astype(jnp.bfloat16)


def stack(*arrays):
    return jnp.concatenate(arrays, axis=0)


def block(seq_len, left, right):
    grams = [
        lax.dot_general(a, b, (((1,), (1,)), ((), ())), preferred_element_type=jnp.float32)
        for a, b in zip(left, right)
    ]
    rows, columns = grams[0].shape
    return (grams[0] * grams[1]).reshape(rows // seq_len, seq_len, columns).sum(axis=1)


def pick_columns(sums, pick):
    rest, terms = sums, []
    for _ in range(3):
        terms.append(rest.astype(jnp.bfloat16))
        rest = rest - terms[-1].astype(jnp.float32)
    n = sums.shape[0]
    out = jnp.dot(stack(*terms), pick[...], preferred_element_type=jnp.float32)
    return out[:n] + out[n : 2 * n] + out[2 * n :]


def early_kernel(
    seq_len, per, layer_ids, flagged, act_f, grad_f, u0, u1, u2, u3, v,
    terms, white, pick, sums, factor, sems,
):
    d = lax.axis_index("blk")
    layer = layer_ids[d // 8]
    copies = [
        pltpu.make_async_copy(src.at[layer], factor.at[i], sems.at[i])
        for i, src in enumerate((act_f, grad_f))
    ]
    for copy in copies:
        copy.start()
    token = lax.broadcasted_iota(jnp.int32, pick.shape, 0)
    spot = token // (seq_len * per)
    slot = spot // 2
    owner = jnp.where(
        slot == 0, d, jnp.where(slot == 1, d ^ 1, jnp.where(slot == 2, d ^ 2, z_near(d)))
    )
    owner = owner ^ (8 * (spot % 2))
    seq = owner * per + token // seq_len % per
    scale = 1.0 / (factor.shape[1] * seq_len)
    pick[...] = jnp.where(seq == flagged[...], scale, 0.0).astype(pick.dtype)
    n = u0.shape[1]
    mine, x, z = [], [], []
    for w in range(2):
        copies[w].wait()
        rest = factor[w]
        for t in range(3):
            term = rest.astype(jnp.bfloat16)
            terms[w, t] = term
            rest = rest - term.astype(jnp.float32)
        rows = whiten(stack(u0[w], v[w], u2[w], u3[w]), terms.at[w])
        white[w] = rows
        mine.append(rows[: 2 * n])
        x.append(rows[2 * n : 3 * n])
        z.append(rows[3 * n :])
    tok = [[u[w] for w in range(2)] for u in (u0, u1, u2, u3)]
    own = [stack(u0[w], v[w]) for w in range(2)]
    sums[...] = jnp.zeros_like(sums)
    r = 2 * per
    sums[0:r, 0 : 2 * n] = block(seq_len, mine, own)
    for slot in (1, 2, 3):
        at = 2 * n * slot
        sums[0:r, at : at + n] = block(seq_len, mine, tok[slot])
    for row, left, slots in ((r, x, (1, 3)), (2 * r, z, (1, 2))):
        for slot in slots:
            at = 2 * n * slot
            sums[row : row + per, at : at + n] = block(seq_len, left, tok[slot])


def return_kernel(seq_len, per, terms, white, pick, sums, u1, u2, u3, *refs):
    v, outs = refs[:3], refs[3:]
    n = u1.shape[1]
    late = [[v[i][w] for w in range(2)] for i in range(3)]
    tok = [[u[w] for w in range(2)] for u in (u1, u2, u3)]
    both = [[stack(tok[i][w], late[i][w]) for w in range(2)] for i in range(3)]
    fresh = [whiten(stack(late[1][w], late[2][w]), terms.at[w]) for w in range(2)]
    zeros = jnp.zeros((per, n), jnp.float32)
    wide = jnp.zeros((per, 2 * n), jnp.float32)
    lines = []
    for i, other in ((1, 2), (2, 1)):
        early = [white[w, (i + 1) * n : (i + 2) * n] for w in range(2)]
        got = block(seq_len, early, [stack(late[0][w], late[other][w]) for w in range(2)])
        cols = {1: jnp.concatenate([zeros, got[:, :n]], axis=1)}
        cols[other + 1] = jnp.concatenate([zeros, got[:, n:]], axis=1)
        lines.append(jnp.concatenate([cols.get(slot, wide) for slot in range(4)], axis=1))
        new = [fresh[w][(i - 1) * n : i * n] for w in range(2)]
        cols = {1: block(seq_len, new, both[0]), other + 1: block(seq_len, new, both[other])}
        lines.append(jnp.concatenate([cols.get(slot, wide) for slot in range(4)], axis=1))
    r = 2 * per
    picked = pick_columns(sums[r:, :] + stack(*lines), pick)
    for i, out in enumerate(outs):
        out[...] = picked[i * r : (i + 1) * r]


def own_kernel(seq_len, per, white, pick, sums, *refs):
    v, out = refs[:3], refs[3]
    n = v[0].shape[1]
    r = 2 * per
    mine = [white[w, : 2 * n] for w in range(2)]
    line = [jnp.zeros((r, 2 * n), jnp.float32)]
    for i in range(3):
        right = [v[i][w] for w in range(2)]
        line += [jnp.zeros((r, n), jnp.float32), block(seq_len, mine, right)]
    out[...] = pick_columns(sums[:r, :] + jnp.concatenate(line, axis=1), pick)


def call(kernel, name, flops, limit, operands, specs, out_shape, scratch=()):
    vmem = pl.BlockSpec(memory_space=pltpu.VMEM)
    return pl.pallas_call(
        kernel,
        out_shape=out_shape,
        in_specs=specs + [vmem] * (len(operands) - len(specs)),
        out_specs=jax.tree.map(lambda _: vmem, out_shape),
        scratch_shapes=scratch,
        compiler_params=pltpu.CompilerParams(vmem_limit_bytes=limit * 1024 * 1024),
        cost_estimate=pl.CostEstimate(flops=flops, bytes_accessed=10**6, transcendentals=0),
        name=name,
    )(*operands)


def paired(activations, out_grads, lengths, layer_ids, flagged, act_factor, grad_factor):
    size = 16
    per = lengths.shape[0]
    tokens, rank = activations.shape[1:]
    seq_len = tokens // per
    f32, bf16 = jnp.float32, jnp.bfloat16

    def send(x, to):
        return lax.ppermute(x, "blk", [(d, to(d)) for d in range(size)])

    def opposite(d):
        return d ^ 8

    ways = (lambda d: d ^ 1, lambda d: d ^ 2, z_near)
    data = (activations, out_grads, lengths, seq_len)
    (away,) = masked(*data, [(False, 0, tokens)])
    v = send(away, opposite)
    away, *data = lax.optimization_barrier((away, *data[:3]))
    (own,) = masked(*data, seq_len, [(True, 0, tokens)])
    u = [own] + [send(own, to) for to in ways[::-1]][::-1]
    late = [send(v, to) for to in ways[::-1]][::-1]

    shape = jax.ShapeDtypeStruct
    columns = flagged.shape[0]
    hbm = pl.BlockSpec(memory_space=pltpu.HBM)
    vmem = pl.BlockSpec(memory_space=pltpu.VMEM)
    terms, white, pick, sums = call(
        functools.partial(early_kernel, seq_len, per),
        "early_pairs",
        10**9,
        51,
        (layer_ids, flagged.reshape(1, -1), act_factor, grad_factor, *u, v),
        [pl.BlockSpec(memory_space=pltpu.SMEM), vmem, hbm, hbm],
        (
            shape((2, 3, rank, rank), bf16),
            shape((2, 4 * tokens, rank), bf16),
            shape((8 * tokens, columns), bf16),
            shape((6 * per, 8 * tokens), f32),
        ),
        [pltpu.VMEM((2, rank, rank), f32), pltpu.SemaphoreType.DMA((2,))],
    )
    rows = shape((2 * per, columns), f32)
    by_x, by_z = call(
        functools.partial(return_kernel, seq_len, per),
        "return_rows",
        10**9,
        40,
        (terms, white, pick, sums, *u[1:], *late),
        [],
        (rows, rows),
    )
    mine = call(
        functools.partial(own_kernel, seq_len, per),
        "own_rows",
        10**9,
        40,
        (white, pick, sums, *late),
        [],
        rows,
    )
    half_sum = mine + send(by_x, lambda d: d ^ 2) + send(by_z, z_near)
    return half_sum[:per] + send(half_sum[per:], opposite)


def solution(mesh):
    in_specs = (
        P(None, ("grp", "blk"), None),
        P(None, ("grp", "blk"), None),
        P(("grp", "blk")),
        P("grp"),
        P("grp"),
        P(),
        P(),
    )
    out_specs = P(("grp", "blk"), None)
    shards = paired if mesh.shape["blk"] == 16 else gathered
    return jax.shard_map(shards, mesh=mesh, in_specs=in_specs, out_specs=out_specs, check_vma=False)
```

```python
import functools

import jax
import jax.numpy as jnp
from jax import lax
from jax.experimental import pallas as pl
from jax.experimental.pallas import tpu as pltpu
from jax.sharding import PartitionSpec as P

HIGHEST = lax.Precision.HIGHEST


def tile_scores(white_acts, white_grads, remote_acts, remote_grads, seq_len):
    gram_acts = jnp.einsum(
        "lqr,lkr->lqk", white_acts, remote_acts, preferred_element_type=jnp.float32
    )
    gram_grads = jnp.einsum(
        "lqr,lkr->lqk", white_grads, remote_grads, preferred_element_type=jnp.float32
    )
    pair = jnp.sum(gram_acts * gram_grads, axis=0)
    rows = pair.shape[0] // seq_len
    columns = pair.shape[1] // seq_len
    width = white_acts.shape[2]
    return pair.reshape(rows, seq_len, columns, seq_len).sum(axis=(1, 3)) * (
        1.0 / (width * seq_len)
    )


def gathered(activations, out_grads, lengths, layer_ids, flagged, act_factor, grad_factor):
    tok_rows = activations.shape[1]
    seq_count = lengths.shape[0]
    seq_len = tok_rows // seq_count
    slots = jnp.arange(tok_rows) % seq_len
    keep = (slots < jnp.repeat(lengths, seq_len)).astype(jnp.bfloat16)
    masked_acts = activations * keep[None, :, None]
    masked_grads = out_grads * keep[None, :, None]
    picked_act = jnp.take(act_factor, layer_ids, axis=0)
    picked_grad = jnp.take(grad_factor, layer_ids, axis=0)
    white_acts = jnp.einsum(
        "ltr,lrs->lts", masked_acts.astype(jnp.float32), picked_act, precision=HIGHEST
    ).astype(jnp.bfloat16)
    white_grads = jnp.einsum(
        "ltr,lrs->lts", masked_grads.astype(jnp.float32), picked_grad, precision=HIGHEST
    ).astype(jnp.bfloat16)
    part_scores = tile_scores(
        white_acts,
        white_grads,
        lax.all_gather(masked_acts, "blk", axis=1, tiled=True),
        lax.all_gather(masked_grads, "blk", axis=1, tiled=True),
        seq_len,
    )
    return jnp.take(part_scores, flagged, axis=1)


def z_near(d):
    return d ^ 4 ^ ((d >> 1) & 1)


def mask_kernel(seq_len, lens, acts, grads, out):
    tokens = acts.shape[1]
    row = lax.broadcasted_iota(jnp.int32, (tokens, 1), 0)
    bound = jnp.zeros_like(row)
    for s in range(tokens // seq_len):
        bound = jnp.where(row // seq_len == s, lens[s] + s * seq_len, bound)
    for w, src in enumerate((acts, grads)):
        x = src[0]
        out[w] = jnp.where(row < bound, x, jnp.zeros_like(x))


def masked(activations, out_grads, lengths, seq_len, kept):
    tokens, rank = activations.shape[1:]

    def layer(i):
        half = lax.axis_index("blk") // 8
        return (half if kept else 1 - half, 0, 0)

    data = pl.BlockSpec((1, tokens, rank), layer)
    return pl.pallas_call(
        functools.partial(mask_kernel, seq_len),
        grid=(1,),
        out_shape=jax.ShapeDtypeStruct((2, tokens, rank), activations.dtype),
        in_specs=[pl.BlockSpec(memory_space=pltpu.SMEM), data, data],
        out_specs=pl.BlockSpec((2, tokens, rank), lambda i: (0, 0, 0)),
        compiler_params=pltpu.CompilerParams(vmem_limit_bytes=59 * 1024 * 1024),
        cost_estimate=pl.CostEstimate(flops=10**9, bytes_accessed=10**6, transcendentals=0),
        name="masked",
    )(lengths, activations, out_grads)


def whiten(x, terms):
    total = jnp.dot(x, terms[0], preferred_element_type=jnp.float32)
    for n in (1, 2):
        total = total + jnp.dot(x, terms[n], preferred_element_type=jnp.float32)
    return total.astype(jnp.bfloat16)


def stack(*arrays):
    return jnp.concatenate(arrays, axis=0)


def block(seq_len, left, right):
    grams = [
        lax.dot_general(a, b, (((1,), (1,)), ((), ())), preferred_element_type=jnp.float32)
        for a, b in zip(left, right)
    ]
    rows, columns = grams[0].shape
    return (grams[0] * grams[1]).reshape(rows // seq_len, seq_len, columns).sum(axis=1)


def pick_columns(sums, pick):
    rest, terms = sums, []
    for _ in range(3):
        terms.append(rest.astype(jnp.bfloat16))
        rest = rest - terms[-1].astype(jnp.float32)
    n = sums.shape[0]
    out = jnp.dot(stack(*terms), pick[...], preferred_element_type=jnp.float32)
    return out[:n] + out[n : 2 * n] + out[2 * n :]


def setup_kernel(seq_len, per, layer_ids, flagged, act_f, grad_f, terms, pick, factor, sems):
    d = lax.axis_index("blk")
    layer = layer_ids[d // 8]
    copies = [
        pltpu.make_async_copy(src.at[layer], factor.at[i], sems.at[i])
        for i, src in enumerate((act_f, grad_f))
    ]
    for copy in copies:
        copy.start()
    token = lax.broadcasted_iota(jnp.int32, pick.shape, 0)
    spot = token // (seq_len * per)
    slot = spot // 2
    owner = jnp.where(
        slot == 0, d, jnp.where(slot == 1, d ^ 1, jnp.where(slot == 2, d ^ 2, z_near(d)))
    )
    owner = owner ^ (8 * (spot % 2))
    seq = owner * per + token // seq_len % per
    scale = 1.0 / (factor.shape[1] * seq_len)
    pick[...] = jnp.where(seq == flagged[...], scale, 0.0).astype(pick.dtype)
    for w, copy in enumerate(copies):
        copy.wait()
        rest = factor[w]
        for t in range(3):
            term = rest.astype(jnp.bfloat16)
            terms[w, t] = term
            rest = rest - term.astype(jnp.float32)


def early_kernel(seq_len, per, terms, u0, v, u3, u2, u1, white, sums):
    n = u0.shape[1]
    mine, x, z = [], [], []
    for w in range(2):
        rows = whiten(stack(u0[w], v[w], u2[w], u3[w]), terms.at[w])
        white[w] = rows
        mine.append(rows[: 2 * n])
        x.append(rows[2 * n : 3 * n])
        z.append(rows[3 * n :])
    tok = [[u[w] for w in range(2)] for u in (u0, u1, u2, u3)]
    own = [stack(u0[w], v[w]) for w in range(2)]
    sums[...] = jnp.zeros_like(sums)
    r = 2 * per
    sums[0:r, 0 : 2 * n] = block(seq_len, mine, own)
    for slot in (1, 2, 3):
        at = 2 * n * slot
        sums[0:r, at : at + n] = block(seq_len, mine, tok[slot])
    for row, left, slots in ((r, x, (1, 3)), (2 * r, z, (1, 2))):
        for slot in slots:
            at = 2 * n * slot
            sums[row : row + per, at : at + n] = block(seq_len, left, tok[slot])


def return_kernel(seq_len, per, terms, white, pick, sums, u3, u2, u1, v3, v2, v1, *outs):
    v = (v1, v2, v3)
    n = u1.shape[1]
    late = [[v[i][w] for w in range(2)] for i in range(3)]
    tok = [[u[w] for w in range(2)] for u in (u1, u2, u3)]
    both = [[stack(tok[i][w], late[i][w]) for w in range(2)] for i in range(3)]
    fresh = [whiten(stack(late[1][w], late[2][w]), terms.at[w]) for w in range(2)]
    zeros = jnp.zeros((per, n), jnp.float32)
    wide = jnp.zeros((per, 2 * n), jnp.float32)
    lines = []
    for i, other in ((1, 2), (2, 1)):
        early = [white[w, (i + 1) * n : (i + 2) * n] for w in range(2)]
        got = block(seq_len, early, [stack(late[0][w], late[other][w]) for w in range(2)])
        cols = {1: jnp.concatenate([zeros, got[:, :n]], axis=1)}
        cols[other + 1] = jnp.concatenate([zeros, got[:, n:]], axis=1)
        lines.append(jnp.concatenate([cols.get(slot, wide) for slot in range(4)], axis=1))
        new = [fresh[w][(i - 1) * n : i * n] for w in range(2)]
        cols = {1: block(seq_len, new, both[0]), other + 1: block(seq_len, new, both[other])}
        lines.append(jnp.concatenate([cols.get(slot, wide) for slot in range(4)], axis=1))
    r = 2 * per
    picked = pick_columns(sums[r:, :] + stack(*lines), pick)
    for i, out in enumerate(outs):
        out[...] = picked[i * r : (i + 1) * r]


def own_kernel(seq_len, per, white, pick, sums, v3, v2, v1, out):
    v = (v1, v2, v3)
    n = v[0].shape[1]
    r = 2 * per
    mine = [white[w, : 2 * n] for w in range(2)]
    line = [jnp.zeros((r, 2 * n), jnp.float32)]
    for i in range(3):
        right = [v[i][w] for w in range(2)]
        line += [jnp.zeros((r, n), jnp.float32), block(seq_len, mine, right)]
    out[...] = pick_columns(sums[:r, :] + jnp.concatenate(line, axis=1), pick)


def call(kernel, name, flops, limit, operands, specs, out_shape, scratch=()):
    vmem = pl.BlockSpec(memory_space=pltpu.VMEM)
    return pl.pallas_call(
        kernel,
        out_shape=out_shape,
        in_specs=specs + [vmem] * (len(operands) - len(specs)),
        out_specs=jax.tree.map(lambda _: vmem, out_shape),
        scratch_shapes=scratch,
        compiler_params=pltpu.CompilerParams(vmem_limit_bytes=limit * 1024 * 1024),
        cost_estimate=pl.CostEstimate(flops=flops, bytes_accessed=10**6, transcendentals=0),
        name=name,
    )(*operands)


def paired(activations, out_grads, lengths, layer_ids, flagged, act_factor, grad_factor):
    size = 16
    per = lengths.shape[0]
    tokens, rank = activations.shape[1:]
    seq_len = tokens // per
    f32, bf16 = jnp.float32, jnp.bfloat16

    def send(x, to):
        return lax.ppermute(x, "blk", [(d, to(d)) for d in range(size)])

    def opposite(d):
        return d ^ 8

    ways = (z_near, lambda d: d ^ 2, lambda d: d ^ 1)
    data = (activations, out_grads, lengths)
    away = masked(*data, seq_len, False)
    v = send(away, opposite)
    away, *data = lax.optimization_barrier((away, *data))
    own = masked(*data, seq_len, True)
    near = [send(own, to) for to in ways]

    shape = jax.ShapeDtypeStruct
    columns = flagged.shape[0]
    hbm = pl.BlockSpec(memory_space=pltpu.HBM)
    vmem = pl.BlockSpec(memory_space=pltpu.VMEM)
    terms, pick = call(
        functools.partial(setup_kernel, seq_len, per),
        "factor_terms",
        10**9,
        51,
        (layer_ids, flagged.reshape(1, -1), act_factor, grad_factor),
        [pl.BlockSpec(memory_space=pltpu.SMEM), vmem, hbm, hbm],
        (shape((2, 3, rank, rank), bf16), shape((8 * tokens, columns), bf16)),
        [pltpu.VMEM((2, rank, rank), f32), pltpu.SemaphoreType.DMA((2,))],
    )
    v, terms, pick = lax.optimization_barrier((v, terms, pick))
    late = [send(v, to) for to in ways]
    white, sums = call(
        functools.partial(early_kernel, seq_len, per),
        "early_pairs",
        10**9,
        40,
        (terms, own, v, *near),
        [],
        (shape((2, 4 * tokens, rank), bf16), shape((6 * per, 8 * tokens), f32)),
    )
    rows = shape((2 * per, columns), f32)
    by_x, by_z = call(
        functools.partial(return_kernel, seq_len, per),
        "return_rows",
        10**9,
        40,
        (terms, white, pick, sums, *near, *late),
        [],
        (rows, rows),
    )
    mine = call(
        functools.partial(own_kernel, seq_len, per),
        "own_rows",
        10**9,
        40,
        (white, pick, sums, *late),
        [],
        rows,
    )
    half_sum = mine + send(by_x, lambda d: d ^ 2) + send(by_z, z_near)
    return half_sum[:per] + send(half_sum[per:], opposite)


def solution(mesh):
    in_specs = (
        P(None, ("grp", "blk"), None),
        P(None, ("grp", "blk"), None),
        P(("grp", "blk")),
        P("grp"),
        P("grp"),
        P(),
        P(),
    )
    out_specs = P(("grp", "blk"), None)
    shards = paired if mesh.shape["blk"] == 16 else gathered
    return jax.shard_map(shards, mesh=mesh, in_specs=in_specs, out_specs=out_specs, check_vma=False)
```

```python
import functools

import jax
import jax.numpy as jnp
from jax import lax
from jax.experimental import pallas as pl
from jax.experimental.pallas import tpu as pltpu
from jax.sharding import PartitionSpec as P

HIGHEST = lax.Precision.HIGHEST


def tile_scores(white_acts, white_grads, remote_acts, remote_grads, seq_len):
    gram_acts = jnp.einsum(
        "lqr,lkr->lqk", white_acts, remote_acts, preferred_element_type=jnp.float32
    )
    gram_grads = jnp.einsum(
        "lqr,lkr->lqk", white_grads, remote_grads, preferred_element_type=jnp.float32
    )
    pair = jnp.sum(gram_acts * gram_grads, axis=0)
    rows = pair.shape[0] // seq_len
    columns = pair.shape[1] // seq_len
    width = white_acts.shape[2]
    return pair.reshape(rows, seq_len, columns, seq_len).sum(axis=(1, 3)) * (
        1.0 / (width * seq_len)
    )


def gathered(activations, out_grads, lengths, layer_ids, flagged, act_factor, grad_factor):
    tok_rows = activations.shape[1]
    seq_count = lengths.shape[0]
    seq_len = tok_rows // seq_count
    slots = jnp.arange(tok_rows) % seq_len
    keep = (slots < jnp.repeat(lengths, seq_len)).astype(jnp.bfloat16)
    masked_acts = activations * keep[None, :, None]
    masked_grads = out_grads * keep[None, :, None]
    picked_act = jnp.take(act_factor, layer_ids, axis=0)
    picked_grad = jnp.take(grad_factor, layer_ids, axis=0)
    white_acts = jnp.einsum(
        "ltr,lrs->lts", masked_acts.astype(jnp.float32), picked_act, precision=HIGHEST
    ).astype(jnp.bfloat16)
    white_grads = jnp.einsum(
        "ltr,lrs->lts", masked_grads.astype(jnp.float32), picked_grad, precision=HIGHEST
    ).astype(jnp.bfloat16)
    part_scores = tile_scores(
        white_acts,
        white_grads,
        lax.all_gather(masked_acts, "blk", axis=1, tiled=True),
        lax.all_gather(masked_grads, "blk", axis=1, tiled=True),
        seq_len,
    )
    return jnp.take(part_scores, flagged, axis=1)


def z_near(d):
    return d ^ 4 ^ ((d >> 1) & 1)


def mask_kernel(seq_len, lens, acts, grads, out):
    tokens = acts.shape[1]
    row = lax.broadcasted_iota(jnp.int32, (tokens, 1), 0)
    bound = jnp.zeros_like(row)
    for s in range(tokens // seq_len):
        bound = jnp.where(row // seq_len == s, lens[s] + s * seq_len, bound)
    for w, src in enumerate((acts, grads)):
        x = src[0]
        out[w] = jnp.where(row < bound, x, jnp.zeros_like(x))


def masked(activations, out_grads, lengths, seq_len, kept):
    tokens, rank = activations.shape[1:]

    def layer(i):
        half = lax.axis_index("blk") // 8
        return (half if kept else 1 - half, 0, 0)

    data = pl.BlockSpec((1, tokens, rank), layer)
    return pl.pallas_call(
        functools.partial(mask_kernel, seq_len),
        grid=(1,),
        out_shape=jax.ShapeDtypeStruct((2, tokens, rank), activations.dtype),
        in_specs=[pl.BlockSpec(memory_space=pltpu.SMEM), data, data],
        out_specs=pl.BlockSpec((2, tokens, rank), lambda i: (0, 0, 0)),
        compiler_params=pltpu.CompilerParams(vmem_limit_bytes=59 * 1024 * 1024),
        cost_estimate=pl.CostEstimate(flops=10**9, bytes_accessed=10**6, transcendentals=0),
        name="masked",
    )(lengths, activations, out_grads)


def whiten(x, terms):
    total = jnp.dot(x, terms[0], preferred_element_type=jnp.float32)
    for n in (1, 2):
        total = total + jnp.dot(x, terms[n], preferred_element_type=jnp.float32)
    return total.astype(jnp.bfloat16)


def stack(*arrays):
    return jnp.concatenate(arrays, axis=0)


def block(seq_len, left, right):
    grams = [
        lax.dot_general(a, b, (((1,), (1,)), ((), ())), preferred_element_type=jnp.float32)
        for a, b in zip(left, right)
    ]
    rows, columns = grams[0].shape
    return (grams[0] * grams[1]).reshape(rows // seq_len, seq_len, columns).sum(axis=1)


def pick_columns(sums, pick):
    rest, terms = sums, []
    for _ in range(3):
        terms.append(rest.astype(jnp.bfloat16))
        rest = rest - terms[-1].astype(jnp.float32)
    n = sums.shape[0]
    out = jnp.dot(stack(*terms), pick[...], preferred_element_type=jnp.float32)
    return out[:n] + out[n : 2 * n] + out[2 * n :]


def setup_kernel(seq_len, per, layer_ids, flagged, act_f, grad_f, terms, pick, factor, sems):
    d = lax.axis_index("blk")
    layer = layer_ids[d // 8]
    copies = [
        pltpu.make_async_copy(src.at[layer], factor.at[i], sems.at[i])
        for i, src in enumerate((act_f, grad_f))
    ]
    for copy in copies:
        copy.start()
    token = lax.broadcasted_iota(jnp.int32, pick.shape, 0)
    spot = token // (seq_len * per)
    slot = spot // 2
    owner = jnp.where(
        slot == 0, d, jnp.where(slot == 1, d ^ 1, jnp.where(slot == 2, d ^ 2, z_near(d)))
    )
    owner = owner ^ (8 * (spot % 2))
    seq = owner * per + token // seq_len % per
    scale = 1.0 / (factor.shape[1] * seq_len)
    pick[...] = jnp.where(seq == flagged[...], scale, 0.0).astype(pick.dtype)
    for w, copy in enumerate(copies):
        copy.wait()
        rest = factor[w]
        for t in range(3):
            term = rest.astype(jnp.bfloat16)
            terms[w, t] = term
            rest = rest - term.astype(jnp.float32)


def early_kernel(seq_len, per, terms, u0, v, u2, u3, u1, white, sums):
    n = u0.shape[1]
    mine, x, z = [], [], []
    for w in range(2):
        rows = whiten(stack(u0[w], v[w], u2[w], u3[w]), terms.at[w])
        white[w] = rows
        mine.append(rows[: 2 * n])
        x.append(rows[2 * n : 3 * n])
        z.append(rows[3 * n :])
    tok = [[u[w] for w in range(2)] for u in (u0, u1, u2, u3)]
    own = [stack(u0[w], v[w]) for w in range(2)]
    sums[...] = jnp.zeros_like(sums)
    r = 2 * per
    sums[0:r, 0 : 2 * n] = block(seq_len, mine, own)
    for slot in (1, 2, 3):
        at = 2 * n * slot
        sums[0:r, at : at + n] = block(seq_len, mine, tok[slot])
    for row, left, slots in ((r, x, (1, 3)), (2 * r, z, (1, 2))):
        for slot in slots:
            at = 2 * n * slot
            sums[row : row + per, at : at + n] = block(seq_len, left, tok[slot])


def return_kernel(seq_len, per, terms, white, pick, sums, u2, u3, u1, v2, v3, v1, *outs):
    v = (v1, v2, v3)
    n = u1.shape[1]
    late = [[v[i][w] for w in range(2)] for i in range(3)]
    tok = [[u[w] for w in range(2)] for u in (u1, u2, u3)]
    both = [[stack(tok[i][w], late[i][w]) for w in range(2)] for i in range(3)]
    fresh = [whiten(stack(late[1][w], late[2][w]), terms.at[w]) for w in range(2)]
    zeros = jnp.zeros((per, n), jnp.float32)
    wide = jnp.zeros((per, 2 * n), jnp.float32)
    lines = []
    for i, other in ((1, 2), (2, 1)):
        early = [white[w, (i + 1) * n : (i + 2) * n] for w in range(2)]
        got = block(seq_len, early, [stack(late[0][w], late[other][w]) for w in range(2)])
        cols = {1: jnp.concatenate([zeros, got[:, :n]], axis=1)}
        cols[other + 1] = jnp.concatenate([zeros, got[:, n:]], axis=1)
        lines.append(jnp.concatenate([cols.get(slot, wide) for slot in range(4)], axis=1))
        new = [fresh[w][(i - 1) * n : i * n] for w in range(2)]
        cols = {1: block(seq_len, new, both[0]), other + 1: block(seq_len, new, both[other])}
        lines.append(jnp.concatenate([cols.get(slot, wide) for slot in range(4)], axis=1))
    r = 2 * per
    picked = pick_columns(sums[r:, :] + stack(*lines), pick)
    for i, out in enumerate(outs):
        out[...] = picked[i * r : (i + 1) * r]


def own_kernel(seq_len, per, white, pick, sums, v2, v3, v1, out):
    v = (v1, v2, v3)
    n = v[0].shape[1]
    r = 2 * per
    mine = [white[w, : 2 * n] for w in range(2)]
    line = [jnp.zeros((r, 2 * n), jnp.float32)]
    for i in range(3):
        right = [v[i][w] for w in range(2)]
        line += [jnp.zeros((r, n), jnp.float32), block(seq_len, mine, right)]
    out[...] = pick_columns(sums[:r, :] + jnp.concatenate(line, axis=1), pick)


def call(kernel, name, flops, limit, operands, specs, out_shape, scratch=()):
    vmem = pl.BlockSpec(memory_space=pltpu.VMEM)
    return pl.pallas_call(
        kernel,
        out_shape=out_shape,
        in_specs=specs + [vmem] * (len(operands) - len(specs)),
        out_specs=jax.tree.map(lambda _: vmem, out_shape),
        scratch_shapes=scratch,
        compiler_params=pltpu.CompilerParams(vmem_limit_bytes=limit * 1024 * 1024),
        cost_estimate=pl.CostEstimate(flops=flops, bytes_accessed=10**6, transcendentals=0),
        name=name,
    )(*operands)


def paired(activations, out_grads, lengths, layer_ids, flagged, act_factor, grad_factor):
    size = 16
    per = lengths.shape[0]
    tokens, rank = activations.shape[1:]
    seq_len = tokens // per
    f32, bf16 = jnp.float32, jnp.bfloat16

    def send(x, to):
        return lax.ppermute(x, "blk", [(d, to(d)) for d in range(size)])

    def opposite(d):
        return d ^ 8

    ways = (lambda d: d ^ 2, z_near, lambda d: d ^ 1)
    data = (activations, out_grads, lengths)
    away = masked(*data, seq_len, False)
    v = send(away, opposite)
    away, *data = lax.optimization_barrier((away, *data))
    own = masked(*data, seq_len, True)
    near = [send(own, to) for to in ways]

    shape = jax.ShapeDtypeStruct
    columns = flagged.shape[0]
    hbm = pl.BlockSpec(memory_space=pltpu.HBM)
    vmem = pl.BlockSpec(memory_space=pltpu.VMEM)
    terms, pick = call(
        functools.partial(setup_kernel, seq_len, per),
        "factor_terms",
        10**9,
        51,
        (layer_ids, flagged.reshape(1, -1), act_factor, grad_factor),
        [pl.BlockSpec(memory_space=pltpu.SMEM), vmem, hbm, hbm],
        (shape((2, 3, rank, rank), bf16), shape((8 * tokens, columns), bf16)),
        [pltpu.VMEM((2, rank, rank), f32), pltpu.SemaphoreType.DMA((2,))],
    )
    v, terms, pick = lax.optimization_barrier((v, terms, pick))
    late = [send(v, to) for to in ways]
    white, sums = call(
        functools.partial(early_kernel, seq_len, per),
        "early_pairs",
        10**9,
        40,
        (terms, own, v, *near),
        [],
        (shape((2, 4 * tokens, rank), bf16), shape((6 * per, 8 * tokens), f32)),
    )
    rows = shape((2 * per, columns), f32)
    by_x, by_z = call(
        functools.partial(return_kernel, seq_len, per),
        "return_rows",
        10**9,
        40,
        (terms, white, pick, sums, *near, *late),
        [],
        (rows, rows),
    )
    mine = call(
        functools.partial(own_kernel, seq_len, per),
        "own_rows",
        10**9,
        40,
        (white, pick, sums, *late),
        [],
        rows,
    )
    half_sum = mine + send(by_x, lambda d: d ^ 2) + send(by_z, z_near)
    return half_sum[:per] + send(half_sum[per:], opposite)


def solution(mesh):
    in_specs = (
        P(None, ("grp", "blk"), None),
        P(None, ("grp", "blk"), None),
        P(("grp", "blk")),
        P("grp"),
        P("grp"),
        P(),
        P(),
    )
    out_specs = P(("grp", "blk"), None)
    shards = paired if mesh.shape["blk"] == 16 else gathered
    return jax.shard_map(shards, mesh=mesh, in_specs=in_specs, out_specs=out_specs, check_vma=False)
```

```python
import functools

import jax
import jax.numpy as jnp
from jax import lax
from jax.experimental import pallas as pl
from jax.experimental.pallas import tpu as pltpu
from jax.sharding import PartitionSpec as P

HIGHEST = lax.Precision.HIGHEST


def tile_scores(white_acts, white_grads, remote_acts, remote_grads, seq_len):
    gram_acts = jnp.einsum(
        "lqr,lkr->lqk", white_acts, remote_acts, preferred_element_type=jnp.float32
    )
    gram_grads = jnp.einsum(
        "lqr,lkr->lqk", white_grads, remote_grads, preferred_element_type=jnp.float32
    )
    pair = jnp.sum(gram_acts * gram_grads, axis=0)
    rows = pair.shape[0] // seq_len
    columns = pair.shape[1] // seq_len
    width = white_acts.shape[2]
    return pair.reshape(rows, seq_len, columns, seq_len).sum(axis=(1, 3)) * (
        1.0 / (width * seq_len)
    )


def gathered(activations, out_grads, lengths, layer_ids, flagged, act_factor, grad_factor):
    tok_rows = activations.shape[1]
    seq_count = lengths.shape[0]
    seq_len = tok_rows // seq_count
    slots = jnp.arange(tok_rows) % seq_len
    keep = (slots < jnp.repeat(lengths, seq_len)).astype(jnp.bfloat16)
    masked_acts = activations * keep[None, :, None]
    masked_grads = out_grads * keep[None, :, None]
    picked_act = jnp.take(act_factor, layer_ids, axis=0)
    picked_grad = jnp.take(grad_factor, layer_ids, axis=0)
    white_acts = jnp.einsum(
        "ltr,lrs->lts", masked_acts.astype(jnp.float32), picked_act, precision=HIGHEST
    ).astype(jnp.bfloat16)
    white_grads = jnp.einsum(
        "ltr,lrs->lts", masked_grads.astype(jnp.float32), picked_grad, precision=HIGHEST
    ).astype(jnp.bfloat16)
    part_scores = tile_scores(
        white_acts,
        white_grads,
        lax.all_gather(masked_acts, "blk", axis=1, tiled=True),
        lax.all_gather(masked_grads, "blk", axis=1, tiled=True),
        seq_len,
    )
    return jnp.take(part_scores, flagged, axis=1)


def z_near(d):
    return d ^ 4 ^ ((d >> 1) & 1)


def mask_kernel(seq_len, lens, acts, grads, out):
    tokens = acts.shape[1]
    row = lax.broadcasted_iota(jnp.int32, (tokens, 1), 0)
    bound = jnp.zeros_like(row)
    for s in range(tokens // seq_len):
        bound = jnp.where(row // seq_len == s, lens[0:1, s : s + 1] + s * seq_len, bound)
    keep = jnp.broadcast_to(row < bound, acts.shape[1:])
    for w, src in enumerate((acts, grads)):
        x = src[0]
        out[w] = jnp.where(keep, x, jnp.zeros_like(x))


def masked(activations, out_grads, lengths, seq_len, kept):
    tokens, rank = activations.shape[1:]

    def layer(i):
        half = lax.axis_index("blk") // 8
        return (half if kept else 1 - half, 0, 0)

    data = pl.BlockSpec((1, tokens, rank), layer)
    return pl.pallas_call(
        functools.partial(mask_kernel, seq_len),
        grid=(1,),
        out_shape=jax.ShapeDtypeStruct((2, tokens, rank), activations.dtype),
        in_specs=[pl.BlockSpec((1, lengths.shape[0]), lambda i: (0, 0)), data, data],
        out_specs=pl.BlockSpec((2, tokens, rank), lambda i: (0, 0, 0)),
        compiler_params=pltpu.CompilerParams(vmem_limit_bytes=59 * 1024 * 1024),
        cost_estimate=pl.CostEstimate(flops=10**9, bytes_accessed=10**6, transcendentals=0),
        name="masked",
    )(lengths.reshape(1, -1), activations, out_grads)


def whiten(x, terms):
    total = jnp.dot(x, terms[0], preferred_element_type=jnp.float32)
    for n in (1, 2):
        total = total + jnp.dot(x, terms[n], preferred_element_type=jnp.float32)
    return total.astype(jnp.bfloat16)


def stack(*arrays):
    return jnp.concatenate(arrays, axis=0)


def block(seq_len, left, right):
    grams = [
        lax.dot_general(a, b, (((1,), (1,)), ((), ())), preferred_element_type=jnp.float32)
        for a, b in zip(left, right)
    ]
    rows, columns = grams[0].shape
    return (grams[0] * grams[1]).reshape(rows // seq_len, seq_len, columns).sum(axis=1)


def pick_columns(sums, pick):
    rest, terms = sums, []
    for _ in range(3):
        terms.append(rest.astype(jnp.bfloat16))
        rest = rest - terms[-1].astype(jnp.float32)
    n = sums.shape[0]
    out = jnp.dot(stack(*terms), pick[...], preferred_element_type=jnp.float32)
    return out[:n] + out[n : 2 * n] + out[2 * n :]


def setup_kernel(seq_len, per, layer_ids, flagged, act_f, grad_f, terms, pick, factor, sems):
    d = lax.axis_index("blk")
    layer = layer_ids[d // 8]
    copies = [
        pltpu.make_async_copy(src.at[layer], factor.at[i], sems.at[i])
        for i, src in enumerate((act_f, grad_f))
    ]
    for copy in copies:
        copy.start()
    token = lax.broadcasted_iota(jnp.int32, pick.shape, 0)
    spot = token // (seq_len * per)
    slot = spot // 2
    owner = jnp.where(
        slot == 0, d, jnp.where(slot == 1, d ^ 1, jnp.where(slot == 2, d ^ 2, z_near(d)))
    )
    owner = owner ^ (8 * (spot % 2))
    seq = owner * per + token // seq_len % per
    scale = 1.0 / (factor.shape[1] * seq_len)
    pick[...] = jnp.where(seq == flagged[...], scale, 0.0).astype(pick.dtype)
    for w, copy in enumerate(copies):
        copy.wait()
        rest = factor[w]
        for t in range(3):
            term = rest.astype(jnp.bfloat16)
            terms[w, t] = term
            rest = rest - term.astype(jnp.float32)


def early_kernel(seq_len, per, terms, u0, v, u3, u2, u1, white, sums):
    n = u0.shape[1]
    mine, x, z = [], [], []
    for w in range(2):
        rows = whiten(stack(u0[w], v[w], u2[w], u3[w]), terms.at[w])
        white[w] = rows
        mine.append(rows[: 2 * n])
        x.append(rows[2 * n : 3 * n])
        z.append(rows[3 * n :])
    tok = [[u[w] for w in range(2)] for u in (u0, u1, u2, u3)]
    own = [stack(u0[w], v[w]) for w in range(2)]
    sums[...] = jnp.zeros_like(sums)
    r = 2 * per
    sums[0:r, 0 : 2 * n] = block(seq_len, mine, own)
    for slot in (1, 2, 3):
        at = 2 * n * slot
        sums[0:r, at : at + n] = block(seq_len, mine, tok[slot])
    for row, left, slots in ((r, x, (1, 3)), (2 * r, z, (1, 2))):
        for slot in slots:
            at = 2 * n * slot
            sums[row : row + per, at : at + n] = block(seq_len, left, tok[slot])


def return_kernel(seq_len, per, terms, white, pick, sums, u3, u2, u1, v3, v2, v1, *outs):
    v = (v1, v2, v3)
    n = u1.shape[1]
    late = [[v[i][w] for w in range(2)] for i in range(3)]
    tok = [[u[w] for w in range(2)] for u in (u1, u2, u3)]
    both = [[stack(tok[i][w], late[i][w]) for w in range(2)] for i in range(3)]
    fresh = [whiten(stack(late[1][w], late[2][w]), terms.at[w]) for w in range(2)]
    zeros = jnp.zeros((per, n), jnp.float32)
    wide = jnp.zeros((per, 2 * n), jnp.float32)
    lines = []
    for i, other in ((1, 2), (2, 1)):
        early = [white[w, (i + 1) * n : (i + 2) * n] for w in range(2)]
        got = block(seq_len, early, [stack(late[0][w], late[other][w]) for w in range(2)])
        cols = {1: jnp.concatenate([zeros, got[:, :n]], axis=1)}
        cols[other + 1] = jnp.concatenate([zeros, got[:, n:]], axis=1)
        lines.append(jnp.concatenate([cols.get(slot, wide) for slot in range(4)], axis=1))
        new = [fresh[w][(i - 1) * n : i * n] for w in range(2)]
        cols = {1: block(seq_len, new, both[0]), other + 1: block(seq_len, new, both[other])}
        lines.append(jnp.concatenate([cols.get(slot, wide) for slot in range(4)], axis=1))
    r = 2 * per
    picked = pick_columns(sums[r:, :] + stack(*lines), pick)
    for i, out in enumerate(outs):
        out[...] = picked[i * r : (i + 1) * r]


def own_kernel(seq_len, per, white, pick, sums, v3, v2, v1, out):
    v = (v1, v2, v3)
    n = v[0].shape[1]
    r = 2 * per
    mine = [white[w, : 2 * n] for w in range(2)]
    line = [jnp.zeros((r, 2 * n), jnp.float32)]
    for i in range(3):
        right = [v[i][w] for w in range(2)]
        line += [jnp.zeros((r, n), jnp.float32), block(seq_len, mine, right)]
    out[...] = pick_columns(sums[:r, :] + jnp.concatenate(line, axis=1), pick)


def call(kernel, name, flops, limit, operands, specs, out_shape, scratch=()):
    vmem = pl.BlockSpec(memory_space=pltpu.VMEM)
    return pl.pallas_call(
        kernel,
        out_shape=out_shape,
        in_specs=specs + [vmem] * (len(operands) - len(specs)),
        out_specs=jax.tree.map(lambda _: vmem, out_shape),
        scratch_shapes=scratch,
        compiler_params=pltpu.CompilerParams(vmem_limit_bytes=limit * 1024 * 1024),
        cost_estimate=pl.CostEstimate(flops=flops, bytes_accessed=10**6, transcendentals=0),
        name=name,
    )(*operands)


def paired(activations, out_grads, lengths, layer_ids, flagged, act_factor, grad_factor):
    size = 16
    per = lengths.shape[0]
    tokens, rank = activations.shape[1:]
    seq_len = tokens // per
    f32, bf16 = jnp.float32, jnp.bfloat16

    def send(x, to):
        return lax.ppermute(x, "blk", [(d, to(d)) for d in range(size)])

    def opposite(d):
        return d ^ 8

    ways = (z_near, lambda d: d ^ 2, lambda d: d ^ 1)
    data = (activations, out_grads, lengths)
    away = masked(*data, seq_len, False)
    v = send(away, opposite)
    away, *data = lax.optimization_barrier((away, *data))
    own = masked(*data, seq_len, True)
    near = [send(own, to) for to in ways]

    shape = jax.ShapeDtypeStruct
    columns = flagged.shape[0]
    hbm = pl.BlockSpec(memory_space=pltpu.HBM)
    vmem = pl.BlockSpec(memory_space=pltpu.VMEM)
    terms, pick = call(
        functools.partial(setup_kernel, seq_len, per),
        "factor_terms",
        10**9,
        51,
        (layer_ids, flagged.reshape(1, -1), act_factor, grad_factor),
        [pl.BlockSpec(memory_space=pltpu.SMEM), vmem, hbm, hbm],
        (shape((2, 3, rank, rank), bf16), shape((8 * tokens, columns), bf16)),
        [pltpu.VMEM((2, rank, rank), f32), pltpu.SemaphoreType.DMA((2,))],
    )
    v, terms, pick = lax.optimization_barrier((v, terms, pick))
    late = [send(v, to) for to in ways]
    white, sums = call(
        functools.partial(early_kernel, seq_len, per),
        "early_pairs",
        10**9,
        40,
        (terms, own, v, *near),
        [],
        (shape((2, 4 * tokens, rank), bf16), shape((6 * per, 8 * tokens), f32)),
    )
    rows = shape((2 * per, columns), f32)
    by_x, by_z = call(
        functools.partial(return_kernel, seq_len, per),
        "return_rows",
        10**9,
        40,
        (terms, white, pick, sums, *near, *late),
        [],
        (rows, rows),
    )
    mine = call(
        functools.partial(own_kernel, seq_len, per),
        "own_rows",
        10**9,
        40,
        (white, pick, sums, *late),
        [],
        rows,
    )
    half_sum = mine + send(by_x, lambda d: d ^ 2) + send(by_z, z_near)
    return half_sum[:per] + send(half_sum[per:], opposite)


def solution(mesh):
    in_specs = (
        P(None, ("grp", "blk"), None),
        P(None, ("grp", "blk"), None),
        P(("grp", "blk")),
        P("grp"),
        P("grp"),
        P(),
        P(),
    )
    out_specs = P(("grp", "blk"), None)
    shards = paired if mesh.shape["blk"] == 16 else gathered
    return jax.shard_map(shards, mesh=mesh, in_specs=in_specs, out_specs=out_specs, check_vma=False)
```

```python
import functools

import jax
import jax.numpy as jnp
from jax import lax
from jax.experimental import pallas as pl
from jax.experimental.pallas import tpu as pltpu
from jax.sharding import PartitionSpec as P

HIGHEST = lax.Precision.HIGHEST


def tile_scores(white_acts, white_grads, remote_acts, remote_grads, seq_len):
    gram_acts = jnp.einsum(
        "lqr,lkr->lqk", white_acts, remote_acts, preferred_element_type=jnp.float32
    )
    gram_grads = jnp.einsum(
        "lqr,lkr->lqk", white_grads, remote_grads, preferred_element_type=jnp.float32
    )
    pair = jnp.sum(gram_acts * gram_grads, axis=0)
    rows = pair.shape[0] // seq_len
    columns = pair.shape[1] // seq_len
    width = white_acts.shape[2]
    return pair.reshape(rows, seq_len, columns, seq_len).sum(axis=(1, 3)) * (
        1.0 / (width * seq_len)
    )


def gathered(activations, out_grads, lengths, layer_ids, flagged, act_factor, grad_factor):
    tok_rows = activations.shape[1]
    seq_count = lengths.shape[0]
    seq_len = tok_rows // seq_count
    slots = jnp.arange(tok_rows) % seq_len
    keep = (slots < jnp.repeat(lengths, seq_len)).astype(jnp.bfloat16)
    masked_acts = activations * keep[None, :, None]
    masked_grads = out_grads * keep[None, :, None]
    picked_act = jnp.take(act_factor, layer_ids, axis=0)
    picked_grad = jnp.take(grad_factor, layer_ids, axis=0)
    white_acts = jnp.einsum(
        "ltr,lrs->lts", masked_acts.astype(jnp.float32), picked_act, precision=HIGHEST
    ).astype(jnp.bfloat16)
    white_grads = jnp.einsum(
        "ltr,lrs->lts", masked_grads.astype(jnp.float32), picked_grad, precision=HIGHEST
    ).astype(jnp.bfloat16)
    part_scores = tile_scores(
        white_acts,
        white_grads,
        lax.all_gather(masked_acts, "blk", axis=1, tiled=True),
        lax.all_gather(masked_grads, "blk", axis=1, tiled=True),
        seq_len,
    )
    return jnp.take(part_scores, flagged, axis=1)


def z_near(d):
    return d ^ 4 ^ ((d >> 1) & 1)


def mask_kernel(seq_len, kept, lens, acts, grads, out, held, sems):
    half = lax.axis_index("blk") // 8
    layer = half if kept else 1 - half
    copies = [
        pltpu.make_async_copy(src, dst, sems.at[i])
        for i, (src, dst) in enumerate(
            ((lens, held), (acts.at[layer], out.at[0]), (grads.at[layer], out.at[1]))
        )
    ]
    for copy in copies:
        copy.start()
    for copy in copies:
        copy.wait()
    tokens = acts.shape[1]
    row = lax.broadcasted_iota(jnp.int32, (tokens, 1), 0)
    bound = jnp.zeros_like(row)
    for s in range(tokens // seq_len):
        bound = jnp.where(row // seq_len == s, held[s] + s * seq_len, bound)
    x = out[0]
    out[0] = jnp.where(row < bound, x, jnp.zeros_like(x))


def masked(activations, out_grads, lengths, seq_len, kept, limit):
    tokens, rank = activations.shape[1:]
    hbm = pl.BlockSpec(memory_space=pltpu.HBM)
    return pl.pallas_call(
        functools.partial(mask_kernel, seq_len, kept),
        out_shape=jax.ShapeDtypeStruct((2, tokens, rank), activations.dtype),
        in_specs=[hbm, hbm, hbm],
        out_specs=pl.BlockSpec(memory_space=pltpu.VMEM),
        scratch_shapes=[pltpu.SMEM(lengths.shape, jnp.int32), pltpu.SemaphoreType.DMA((3,))],
        compiler_params=pltpu.CompilerParams(vmem_limit_bytes=limit),
        cost_estimate=pl.CostEstimate(flops=10**9, bytes_accessed=10**6, transcendentals=0),
        name="masked",
    )(lengths, activations, out_grads)


def whiten(x, terms):
    total = jnp.dot(x, terms[0], preferred_element_type=jnp.float32)
    for n in (1, 2):
        total = total + jnp.dot(x, terms[n], preferred_element_type=jnp.float32)
    return total.astype(jnp.bfloat16)


def stack(*arrays):
    return jnp.concatenate(arrays, axis=0)


def block(seq_len, left, right):
    grams = [
        lax.dot_general(a, b, (((1,), (1,)), ((), ())), preferred_element_type=jnp.float32)
        for a, b in zip(left, right)
    ]
    rows, columns = grams[0].shape
    return (grams[0] * grams[1]).reshape(rows // seq_len, seq_len, columns).sum(axis=1)


def pick_columns(sums, pick):
    rest, terms = sums, []
    for _ in range(3):
        terms.append(rest.astype(jnp.bfloat16))
        rest = rest - terms[-1].astype(jnp.float32)
    n = sums.shape[0]
    out = jnp.dot(stack(*terms), pick[...], preferred_element_type=jnp.float32)
    return out[:n] + out[n : 2 * n] + out[2 * n :]


def setup_kernel(seq_len, per, layer_ids, flagged, act_f, grad_f, terms, pick, factor, sems):
    d = lax.axis_index("blk")
    layer = layer_ids[d // 8]
    copies = [
        pltpu.make_async_copy(src.at[layer], factor.at[i], sems.at[i])
        for i, src in enumerate((act_f, grad_f))
    ]
    for copy in copies:
        copy.start()
    token = lax.broadcasted_iota(jnp.int32, pick.shape, 0)
    spot = token // (seq_len * per)
    slot = spot // 2
    owner = jnp.where(
        slot == 0, d, jnp.where(slot == 1, d ^ 1, jnp.where(slot == 2, d ^ 2, z_near(d)))
    )
    owner = owner ^ (8 * (spot % 2))
    seq = owner * per + token // seq_len % per
    scale = 1.0 / (factor.shape[1] * seq_len)
    pick[...] = jnp.where(seq == flagged[...], scale, 0.0).astype(pick.dtype)
    for w, copy in enumerate(copies):
        copy.wait()
        rest = factor[w]
        for t in range(3):
            term = rest.astype(jnp.bfloat16)
            terms[w, t] = term
            rest = rest - term.astype(jnp.float32)


def early_kernel(seq_len, per, terms, u0, v, u3, u2, u1, white, sums):
    n = u0.shape[1]
    mine, x, z = [], [], []
    for w in range(2):
        rows = whiten(stack(u0[w], v[w], u2[w], u3[w]), terms.at[w])
        white[w] = rows
        mine.append(rows[: 2 * n])
        x.append(rows[2 * n : 3 * n])
        z.append(rows[3 * n :])
    tok = [[u[w] for w in range(2)] for u in (u0, u1, u2, u3)]
    own = [stack(u0[w], v[w]) for w in range(2)]
    sums[...] = jnp.zeros_like(sums)
    r = 2 * per
    sums[0:r, 0 : 2 * n] = block(seq_len, mine, own)
    for slot in (1, 2, 3):
        at = 2 * n * slot
        sums[0:r, at : at + n] = block(seq_len, mine, tok[slot])
    for row, left, slots in ((r, x, (1, 3)), (2 * r, z, (1, 2))):
        for slot in slots:
            at = 2 * n * slot
            sums[row : row + per, at : at + n] = block(seq_len, left, tok[slot])


def return_kernel(seq_len, per, terms, white, pick, sums, u3, u2, u1, v3, v2, v1, *outs):
    v = (v1, v2, v3)
    n = u1.shape[1]
    late = [[v[i][w] for w in range(2)] for i in range(3)]
    tok = [[u[w] for w in range(2)] for u in (u1, u2, u3)]
    both = [[stack(tok[i][w], late[i][w]) for w in range(2)] for i in range(3)]
    fresh = [whiten(stack(late[1][w], late[2][w]), terms.at[w]) for w in range(2)]
    zeros = jnp.zeros((per, n), jnp.float32)
    wide = jnp.zeros((per, 2 * n), jnp.float32)
    lines = []
    for i, other in ((1, 2), (2, 1)):
        early = [white[w, (i + 1) * n : (i + 2) * n] for w in range(2)]
        got = block(seq_len, early, [stack(late[0][w], late[other][w]) for w in range(2)])
        cols = {1: jnp.concatenate([zeros, got[:, :n]], axis=1)}
        cols[other + 1] = jnp.concatenate([zeros, got[:, n:]], axis=1)
        lines.append(jnp.concatenate([cols.get(slot, wide) for slot in range(4)], axis=1))
        new = [fresh[w][(i - 1) * n : i * n] for w in range(2)]
        cols = {1: block(seq_len, new, both[0]), other + 1: block(seq_len, new, both[other])}
        lines.append(jnp.concatenate([cols.get(slot, wide) for slot in range(4)], axis=1))
    r = 2 * per
    picked = pick_columns(sums[r:, :] + stack(*lines), pick)
    for i, out in enumerate(outs):
        out[...] = picked[i * r : (i + 1) * r]


def own_kernel(seq_len, per, white, pick, sums, v3, v2, v1, out):
    v = (v1, v2, v3)
    n = v[0].shape[1]
    r = 2 * per
    mine = [white[w, : 2 * n] for w in range(2)]
    line = [jnp.zeros((r, 2 * n), jnp.float32)]
    for i in range(3):
        right = [v[i][w] for w in range(2)]
        line += [jnp.zeros((r, n), jnp.float32), block(seq_len, mine, right)]
    out[...] = pick_columns(sums[:r, :] + jnp.concatenate(line, axis=1), pick)


def call(kernel, name, flops, limit, operands, specs, out_shape, scratch=()):
    vmem = pl.BlockSpec(memory_space=pltpu.VMEM)
    return pl.pallas_call(
        kernel,
        out_shape=out_shape,
        in_specs=specs + [vmem] * (len(operands) - len(specs)),
        out_specs=jax.tree.map(lambda _: vmem, out_shape),
        scratch_shapes=scratch,
        compiler_params=pltpu.CompilerParams(vmem_limit_bytes=limit * 1024 * 1024),
        cost_estimate=pl.CostEstimate(flops=flops, bytes_accessed=10**6, transcendentals=0),
        name=name,
    )(*operands)


def paired(activations, out_grads, lengths, layer_ids, flagged, act_factor, grad_factor):
    size = 16
    per = lengths.shape[0]
    tokens, rank = activations.shape[1:]
    seq_len = tokens // per
    f32, bf16 = jnp.float32, jnp.bfloat16

    def send(x, to):
        return lax.ppermute(x, "blk", [(d, to(d)) for d in range(size)])

    def opposite(d):
        return d ^ 8

    ways = (z_near, lambda d: d ^ 2, lambda d: d ^ 1)
    data = (activations, out_grads, lengths)
    away = masked(*data, seq_len, False, 59 * 1024 * 1024)
    v = send(away, opposite)
    away, *data = lax.optimization_barrier((away, *data))
    own = masked(*data, seq_len, True, 59 * 1024 * 1024)
    near = [send(own, to) for to in ways]

    shape = jax.ShapeDtypeStruct
    columns = flagged.shape[0]
    hbm = pl.BlockSpec(memory_space=pltpu.HBM)
    vmem = pl.BlockSpec(memory_space=pltpu.VMEM)
    terms, pick = call(
        functools.partial(setup_kernel, seq_len, per),
        "factor_terms",
        10**9,
        51,
        (layer_ids, flagged.reshape(1, -1), act_factor, grad_factor),
        [pl.BlockSpec(memory_space=pltpu.SMEM), vmem, hbm, hbm],
        (shape((2, 3, rank, rank), bf16), shape((8 * tokens, columns), bf16)),
        [pltpu.VMEM((2, rank, rank), f32), pltpu.SemaphoreType.DMA((2,))],
    )
    v, terms, pick = lax.optimization_barrier((v, terms, pick))
    late = [send(v, to) for to in ways]
    white, sums = call(
        functools.partial(early_kernel, seq_len, per),
        "early_pairs",
        10**9,
        40,
        (terms, own, v, *near),
        [],
        (shape((2, 4 * tokens, rank), bf16), shape((6 * per, 8 * tokens), f32)),
    )
    rows = shape((2 * per, columns), f32)
    by_x, by_z = call(
        functools.partial(return_kernel, seq_len, per),
        "return_rows",
        10**9,
        40,
        (terms, white, pick, sums, *near, *late),
        [],
        (rows, rows),
    )
    mine = call(
        functools.partial(own_kernel, seq_len, per),
        "own_rows",
        10**9,
        40,
        (white, pick, sums, *late),
        [],
        rows,
    )
    half_sum = mine + send(by_x, lambda d: d ^ 2) + send(by_z, z_near)
    return half_sum[:per] + send(half_sum[per:], opposite)


def solution(mesh):
    in_specs = (
        P(None, ("grp", "blk"), None),
        P(None, ("grp", "blk"), None),
        P(("grp", "blk")),
        P("grp"),
        P("grp"),
        P(),
        P(),
    )
    out_specs = P(("grp", "blk"), None)
    shards = paired if mesh.shape["blk"] == 16 else gathered
    return jax.shard_map(shards, mesh=mesh, in_specs=in_specs, out_specs=out_specs, check_vma=False)
```

```python
import functools

import jax
import jax.numpy as jnp
from jax import lax
from jax.experimental import pallas as pl
from jax.experimental.pallas import tpu as pltpu
from jax.sharding import PartitionSpec as P

HIGHEST = lax.Precision.HIGHEST


def tile_scores(white_acts, white_grads, remote_acts, remote_grads, seq_len):
    gram_acts = jnp.einsum(
        "lqr,lkr->lqk", white_acts, remote_acts, preferred_element_type=jnp.float32
    )
    gram_grads = jnp.einsum(
        "lqr,lkr->lqk", white_grads, remote_grads, preferred_element_type=jnp.float32
    )
    pair = jnp.sum(gram_acts * gram_grads, axis=0)
    rows = pair.shape[0] // seq_len
    columns = pair.shape[1] // seq_len
    width = white_acts.shape[2]
    return pair.reshape(rows, seq_len, columns, seq_len).sum(axis=(1, 3)) * (
        1.0 / (width * seq_len)
    )


def gathered(activations, out_grads, lengths, layer_ids, flagged, act_factor, grad_factor):
    tok_rows = activations.shape[1]
    seq_count = lengths.shape[0]
    seq_len = tok_rows // seq_count
    slots = jnp.arange(tok_rows) % seq_len
    keep = (slots < jnp.repeat(lengths, seq_len)).astype(jnp.bfloat16)
    masked_acts = activations * keep[None, :, None]
    masked_grads = out_grads * keep[None, :, None]
    picked_act = jnp.take(act_factor, layer_ids, axis=0)
    picked_grad = jnp.take(grad_factor, layer_ids, axis=0)
    white_acts = jnp.einsum(
        "ltr,lrs->lts", masked_acts.astype(jnp.float32), picked_act, precision=HIGHEST
    ).astype(jnp.bfloat16)
    white_grads = jnp.einsum(
        "ltr,lrs->lts", masked_grads.astype(jnp.float32), picked_grad, precision=HIGHEST
    ).astype(jnp.bfloat16)
    part_scores = tile_scores(
        white_acts,
        white_grads,
        lax.all_gather(masked_acts, "blk", axis=1, tiled=True),
        lax.all_gather(masked_grads, "blk", axis=1, tiled=True),
        seq_len,
    )
    return jnp.take(part_scores, flagged, axis=1)


def z_near(d):
    return d ^ 4 ^ ((d >> 1) & 1)


def copy_layer(acts, grads, layer, out, sems):
    copies = [
        pltpu.make_async_copy(src.at[layer], out.at[i], sems.at[i])
        for i, src in enumerate((acts, grads))
    ]
    for copy in copies:
        copy.start()
    for copy in copies:
        copy.wait()


def keep_slots(lens, tokens, seq_len):
    row = lax.broadcasted_iota(jnp.int32, (tokens, 1), 0)
    bound = jnp.zeros_like(row)
    for s in range(tokens // seq_len):
        bound = jnp.where(row // seq_len == s, lens[0:1, s : s + 1] + s * seq_len, bound)
    return row < bound


def away_kernel(acts, grads, out, sems):
    copy_layer(acts, grads, 1 - lax.axis_index("blk") // 8, out, sems)


def own_kernel(seq_len, acts, grads, lens, out, sems):
    copy_layer(acts, grads, lax.axis_index("blk") // 8, out, sems)
    x = out[0]
    out[0] = jnp.where(keep_slots(lens, x.shape[0], seq_len), x, jnp.zeros_like(x))


def far_kernel(seq_len, lens, v, out):
    x = v[0]
    out[0] = jnp.where(keep_slots(lens, x.shape[0], seq_len), x, jnp.zeros_like(x))
    out[1] = v[1]


def whiten(x, terms):
    total = jnp.dot(x, terms[0], preferred_element_type=jnp.float32)
    for n in (1, 2):
        total = total + jnp.dot(x, terms[n], preferred_element_type=jnp.float32)
    return total.astype(jnp.bfloat16)


def stack(*arrays):
    return jnp.concatenate(arrays, axis=0)


def block(seq_len, left, right):
    grams = [
        lax.dot_general(a, b, (((1,), (1,)), ((), ())), preferred_element_type=jnp.float32)
        for a, b in zip(left, right)
    ]
    rows, columns = grams[0].shape
    return (grams[0] * grams[1]).reshape(rows // seq_len, seq_len, columns).sum(axis=1)


def pick_columns(sums, pick):
    rest, terms = sums, []
    for _ in range(3):
        terms.append(rest.astype(jnp.bfloat16))
        rest = rest - terms[-1].astype(jnp.float32)
    n = sums.shape[0]
    out = jnp.dot(stack(*terms), pick[...], preferred_element_type=jnp.float32)
    return out[:n] + out[n : 2 * n] + out[2 * n :]


def setup_kernel(seq_len, per, layer_ids, flagged, act_f, grad_f, terms, pick, factor, sems):
    d = lax.axis_index("blk")
    layer = layer_ids[d // 8]
    copies = [
        pltpu.make_async_copy(src.at[layer], factor.at[i], sems.at[i])
        for i, src in enumerate((act_f, grad_f))
    ]
    for copy in copies:
        copy.start()
    token = lax.broadcasted_iota(jnp.int32, pick.shape, 0)
    spot = token // (seq_len * per)
    slot = spot // 2
    owner = jnp.where(
        slot == 0, d, jnp.where(slot == 1, d ^ 1, jnp.where(slot == 2, d ^ 2, z_near(d)))
    )
    owner = owner ^ (8 * (spot % 2))
    seq = owner * per + token // seq_len % per
    scale = 1.0 / (factor.shape[1] * seq_len)
    pick[...] = jnp.where(seq == flagged[...], scale, 0.0).astype(pick.dtype)
    for w, copy in enumerate(copies):
        copy.wait()
        rest = factor[w]
        for t in range(3):
            term = rest.astype(jnp.bfloat16)
            terms[w, t] = term
            rest = rest - term.astype(jnp.float32)


def early_kernel(seq_len, per, terms, u0, v, u3, u2, u1, white, sums):
    n = u0.shape[1]
    mine, x, z = [], [], []
    for w in range(2):
        rows = whiten(stack(u0[w], v[w], u2[w], u3[w]), terms.at[w])
        white[w] = rows
        mine.append(rows[: 2 * n])
        x.append(rows[2 * n : 3 * n])
        z.append(rows[3 * n :])
    tok = [[u[w] for w in range(2)] for u in (u0, u1, u2, u3)]
    own = [stack(u0[w], v[w]) for w in range(2)]
    sums[...] = jnp.zeros_like(sums)
    r = 2 * per
    sums[0:r, 0 : 2 * n] = block(seq_len, mine, own)
    for slot in (1, 2, 3):
        at = 2 * n * slot
        sums[0:r, at : at + n] = block(seq_len, mine, tok[slot])
    for row, left, slots in ((r, x, (1, 3)), (2 * r, z, (1, 2))):
        for slot in slots:
            at = 2 * n * slot
            sums[row : row + per, at : at + n] = block(seq_len, left, tok[slot])


def return_kernel(seq_len, per, terms, white, pick, sums, u3, u2, u1, v3, v2, v1, *outs):
    v = (v1, v2, v3)
    n = u1.shape[1]
    late = [[v[i][w] for w in range(2)] for i in range(3)]
    tok = [[u[w] for w in range(2)] for u in (u1, u2, u3)]
    both = [[stack(tok[i][w], late[i][w]) for w in range(2)] for i in range(3)]
    fresh = [whiten(stack(late[1][w], late[2][w]), terms.at[w]) for w in range(2)]
    zeros = jnp.zeros((per, n), jnp.float32)
    wide = jnp.zeros((per, 2 * n), jnp.float32)
    lines = []
    for i, other in ((1, 2), (2, 1)):
        early = [white[w, (i + 1) * n : (i + 2) * n] for w in range(2)]
        got = block(seq_len, early, [stack(late[0][w], late[other][w]) for w in range(2)])
        cols = {1: jnp.concatenate([zeros, got[:, :n]], axis=1)}
        cols[other + 1] = jnp.concatenate([zeros, got[:, n:]], axis=1)
        lines.append(jnp.concatenate([cols.get(slot, wide) for slot in range(4)], axis=1))
        new = [fresh[w][(i - 1) * n : i * n] for w in range(2)]
        cols = {1: block(seq_len, new, both[0]), other + 1: block(seq_len, new, both[other])}
        lines.append(jnp.concatenate([cols.get(slot, wide) for slot in range(4)], axis=1))
    r = 2 * per
    picked = pick_columns(sums[r:, :] + stack(*lines), pick)
    for i, out in enumerate(outs):
        out[...] = picked[i * r : (i + 1) * r]


def rows_kernel(seq_len, per, white, pick, sums, v3, v2, v1, out):
    v = (v1, v2, v3)
    n = v[0].shape[1]
    r = 2 * per
    mine = [white[w, : 2 * n] for w in range(2)]
    line = [jnp.zeros((r, 2 * n), jnp.float32)]
    for i in range(3):
        right = [v[i][w] for w in range(2)]
        line += [jnp.zeros((r, n), jnp.float32), block(seq_len, mine, right)]
    out[...] = pick_columns(sums[:r, :] + jnp.concatenate(line, axis=1), pick)


def call(kernel, name, flops, limit, operands, specs, out_shape, scratch=(), **more):
    vmem = pl.BlockSpec(memory_space=pltpu.VMEM)
    return pl.pallas_call(
        kernel,
        out_shape=out_shape,
        in_specs=specs + [vmem] * (len(operands) - len(specs)),
        out_specs=jax.tree.map(lambda _: vmem, out_shape),
        scratch_shapes=scratch,
        compiler_params=pltpu.CompilerParams(vmem_limit_bytes=int(limit * 1024 * 1024)),
        cost_estimate=pl.CostEstimate(flops=flops, bytes_accessed=10**6, transcendentals=0),
        name=name,
        **more,
    )(*operands)


def paired(activations, out_grads, lengths, layer_ids, flagged, act_factor, grad_factor):
    size = 16
    per = lengths.shape[0]
    tokens, rank = activations.shape[1:]
    seq_len = tokens // per
    f32, bf16 = jnp.float32, jnp.bfloat16

    def send(x, to):
        return lax.ppermute(x, "blk", [(d, to(d)) for d in range(size)])

    def opposite(d):
        return d ^ 8

    ways = (z_near, lambda d: d ^ 2, lambda d: d ^ 1)
    hbm = pl.BlockSpec(memory_space=pltpu.HBM)
    vmem = pl.BlockSpec(memory_space=pltpu.VMEM)
    shape = jax.ShapeDtypeStruct
    columns = flagged.shape[0]
    unit = shape((2, tokens, rank), bf16)
    pair_of_copies = [pltpu.SemaphoreType.DMA((2,))]
    data = (activations, out_grads)
    away = call(away_kernel, "away", 10**9, 53.71, data, [hbm, hbm], unit, pair_of_copies)
    v = send(away, opposite)
    away, lens, *data = lax.optimization_barrier((away, lengths.reshape(1, -1), *data))
    far_lens = send(lens, opposite)
    own = call(
        functools.partial(own_kernel, seq_len),
        "own",
        10**9,
        59,
        (*data, lens),
        [hbm, hbm],
        unit,
        pair_of_copies,
    )
    near = [send(own, to) for to in ways]
    terms, pick = call(
        functools.partial(setup_kernel, seq_len, per),
        "factor_terms",
        10**9,
        51,
        (layer_ids, flagged.reshape(1, -1), act_factor, grad_factor),
        [pl.BlockSpec(memory_space=pltpu.SMEM), vmem, hbm, hbm],
        (shape((2, 3, rank, rank), bf16), shape((8 * tokens, columns), bf16)),
        [pltpu.VMEM((2, rank, rank), f32), pltpu.SemaphoreType.DMA((2,))],
    )
    v, terms, pick = lax.optimization_barrier((v, terms, pick))
    v = call(
        functools.partial(far_kernel, seq_len),
        "far",
        10**4,
        40,
        (far_lens, v),
        [],
        unit,
        input_output_aliases={1: 0},
    )
    late = [send(v, to) for to in ways]
    white, sums = call(
        functools.partial(early_kernel, seq_len, per),
        "early_pairs",
        10**9,
        40,
        (terms, own, v, *near),
        [],
        (shape((2, 4 * tokens, rank), bf16), shape((6 * per, 8 * tokens), f32)),
    )
    rows = shape((2 * per, columns), f32)
    by_x, by_z = call(
        functools.partial(return_kernel, seq_len, per),
        "return_rows",
        10**9,
        40,
        (terms, white, pick, sums, *near, *late),
        [],
        (rows, rows),
    )
    mine = call(
        functools.partial(rows_kernel, seq_len, per),
        "own_rows",
        10**9,
        40,
        (white, pick, sums, *late),
        [],
        rows,
    )
    half_sum = mine + send(by_x, lambda d: d ^ 2) + send(by_z, z_near)
    return half_sum[:per] + send(half_sum[per:], opposite)


def solution(mesh):
    in_specs = (
        P(None, ("grp", "blk"), None),
        P(None, ("grp", "blk"), None),
        P(("grp", "blk")),
        P("grp"),
        P("grp"),
        P(),
        P(),
    )
    out_specs = P(("grp", "blk"), None)
    shards = paired if mesh.shape["blk"] == 16 else gathered
    return jax.shard_map(shards, mesh=mesh, in_specs=in_specs, out_specs=out_specs, check_vma=False)
```

```python
import functools

import jax
import jax.numpy as jnp
from jax import lax
from jax.experimental import pallas as pl
from jax.experimental.pallas import tpu as pltpu
from jax.sharding import PartitionSpec as P

HIGHEST = lax.Precision.HIGHEST


def tile_scores(white_acts, white_grads, remote_acts, remote_grads, seq_len):
    gram_acts = jnp.einsum(
        "lqr,lkr->lqk", white_acts, remote_acts, preferred_element_type=jnp.float32
    )
    gram_grads = jnp.einsum(
        "lqr,lkr->lqk", white_grads, remote_grads, preferred_element_type=jnp.float32
    )
    pair = jnp.sum(gram_acts * gram_grads, axis=0)
    rows = pair.shape[0] // seq_len
    columns = pair.shape[1] // seq_len
    width = white_acts.shape[2]
    return pair.reshape(rows, seq_len, columns, seq_len).sum(axis=(1, 3)) * (
        1.0 / (width * seq_len)
    )


def gathered(activations, out_grads, lengths, layer_ids, flagged, act_factor, grad_factor):
    tok_rows = activations.shape[1]
    seq_count = lengths.shape[0]
    seq_len = tok_rows // seq_count
    slots = jnp.arange(tok_rows) % seq_len
    keep = (slots < jnp.repeat(lengths, seq_len)).astype(jnp.bfloat16)
    masked_acts = activations * keep[None, :, None]
    masked_grads = out_grads * keep[None, :, None]
    picked_act = jnp.take(act_factor, layer_ids, axis=0)
    picked_grad = jnp.take(grad_factor, layer_ids, axis=0)
    white_acts = jnp.einsum(
        "ltr,lrs->lts", masked_acts.astype(jnp.float32), picked_act, precision=HIGHEST
    ).astype(jnp.bfloat16)
    white_grads = jnp.einsum(
        "ltr,lrs->lts", masked_grads.astype(jnp.float32), picked_grad, precision=HIGHEST
    ).astype(jnp.bfloat16)
    part_scores = tile_scores(
        white_acts,
        white_grads,
        lax.all_gather(masked_acts, "blk", axis=1, tiled=True),
        lax.all_gather(masked_grads, "blk", axis=1, tiled=True),
        seq_len,
    )
    return jnp.take(part_scores, flagged, axis=1)


def z_near(d):
    return d ^ 4 ^ ((d >> 1) & 1)


def away_kernel(acts, grads, out, sems):
    layer = 1 - lax.axis_index("blk") // 8
    copies = [
        pltpu.make_async_copy(src.at[layer], out.at[i], sems.at[i])
        for i, src in enumerate((acts, grads))
    ]
    for copy in copies:
        copy.start()
    for copy in copies:
        copy.wait()


def masked_acts(x, lens, seq_len):
    row = lax.broadcasted_iota(jnp.int32, (x.shape[0], 1), 0)
    bound = jnp.zeros_like(row)
    for s in range(x.shape[0] // seq_len):
        bound = jnp.where(row // seq_len == s, lens[0:1, s : s + 1] + s * seq_len, bound)
    return jnp.where(row < bound, x, jnp.zeros_like(x))


def away_mask_kernel(seq_len, lens, unit, out):
    out[0] = masked_acts(unit[0], lens, seq_len)
    out[1] = unit[1]


def own_kernel(seq_len, lens, acts, grads, out):
    half = lax.axis_index("blk") // 8
    out[0] = masked_acts(acts[half], lens, seq_len)
    out[1] = grads[half]


def whiten(x, terms):
    total = jnp.dot(x, terms[0], preferred_element_type=jnp.float32)
    for n in (1, 2):
        total = total + jnp.dot(x, terms[n], preferred_element_type=jnp.float32)
    return total.astype(jnp.bfloat16)


def stack(*arrays):
    return jnp.concatenate(arrays, axis=0)


def block(seq_len, left, right):
    grams = [
        lax.dot_general(a, b, (((1,), (1,)), ((), ())), preferred_element_type=jnp.float32)
        for a, b in zip(left, right)
    ]
    rows, columns = grams[0].shape
    return (grams[0] * grams[1]).reshape(rows // seq_len, seq_len, columns).sum(axis=1)


def pick_columns(sums, pick):
    rest, terms = sums, []
    for _ in range(3):
        terms.append(rest.astype(jnp.bfloat16))
        rest = rest - terms[-1].astype(jnp.float32)
    n = sums.shape[0]
    out = jnp.dot(stack(*terms), pick[...], preferred_element_type=jnp.float32)
    return out[:n] + out[n : 2 * n] + out[2 * n :]


def setup_kernel(seq_len, per, layer_ids, flagged, act_f, grad_f, terms, pick, factor, sems):
    d = lax.axis_index("blk")
    layer = layer_ids[d // 8]
    copies = [
        pltpu.make_async_copy(src.at[layer], factor.at[i], sems.at[i])
        for i, src in enumerate((act_f, grad_f))
    ]
    for copy in copies:
        copy.start()
    token = lax.broadcasted_iota(jnp.int32, pick.shape, 0)
    spot = token // (seq_len * per)
    slot = spot // 2
    owner = jnp.where(
        slot == 0, d, jnp.where(slot == 1, d ^ 1, jnp.where(slot == 2, d ^ 2, z_near(d)))
    )
    owner = owner ^ (8 * (spot % 2))
    seq = owner * per + token // seq_len % per
    scale = 1.0 / (factor.shape[1] * seq_len)
    pick[...] = jnp.where(seq == flagged[...], scale, 0.0).astype(pick.dtype)
    for w, copy in enumerate(copies):
        copy.wait()
        rest = factor[w]
        for t in range(3):
            term = rest.astype(jnp.bfloat16)
            terms[w, t] = term
            rest = rest - term.astype(jnp.float32)


def early_kernel(seq_len, per, terms, u0, v, u3, u2, u1, white, sums):
    n = u0.shape[1]
    mine, x, z = [], [], []
    for w in range(2):
        rows = whiten(stack(u0[w], v[w], u2[w], u3[w]), terms.at[w])
        white[w] = rows
        mine.append(rows[: 2 * n])
        x.append(rows[2 * n : 3 * n])
        z.append(rows[3 * n :])
    tok = [[u[w] for w in range(2)] for u in (u0, u1, u2, u3)]
    own = [stack(u0[w], v[w]) for w in range(2)]
    sums[...] = jnp.zeros_like(sums)
    r = 2 * per
    sums[0:r, 0 : 2 * n] = block(seq_len, mine, own)
    for slot in (1, 2, 3):
        at = 2 * n * slot
        sums[0:r, at : at + n] = block(seq_len, mine, tok[slot])
    for row, left, slots in ((r, x, (1, 3)), (2 * r, z, (1, 2))):
        for slot in slots:
            at = 2 * n * slot
            sums[row : row + per, at : at + n] = block(seq_len, left, tok[slot])


def return_kernel(seq_len, per, terms, white, pick, sums, u3, u2, u1, v3, v2, v1, *outs):
    v = (v1, v2, v3)
    n = u1.shape[1]
    late = [[v[i][w] for w in range(2)] for i in range(3)]
    tok = [[u[w] for w in range(2)] for u in (u1, u2, u3)]
    both = [[stack(tok[i][w], late[i][w]) for w in range(2)] for i in range(3)]
    fresh = [whiten(stack(late[1][w], late[2][w]), terms.at[w]) for w in range(2)]
    zeros = jnp.zeros((per, n), jnp.float32)
    wide = jnp.zeros((per, 2 * n), jnp.float32)
    lines = []
    for i, other in ((1, 2), (2, 1)):
        early = [white[w, (i + 1) * n : (i + 2) * n] for w in range(2)]
        got = block(seq_len, early, [stack(late[0][w], late[other][w]) for w in range(2)])
        cols = {1: jnp.concatenate([zeros, got[:, :n]], axis=1)}
        cols[other + 1] = jnp.concatenate([zeros, got[:, n:]], axis=1)
        lines.append(jnp.concatenate([cols.get(slot, wide) for slot in range(4)], axis=1))
        new = [fresh[w][(i - 1) * n : i * n] for w in range(2)]
        cols = {1: block(seq_len, new, both[0]), other + 1: block(seq_len, new, both[other])}
        lines.append(jnp.concatenate([cols.get(slot, wide) for slot in range(4)], axis=1))
    r = 2 * per
    picked = pick_columns(sums[r:, :] + stack(*lines), pick)
    for i, out in enumerate(outs):
        out[...] = picked[i * r : (i + 1) * r]


def rows_kernel(seq_len, per, white, pick, sums, v3, v2, v1, out):
    v = (v1, v2, v3)
    n = v[0].shape[1]
    r = 2 * per
    mine = [white[w, : 2 * n] for w in range(2)]
    line = [jnp.zeros((r, 2 * n), jnp.float32)]
    for i in range(3):
        right = [v[i][w] for w in range(2)]
        line += [jnp.zeros((r, n), jnp.float32), block(seq_len, mine, right)]
    out[...] = pick_columns(sums[:r, :] + jnp.concatenate(line, axis=1), pick)


def call(kernel, name, flops, limit, operands, specs, out_shape, scratch=(), **more):
    vmem = pl.BlockSpec(memory_space=pltpu.VMEM)
    return pl.pallas_call(
        kernel,
        out_shape=out_shape,
        in_specs=specs + [vmem] * (len(operands) - len(specs)),
        out_specs=jax.tree.map(lambda _: vmem, out_shape),
        scratch_shapes=scratch,
        compiler_params=pltpu.CompilerParams(vmem_limit_bytes=int(limit * 1024 * 1024)),
        cost_estimate=pl.CostEstimate(flops=flops, bytes_accessed=10**6, transcendentals=0),
        name=name,
        **more,
    )(*operands)


def paired(activations, out_grads, lengths, layer_ids, flagged, act_factor, grad_factor):
    size = 16
    per = lengths.shape[0]
    tokens, rank = activations.shape[1:]
    seq_len = tokens // per
    f32, bf16 = jnp.float32, jnp.bfloat16

    def send(x, to):
        return lax.ppermute(x, "blk", [(d, to(d)) for d in range(size)])

    def opposite(d):
        return d ^ 8

    ways = (z_near, lambda d: d ^ 2, lambda d: d ^ 1)
    hbm = pl.BlockSpec(memory_space=pltpu.HBM)
    vmem = pl.BlockSpec(memory_space=pltpu.VMEM)
    shape = jax.ShapeDtypeStruct
    columns = flagged.shape[0]
    unit = shape((2, tokens, rank), bf16)
    data = (activations, out_grads)
    lens = lengths.reshape(1, -1)
    copies = [pltpu.SemaphoreType.DMA((2,))]
    away = call(away_kernel, "away", 3 * 10**9, 53.71, data, [hbm, hbm], unit, copies)
    away = call(
        functools.partial(away_mask_kernel, seq_len),
        "away_mask",
        10**4,
        40,
        (lens, away),
        [],
        unit,
        input_output_aliases={1: 0},
    )
    v = send(away, opposite)
    away, lens, *data = lax.optimization_barrier((away, lens, *data))
    own = call(
        functools.partial(own_kernel, seq_len), "own", 10**9, 40, (lens, *data), [], unit
    )
    near = [send(own, to) for to in ways]
    terms, pick = call(
        functools.partial(setup_kernel, seq_len, per),
        "factor_terms",
        10**9,
        51,
        (layer_ids, flagged.reshape(1, -1), act_factor, grad_factor),
        [pl.BlockSpec(memory_space=pltpu.SMEM), vmem, hbm, hbm],
        (shape((2, 3, rank, rank), bf16), shape((8 * tokens, columns), bf16)),
        [pltpu.VMEM((2, rank, rank), f32), pltpu.SemaphoreType.DMA((2,))],
    )
    v, terms, pick = lax.optimization_barrier((v, terms, pick))
    late = [send(v, to) for to in ways]
    white, sums = call(
        functools.partial(early_kernel, seq_len, per),
        "early_pairs",
        10**9,
        40,
        (terms, own, v, *near),
        [],
        (shape((2, 4 * tokens, rank), bf16), shape((6 * per, 8 * tokens), f32)),
    )
    rows = shape((2 * per, columns), f32)
    by_x, by_z = call(
        functools.partial(return_kernel, seq_len, per),
        "return_rows",
        10**9,
        40,
        (terms, white, pick, sums, *near, *late),
        [],
        (rows, rows),
    )
    mine = call(
        functools.partial(rows_kernel, seq_len, per),
        "own_rows",
        10**9,
        40,
        (white, pick, sums, *late),
        [],
        rows,
    )
    half_sum = mine + send(by_x, lambda d: d ^ 2) + send(by_z, z_near)
    return half_sum[:per] + send(half_sum[per:], opposite)


def solution(mesh):
    in_specs = (
        P(None, ("grp", "blk"), None),
        P(None, ("grp", "blk"), None),
        P(("grp", "blk")),
        P("grp"),
        P("grp"),
        P(),
        P(),
    )
    out_specs = P(("grp", "blk"), None)
    shards = paired if mesh.shape["blk"] == 16 else gathered
    return jax.shard_map(shards, mesh=mesh, in_specs=in_specs, out_specs=out_specs, check_vma=False)
```

```python
import functools

import jax
import jax.numpy as jnp
from jax import lax
from jax.experimental import pallas as pl
from jax.experimental.pallas import tpu as pltpu
from jax.sharding import PartitionSpec as P

HIGHEST = lax.Precision.HIGHEST


def tile_scores(white_acts, white_grads, remote_acts, remote_grads, seq_len):
    gram_acts = jnp.einsum(
        "lqr,lkr->lqk", white_acts, remote_acts, preferred_element_type=jnp.float32
    )
    gram_grads = jnp.einsum(
        "lqr,lkr->lqk", white_grads, remote_grads, preferred_element_type=jnp.float32
    )
    pair = jnp.sum(gram_acts * gram_grads, axis=0)
    rows = pair.shape[0] // seq_len
    columns = pair.shape[1] // seq_len
    width = white_acts.shape[2]
    return pair.reshape(rows, seq_len, columns, seq_len).sum(axis=(1, 3)) * (
        1.0 / (width * seq_len)
    )


def gathered(activations, out_grads, lengths, layer_ids, flagged, act_factor, grad_factor):
    tok_rows = activations.shape[1]
    seq_count = lengths.shape[0]
    seq_len = tok_rows // seq_count
    slots = jnp.arange(tok_rows) % seq_len
    keep = (slots < jnp.repeat(lengths, seq_len)).astype(jnp.bfloat16)
    masked_acts = activations * keep[None, :, None]
    masked_grads = out_grads * keep[None, :, None]
    picked_act = jnp.take(act_factor, layer_ids, axis=0)
    picked_grad = jnp.take(grad_factor, layer_ids, axis=0)
    white_acts = jnp.einsum(
        "ltr,lrs->lts", masked_acts.astype(jnp.float32), picked_act, precision=HIGHEST
    ).astype(jnp.bfloat16)
    white_grads = jnp.einsum(
        "ltr,lrs->lts", masked_grads.astype(jnp.float32), picked_grad, precision=HIGHEST
    ).astype(jnp.bfloat16)
    part_scores = tile_scores(
        white_acts,
        white_grads,
        lax.all_gather(masked_acts, "blk", axis=1, tiled=True),
        lax.all_gather(masked_grads, "blk", axis=1, tiled=True),
        seq_len,
    )
    return jnp.take(part_scores, flagged, axis=1)


def z_near(d):
    return d ^ 4 ^ ((d >> 1) & 1)


def away_kernel(acts, grads, out_acts, out_grads, sems):
    layer = 1 - lax.axis_index("blk") // 8
    copies = [
        pltpu.make_async_copy(src.at[layer], out, sems.at[i])
        for i, (src, out) in enumerate(((acts, out_acts), (grads, out_grads)))
    ]
    for copy in copies:
        copy.start()
    for copy in copies:
        copy.wait()


def masked_acts(x, lens, seq_len):
    row = lax.broadcasted_iota(jnp.int32, (x.shape[0], 1), 0)
    bound = jnp.zeros_like(row)
    for s in range(x.shape[0] // seq_len):
        bound = jnp.where(row // seq_len == s, lens[0:1, s : s + 1] + s * seq_len, bound)
    return jnp.where(row < bound, x, jnp.zeros_like(x))


def away_mask_kernel(seq_len, lens, acts, out):
    out[...] = masked_acts(acts[...], lens, seq_len)


def own_kernel(seq_len, lens, acts, grads, out):
    half = lax.axis_index("blk") // 8
    out[0] = masked_acts(acts[half], lens, seq_len)
    out[1] = grads[half]


def whiten(x, terms):
    total = jnp.dot(x, terms[0], preferred_element_type=jnp.float32)
    for n in (1, 2):
        total = total + jnp.dot(x, terms[n], preferred_element_type=jnp.float32)
    return total.astype(jnp.bfloat16)


def stack(*arrays):
    return jnp.concatenate(arrays, axis=0)


def block(seq_len, left, right):
    grams = [
        lax.dot_general(a, b, (((1,), (1,)), ((), ())), preferred_element_type=jnp.float32)
        for a, b in zip(left, right)
    ]
    rows, columns = grams[0].shape
    return (grams[0] * grams[1]).reshape(rows // seq_len, seq_len, columns).sum(axis=1)


def pick_columns(sums, pick):
    rest, terms = sums, []
    for _ in range(3):
        terms.append(rest.astype(jnp.bfloat16))
        rest = rest - terms[-1].astype(jnp.float32)
    n = sums.shape[0]
    out = jnp.dot(stack(*terms), pick[...], preferred_element_type=jnp.float32)
    return out[:n] + out[n : 2 * n] + out[2 * n :]


def terms_kernel(layer_ids, act_f, grad_f, terms, factor, sems):
    layer = layer_ids[lax.axis_index("blk") // 8]
    copies = [
        pltpu.make_async_copy(src.at[layer], factor.at[i], sems.at[i])
        for i, src in enumerate((act_f, grad_f))
    ]
    for copy in copies:
        copy.start()
    for w, copy in enumerate(copies):
        copy.wait()
        rest = factor[w]
        for t in range(3):
            term = rest.astype(jnp.bfloat16)
            terms[w, t] = term
            rest = rest - term.astype(jnp.float32)


def pick_kernel(seq_len, per, rank, flagged, pick):
    d = lax.axis_index("blk")
    token = lax.broadcasted_iota(jnp.int32, pick.shape, 0)
    spot = token // (seq_len * per)
    slot = spot // 2
    owner = jnp.where(
        slot == 0, d, jnp.where(slot == 1, d ^ 1, jnp.where(slot == 2, d ^ 2, z_near(d)))
    )
    owner = owner ^ (8 * (spot % 2))
    seq = owner * per + token // seq_len % per
    pick[...] = jnp.where(seq == flagged[...], 1.0 / (rank * seq_len), 0.0).astype(pick.dtype)


def whiten(x, terms):
    total = jnp.dot(x, terms[0], preferred_element_type=jnp.float32)
    for n in (1, 2):
        total = total + jnp.dot(x, terms[n], preferred_element_type=jnp.float32)
    return total.astype(jnp.bfloat16)


def stack(*arrays):
    return jnp.concatenate(arrays, axis=0)


def gram(left, right):
    return lax.dot_general(
        left, right, (((1,), (1,)), ((), ())), preferred_element_type=jnp.float32
    )


def over_rows(pair, seq_len):
    rows, columns = pair.shape
    return pair.reshape(rows // seq_len, seq_len, columns).sum(axis=1)


def pick_columns(sums, pick):
    rest, terms = sums, []
    for _ in range(3):
        terms.append(rest.astype(jnp.bfloat16))
        rest = rest - terms[-1].astype(jnp.float32)
    n = sums.shape[0]
    out = jnp.dot(stack(*terms), pick[...], preferred_element_type=jnp.float32)
    return out[:n] + out[n : 2 * n] + out[2 * n :]


def late_blocks():
    out = [(("uv", 0), [("v", 1), ("v", 2), ("v", 3)])]
    for slot, other in ((2, 3), (3, 2)):
        out.append((("u", slot), [("v", 1), ("v", other)]))
        out.append((("v", slot), [("u", 1), ("v", 1), ("u", other), ("v", other)]))
    return out


def place(got, columns, n):
    zeros = jnp.zeros((got.shape[0], n), jnp.float32)
    at = {(kind, slot): got[:, i * n : (i + 1) * n] for i, (kind, slot) in enumerate(columns)}
    return jnp.concatenate(
        [at.get((kind, slot), zeros) for slot in range(4) for kind in "uv"], axis=1
    )


def early_kernel(seq_len, terms, u0, va0, vg0, u3, u2, u1, vg3, vg2, vg1, white, sums, *grams):
    n = va0.shape[0]
    per = n // seq_len
    tok = {("u", i): (u[0], u[1]) for i, u in enumerate((u0, u1, u2, u3))}
    tok["v", 0] = (va0[...], vg0[...])
    for i, vg in ((1, vg1), (2, vg2), (3, vg3)):
        tok["v", i] = (None, vg[...])
    rows = [("u", 0), ("v", 0), ("u", 2), ("u", 3)]
    acts = whiten(stack(*[tok[r][0] for r in rows]), terms.at[0])
    white[...] = acts
    rows = rows + [("v", 2), ("v", 3)]
    grads = whiten(stack(*[tok[r][1] for r in rows]), terms.at[1])
    part = {r: slice(i * n, (i + 1) * n) for i, r in enumerate(rows)}
    part["uv", 0] = slice(0, 2 * n)
    now = (
        (("uv", 0), [("u", 0), ("v", 0), ("u", 1), ("u", 2), ("u", 3)]),
        (("u", 2), [("u", 1), ("u", 3)]),
        (("u", 3), [("u", 1), ("u", 2)]),
    )
    lines = {}
    for row, columns in now:
        pair = gram(acts[part[row]], stack(*[tok[c][0] for c in columns])) * gram(
            grads[part[row]], stack(*[tok[c][1] for c in columns])
        )
        lines[row] = place(over_rows(pair, seq_len), columns, n)
    none = jnp.zeros((per, 8 * n), jnp.float32)
    sums[...] = stack(lines["uv", 0], lines["u", 2], none, lines["u", 3], none)
    for out, (row, columns) in zip(grams, late_blocks()):
        out[...] = gram(grads[part[row]], stack(*[tok[c][1] for c in columns]))


def partner_kernel(
    seq_len, terms, white, pick, sums, g2u, g2v, g3u, g3v, u3, u2, u1, va3, va2, va1, by_x, by_z
):
    n = va1.shape[0]
    per = n // seq_len
    tok = {("u", i): u[0] for i, u in ((1, u1), (2, u2), (3, u3))}
    tok |= {("v", i): va[...] for i, va in ((1, va1), (2, va2), (3, va3))}
    fresh = whiten(stack(tok["v", 2], tok["v", 3]), terms.at[0])
    left = {
        ("u", 2): white[2 * n : 3 * n],
        ("u", 3): white[3 * n : 4 * n],
        ("v", 2): fresh[:n],
        ("v", 3): fresh[n:],
    }
    lines = []
    for other, (row, columns) in zip((g2u, g2v, g3u, g3v), late_blocks()[1:]):
        pair = gram(left[row], stack(*[tok[c] for c in columns])) * other[...]
        lines.append(place(over_rows(pair, seq_len), columns, n))
    picked = pick_columns(sums[2 * per :, :] + stack(*lines), pick)
    by_x[...] = picked[: 2 * per]
    by_z[...] = picked[2 * per :]


def rows_kernel(seq_len, white, pick, sums, g0, va3, va2, va1, out):
    n = va1.shape[0]
    per = n // seq_len
    columns = late_blocks()[0][1]
    pair = gram(white[: 2 * n], stack(va1[...], va2[...], va3[...])) * g0[...]
    late = place(over_rows(pair, seq_len), columns, n)
    out[...] = pick_columns(sums[: 2 * per, :] + late, pick)


def call(kernel, name, flops, limit, operands, specs, out_shape, scratch=(), **more):
    vmem = pl.BlockSpec(memory_space=pltpu.VMEM)
    return pl.pallas_call(
        kernel,
        out_shape=out_shape,
        in_specs=specs + [vmem] * (len(operands) - len(specs)),
        out_specs=jax.tree.map(lambda _: vmem, out_shape),
        scratch_shapes=scratch,
        compiler_params=pltpu.CompilerParams(vmem_limit_bytes=int(limit * 1024 * 1024)),
        cost_estimate=pl.CostEstimate(flops=flops, bytes_accessed=10**6, transcendentals=0),
        name=name,
        **more,
    )(*operands)


def paired(activations, out_grads, lengths, layer_ids, flagged, act_factor, grad_factor):
    size = 16
    per = lengths.shape[0]
    tokens, rank = activations.shape[1:]
    seq_len = tokens // per
    f32, bf16 = jnp.float32, jnp.bfloat16

    def send(x, to):
        return lax.ppermute(x, "blk", [(d, to(d)) for d in range(size)])

    def opposite(d):
        return d ^ 8

    ways = (z_near, lambda d: d ^ 2, lambda d: d ^ 1)
    hbm = pl.BlockSpec(memory_space=pltpu.HBM)
    smem = pl.BlockSpec(memory_space=pltpu.SMEM)
    shape = jax.ShapeDtypeStruct
    columns = flagged.shape[0]
    half_unit = shape((tokens, rank), bf16)
    data = (activations, out_grads)
    lens = lengths.reshape(1, -1)
    away_acts, away_grads = call(
        away_kernel,
        "away",
        3 * 10**9,
        53.71,
        data,
        [hbm, hbm],
        (half_unit, half_unit),
        [pltpu.SemaphoreType.DMA((2,))],
    )
    vg = send(away_grads, opposite)
    away_acts = call(
        functools.partial(away_mask_kernel, seq_len),
        "away_mask",
        10**4,
        40,
        (lens, away_acts),
        [],
        half_unit,
        input_output_aliases={1: 0},
    )
    va = send(away_acts, opposite)
    away_acts, lens, *data = lax.optimization_barrier((away_acts, lens, *data))
    own = call(
        functools.partial(own_kernel, seq_len),
        "own",
        10**4,
        40,
        (lens, *data),
        [],
        shape((2, tokens, rank), bf16),
    )
    near = [send(own, to) for to in ways]
    own, layer_ids = lax.optimization_barrier((own, layer_ids))
    terms = call(
        terms_kernel,
        "factor_terms",
        10**4,
        51,
        (layer_ids, act_factor, grad_factor),
        [smem, hbm, hbm],
        shape((2, 3, rank, rank), bf16),
        [pltpu.VMEM((2, rank, rank), f32), pltpu.SemaphoreType.DMA((2,))],
    )
    vg, terms, flags = lax.optimization_barrier((vg, terms, flagged.reshape(1, -1)))
    pick = call(
        functools.partial(pick_kernel, seq_len, per, rank),
        "column_pick",
        15 * 10**8,
        40,
        (flags,),
        [],
        shape((8 * tokens, columns), bf16),
    )
    vg, pick, near = lax.optimization_barrier((vg, pick, near))
    late_grads = [send(vg, to) for to in ways]
    late_acts = [send(va, to) for to in ways]
    size_of = {"uv": 2, "u": 1, "v": 1}
    white, sums, *grams = call(
        functools.partial(early_kernel, seq_len),
        "early_pairs",
        10**9,
        40,
        (terms, own, va, vg, *near, *late_grads),
        [],
        [shape((4 * tokens, rank), bf16), shape((6 * per, 8 * tokens), f32)]
        + [
            shape((size_of[row[0]] * tokens, len(cols) * tokens), f32)
            for row, cols in late_blocks()
        ],
    )
    rows = shape((2 * per, columns), f32)
    by_x, by_z = call(
        functools.partial(partner_kernel, seq_len),
        "partner_rows",
        10**9,
        40,
        (terms, white, pick, sums, *grams[1:], *near, *late_acts),
        [],
        (rows, rows),
    )
    mine = call(
        functools.partial(rows_kernel, seq_len),
        "own_rows",
        10**9,
        40,
        (white, pick, sums, grams[0], *late_acts),
        [],
        rows,
    )
    half_sum = mine + send(by_x, lambda d: d ^ 2) + send(by_z, z_near)
    return half_sum[:per] + send(half_sum[per:], opposite)


def solution(mesh):
    in_specs = (
        P(None, ("grp", "blk"), None),
        P(None, ("grp", "blk"), None),
        P(("grp", "blk")),
        P("grp"),
        P("grp"),
        P(),
        P(),
    )
    out_specs = P(("grp", "blk"), None)
    shards = paired if mesh.shape["blk"] == 16 else gathered
    return jax.shard_map(shards, mesh=mesh, in_specs=in_specs, out_specs=out_specs, check_vma=False)
```

```python
import functools

import jax
import jax.numpy as jnp
from jax import lax
from jax.experimental import pallas as pl
from jax.experimental.pallas import tpu as pltpu
from jax.sharding import PartitionSpec as P

HIGHEST = lax.Precision.HIGHEST


def tile_scores(white_acts, white_grads, remote_acts, remote_grads, seq_len):
    gram_acts = jnp.einsum(
        "lqr,lkr->lqk", white_acts, remote_acts, preferred_element_type=jnp.float32
    )
    gram_grads = jnp.einsum(
        "lqr,lkr->lqk", white_grads, remote_grads, preferred_element_type=jnp.float32
    )
    pair = jnp.sum(gram_acts * gram_grads, axis=0)
    rows = pair.shape[0] // seq_len
    columns = pair.shape[1] // seq_len
    width = white_acts.shape[2]
    return pair.reshape(rows, seq_len, columns, seq_len).sum(axis=(1, 3)) * (
        1.0 / (width * seq_len)
    )


def gathered(activations, out_grads, lengths, layer_ids, flagged, act_factor, grad_factor):
    tok_rows = activations.shape[1]
    seq_count = lengths.shape[0]
    seq_len = tok_rows // seq_count
    slots = jnp.arange(tok_rows) % seq_len
    keep = (slots < jnp.repeat(lengths, seq_len)).astype(jnp.bfloat16)
    masked_acts = activations * keep[None, :, None]
    masked_grads = out_grads * keep[None, :, None]
    picked_act = jnp.take(act_factor, layer_ids, axis=0)
    picked_grad = jnp.take(grad_factor, layer_ids, axis=0)
    white_acts = jnp.einsum(
        "ltr,lrs->lts", masked_acts.astype(jnp.float32), picked_act, precision=HIGHEST
    ).astype(jnp.bfloat16)
    white_grads = jnp.einsum(
        "ltr,lrs->lts", masked_grads.astype(jnp.float32), picked_grad, precision=HIGHEST
    ).astype(jnp.bfloat16)
    part_scores = tile_scores(
        white_acts,
        white_grads,
        lax.all_gather(masked_acts, "blk", axis=1, tiled=True),
        lax.all_gather(masked_grads, "blk", axis=1, tiled=True),
        seq_len,
    )
    return jnp.take(part_scores, flagged, axis=1)


INNER = range(4, 12)
OUTER = (0, 1, 2, 3, 12, 13, 14, 15)


def z_near(d):
    return d ^ 4 ^ ((d >> 1) & 1)


def away_kernel(acts, grads, out, sems):
    layer = 1 - lax.axis_index("blk") // 8
    copies = [
        pltpu.make_async_copy(src.at[layer], out.at[i], sems.at[i])
        for i, src in enumerate((acts, grads))
    ]
    for copy in copies:
        copy.start()
    for copy in copies:
        copy.wait()


def masked_acts(x, lens, seq_len):
    row = lax.broadcasted_iota(jnp.int32, (x.shape[0], 1), 0)
    bound = jnp.zeros_like(row)
    for s in range(x.shape[0] // seq_len):
        bound = jnp.where(row // seq_len == s, lens[0:1, s : s + 1] + s * seq_len, bound)
    return jnp.where(row < bound, x, jnp.zeros_like(x))


def away_mask_kernel(seq_len, lens, unit, out):
    out[0] = masked_acts(unit[0], lens, seq_len)
    out[1] = unit[1]


def own_kernel(seq_len, lens, acts, grads, out):
    half = lax.axis_index("blk") // 8
    out[0] = masked_acts(acts[half], lens, seq_len)
    out[1] = grads[half]


def whiten(x, terms):
    total = jnp.dot(x, terms[0], preferred_element_type=jnp.float32)
    for n in (1, 2):
        total = total + jnp.dot(x, terms[n], preferred_element_type=jnp.float32)
    return total.astype(jnp.bfloat16)


def stack(*arrays):
    return jnp.concatenate(arrays, axis=0)


def block(seq_len, left, right):
    grams = [
        lax.dot_general(a, b, (((1,), (1,)), ((), ())), preferred_element_type=jnp.float32)
        for a, b in zip(left, right)
    ]
    rows, columns = grams[0].shape
    return (grams[0] * grams[1]).reshape(rows // seq_len, seq_len, columns).sum(axis=1)


def pick_columns(sums, pick):
    rest, terms = sums, []
    for _ in range(3):
        terms.append(rest.astype(jnp.bfloat16))
        rest = rest - terms[-1].astype(jnp.float32)
    n = sums.shape[0]
    out = jnp.dot(stack(*terms), pick[...], preferred_element_type=jnp.float32)
    return out[:n] + out[n : 2 * n] + out[2 * n :]


def setup_kernel(seq_len, per, layer_ids, flagged, act_f, grad_f, terms, pick, factor, sems):
    d = lax.axis_index("blk")
    layer = layer_ids[d // 8]
    copies = [
        pltpu.make_async_copy(src.at[layer], factor.at[i], sems.at[i])
        for i, src in enumerate((act_f, grad_f))
    ]
    for copy in copies:
        copy.start()
    token = lax.broadcasted_iota(jnp.int32, pick.shape, 0)
    spot = token // (seq_len * per)
    slot = spot // 2
    owner = jnp.where(
        slot == 0, d, jnp.where(slot == 1, d ^ 1, jnp.where(slot == 2, d ^ 2, z_near(d)))
    )
    owner = owner ^ (8 * (spot % 2))
    seq = owner * per + token // seq_len % per
    scale = 1.0 / (factor.shape[1] * seq_len)
    pick[...] = jnp.where(seq == flagged[...], scale, 0.0).astype(pick.dtype)
    for w, copy in enumerate(copies):
        copy.wait()
        rest = factor[w]
        for t in range(3):
            term = rest.astype(jnp.bfloat16)
            terms[w, t] = term
            rest = rest - term.astype(jnp.float32)


def early_kernel(seq_len, per, terms, u0, v, u3, u2, u1, white, sums):
    n = u0.shape[1]
    mine, x, z = [], [], []
    for w in range(2):
        rows = whiten(stack(u0[w], v[w], u2[w], u3[w]), terms.at[w])
        white[w] = rows
        mine.append(rows[: 2 * n])
        x.append(rows[2 * n : 3 * n])
        z.append(rows[3 * n :])
    tok = [[u[w] for w in range(2)] for u in (u0, u1, u2, u3)]
    own = [stack(u0[w], v[w]) for w in range(2)]
    sums[...] = jnp.zeros_like(sums)
    r = 2 * per
    sums[0:r, 0 : 2 * n] = block(seq_len, mine, own)
    for slot in (1, 2, 3):
        at = 2 * n * slot
        sums[0:r, at : at + n] = block(seq_len, mine, tok[slot])
    for row, left, slots in ((r, x, (1, 3)), (2 * r, z, (1, 2))):
        for slot in slots:
            at = 2 * n * slot
            sums[row : row + per, at : at + n] = block(seq_len, left, tok[slot])


def return_kernel(seq_len, per, terms, white, pick, sums, u3, u2, u1, v2_in, v3, v2_out, v1, *outs):
    v = (v1, v2_in[...] + v2_out[...], v3)
    n = u1.shape[1]
    late = [[v[i][w] for w in range(2)] for i in range(3)]
    tok = [[u[w] for w in range(2)] for u in (u1, u2, u3)]
    both = [[stack(tok[i][w], late[i][w]) for w in range(2)] for i in range(3)]
    fresh = [whiten(stack(late[1][w], late[2][w]), terms.at[w]) for w in range(2)]
    zeros = jnp.zeros((per, n), jnp.float32)
    wide = jnp.zeros((per, 2 * n), jnp.float32)
    lines = []
    for i, other in ((1, 2), (2, 1)):
        early = [white[w, (i + 1) * n : (i + 2) * n] for w in range(2)]
        got = block(seq_len, early, [stack(late[0][w], late[other][w]) for w in range(2)])
        cols = {1: jnp.concatenate([zeros, got[:, :n]], axis=1)}
        cols[other + 1] = jnp.concatenate([zeros, got[:, n:]], axis=1)
        lines.append(jnp.concatenate([cols.get(slot, wide) for slot in range(4)], axis=1))
        new = [fresh[w][(i - 1) * n : i * n] for w in range(2)]
        cols = {1: block(seq_len, new, both[0]), other + 1: block(seq_len, new, both[other])}
        lines.append(jnp.concatenate([cols.get(slot, wide) for slot in range(4)], axis=1))
    r = 2 * per
    picked = pick_columns(sums[r:, :] + stack(*lines), pick)
    for i, out in enumerate(outs):
        out[...] = picked[i * r : (i + 1) * r]


def rows_kernel(seq_len, per, white, pick, sums, v2_in, v3, v2_out, v1, out):
    v = (v1, v2_in[...] + v2_out[...], v3)
    n = v[0].shape[1]
    r = 2 * per
    mine = [white[w, : 2 * n] for w in range(2)]
    line = [jnp.zeros((r, 2 * n), jnp.float32)]
    for i in range(3):
        right = [v[i][w] for w in range(2)]
        line += [jnp.zeros((r, n), jnp.float32), block(seq_len, mine, right)]
    out[...] = pick_columns(sums[:r, :] + jnp.concatenate(line, axis=1), pick)


def call(kernel, name, flops, limit, operands, specs, out_shape, scratch=(), **more):
    vmem = pl.BlockSpec(memory_space=pltpu.VMEM)
    return pl.pallas_call(
        kernel,
        out_shape=out_shape,
        in_specs=specs + [vmem] * (len(operands) - len(specs)),
        out_specs=jax.tree.map(lambda _: vmem, out_shape),
        scratch_shapes=scratch,
        compiler_params=pltpu.CompilerParams(vmem_limit_bytes=int(limit * 1024 * 1024)),
        cost_estimate=pl.CostEstimate(flops=flops, bytes_accessed=10**6, transcendentals=0),
        name=name,
        **more,
    )(*operands)


def paired(activations, out_grads, lengths, layer_ids, flagged, act_factor, grad_factor):
    per = lengths.shape[0]
    tokens, rank = activations.shape[1:]
    seq_len = tokens // per
    f32, bf16 = jnp.float32, jnp.bfloat16

    def send(x, to, among=range(16)):
        return lax.ppermute(x, "blk", [(d, to(d)) for d in among])

    def opposite(d):
        return d ^ 8

    ways = (z_near, lambda d: d ^ 2, lambda d: d ^ 1)
    hbm = pl.BlockSpec(memory_space=pltpu.HBM)
    vmem = pl.BlockSpec(memory_space=pltpu.VMEM)
    shape = jax.ShapeDtypeStruct
    columns = flagged.shape[0]
    unit = shape((2, tokens, rank), bf16)
    data = (activations, out_grads)
    lens = lengths.reshape(1, -1)
    copies = [pltpu.SemaphoreType.DMA((2,))]
    away = call(away_kernel, "away", 3 * 10**9, 53.71, data, [hbm, hbm], unit, copies)
    away = call(
        functools.partial(away_mask_kernel, seq_len),
        "away_mask",
        10**4,
        40,
        (lens, away),
        [],
        unit,
        input_output_aliases={1: 0},
    )
    v = send(away, opposite)
    away, lens, *data = lax.optimization_barrier((away, lens, *data))
    own = call(
        functools.partial(own_kernel, seq_len), "own", 10**9, 40, (lens, *data), [], unit
    )
    near = [send(own, to) for to in ways]
    terms, pick = call(
        functools.partial(setup_kernel, seq_len, per),
        "factor_terms",
        10**9,
        51,
        (layer_ids, flagged.reshape(1, -1), act_factor, grad_factor),
        [pl.BlockSpec(memory_space=pltpu.SMEM), vmem, hbm, hbm],
        (shape((2, 3, rank, rank), bf16), shape((8 * tokens, columns), bf16)),
        [pltpu.VMEM((2, rank, rank), f32), pltpu.SemaphoreType.DMA((2,))],
    )
    v, terms, pick = lax.optimization_barrier((v, terms, pick))
    late = [send(v, lambda d: d ^ 2, INNER)]
    late += [send(v, z_near), send(v, lambda d: d ^ 2, OUTER), send(v, lambda d: d ^ 1)]
    white, sums = call(
        functools.partial(early_kernel, seq_len, per),
        "early_pairs",
        10**9,
        40,
        (terms, own, v, *near),
        [],
        (shape((2, 4 * tokens, rank), bf16), shape((6 * per, 8 * tokens), f32)),
    )
    rows = shape((2 * per, columns), f32)
    by_x, by_z = call(
        functools.partial(return_kernel, seq_len, per),
        "return_rows",
        10**9,
        40,
        (terms, white, pick, sums, *near, *late),
        [],
        (rows, rows),
    )
    mine = call(
        functools.partial(rows_kernel, seq_len, per),
        "own_rows",
        10**9,
        40,
        (white, pick, sums, *late),
        [],
        rows,
    )
    half_sum = mine + send(by_x, lambda d: d ^ 2) + send(by_z, z_near)
    return half_sum[:per] + send(half_sum[per:], opposite)


def solution(mesh):
    in_specs = (
        P(None, ("grp", "blk"), None),
        P(None, ("grp", "blk"), None),
        P(("grp", "blk")),
        P("grp"),
        P("grp"),
        P(),
        P(),
    )
    out_specs = P(("grp", "blk"), None)
    shards = paired if mesh.shape["blk"] == 16 else gathered
    return jax.shard_map(shards, mesh=mesh, in_specs=in_specs, out_specs=out_specs, check_vma=False)
```

```python
import functools

import jax
import jax.numpy as jnp
from jax import lax
from jax.experimental import pallas as pl
from jax.experimental.pallas import tpu as pltpu
from jax.sharding import PartitionSpec as P

HIGHEST = lax.Precision.HIGHEST


def tile_scores(white_acts, white_grads, remote_acts, remote_grads, seq_len):
    gram_acts = jnp.einsum(
        "lqr,lkr->lqk", white_acts, remote_acts, preferred_element_type=jnp.float32
    )
    gram_grads = jnp.einsum(
        "lqr,lkr->lqk", white_grads, remote_grads, preferred_element_type=jnp.float32
    )
    pair = jnp.sum(gram_acts * gram_grads, axis=0)
    rows = pair.shape[0] // seq_len
    columns = pair.shape[1] // seq_len
    width = white_acts.shape[2]
    return pair.reshape(rows, seq_len, columns, seq_len).sum(axis=(1, 3)) * (
        1.0 / (width * seq_len)
    )


def gathered(activations, out_grads, lengths, layer_ids, flagged, act_factor, grad_factor):
    tok_rows = activations.shape[1]
    seq_count = lengths.shape[0]
    seq_len = tok_rows // seq_count
    slots = jnp.arange(tok_rows) % seq_len
    keep = (slots < jnp.repeat(lengths, seq_len)).astype(jnp.bfloat16)
    masked_acts = activations * keep[None, :, None]
    masked_grads = out_grads * keep[None, :, None]
    picked_act = jnp.take(act_factor, layer_ids, axis=0)
    picked_grad = jnp.take(grad_factor, layer_ids, axis=0)
    white_acts = jnp.einsum(
        "ltr,lrs->lts", masked_acts.astype(jnp.float32), picked_act, precision=HIGHEST
    ).astype(jnp.bfloat16)
    white_grads = jnp.einsum(
        "ltr,lrs->lts", masked_grads.astype(jnp.float32), picked_grad, precision=HIGHEST
    ).astype(jnp.bfloat16)
    part_scores = tile_scores(
        white_acts,
        white_grads,
        lax.all_gather(masked_acts, "blk", axis=1, tiled=True),
        lax.all_gather(masked_grads, "blk", axis=1, tiled=True),
        seq_len,
    )
    return jnp.take(part_scores, flagged, axis=1)


def z_near(d):
    return d ^ 4 ^ ((d >> 1) & 1)


def away_kernel(acts, grads, out, sems):
    layer = 1 - lax.axis_index("blk") // 8
    copies = [
        pltpu.make_async_copy(src.at[layer], out.at[i], sems.at[i])
        for i, src in enumerate((acts, grads))
    ]
    for copy in copies:
        copy.start()
    for copy in copies:
        copy.wait()


def masked_acts(x, lens, seq_len):
    row = lax.broadcasted_iota(jnp.int32, (x.shape[0], 1), 0)
    bound = jnp.zeros_like(row)
    for s in range(x.shape[0] // seq_len):
        bound = jnp.where(row // seq_len == s, lens[0:1, s : s + 1] + s * seq_len, bound)
    return jnp.where(row < bound, x, jnp.zeros_like(x))


def away_mask_kernel(seq_len, lens, unit, out):
    out[0] = masked_acts(unit[0], lens, seq_len)
    out[1] = unit[1]


def own_kernel(seq_len, lens, acts, grads, out):
    half = lax.axis_index("blk") // 8
    out[0] = masked_acts(acts[half], lens, seq_len)
    out[1] = grads[half]


def whiten(x, terms):
    total = jnp.dot(x, terms[0], preferred_element_type=jnp.float32)
    for n in (1, 2):
        total = total + jnp.dot(x, terms[n], preferred_element_type=jnp.float32)
    return total.astype(jnp.bfloat16)


def stack(*arrays):
    return jnp.concatenate(arrays, axis=0)


def block(seq_len, left, right):
    grams = [
        lax.dot_general(a, b, (((1,), (1,)), ((), ())), preferred_element_type=jnp.float32)
        for a, b in zip(left, right)
    ]
    rows, columns = grams[0].shape
    return (grams[0] * grams[1]).reshape(rows // seq_len, seq_len, columns).sum(axis=1)


def pick_columns(sums, pick):
    rest, terms = sums, []
    for _ in range(3):
        terms.append(rest.astype(jnp.bfloat16))
        rest = rest - terms[-1].astype(jnp.float32)
    n = sums.shape[0]
    out = jnp.dot(stack(*terms), pick[...], preferred_element_type=jnp.float32)
    return out[:n] + out[n : 2 * n] + out[2 * n :]


def setup_kernel(seq_len, per, layer_ids, flagged, act_f, grad_f, terms, pick, factor, sems):
    d = lax.axis_index("blk")
    layer = layer_ids[d // 8]
    copies = [
        pltpu.make_async_copy(src.at[layer], factor.at[i], sems.at[i])
        for i, src in enumerate((act_f, grad_f))
    ]
    for copy in copies:
        copy.start()
    token = lax.broadcasted_iota(jnp.int32, pick.shape, 0)
    spot = token // (seq_len * per)
    slot = spot // 2
    owner = jnp.where(
        slot == 0, d, jnp.where(slot == 1, d ^ 1, jnp.where(slot == 2, d ^ 2, z_near(d)))
    )
    owner = owner ^ (8 * (spot % 2))
    seq = owner * per + token // seq_len % per
    scale = 1.0 / (factor.shape[1] * seq_len)
    pick[...] = jnp.where(seq == flagged[...], scale, 0.0).astype(pick.dtype)
    for w, copy in enumerate(copies):
        copy.wait()
        rest = factor[w]
        for t in range(3):
            term = rest.astype(jnp.bfloat16)
            terms[w, t] = term
            rest = rest - term.astype(jnp.float32)


def early_kernel(seq_len, per, terms, u0, v, u3, u2, u1, white, mine, side):
    n = u0.shape[1]
    rows = []
    for w in range(2):
        white[w] = whiten(stack(u0[w], v[w], u2[w], u3[w], u1[w]), terms.at[w])
        rows.append(white[w])
    left = {
        0: [r[: 2 * n] for r in rows],
        2: [r[2 * n : 3 * n] for r in rows],
        3: [r[3 * n : 4 * n] for r in rows],
    }
    tok = [[u[w] for w in range(2)] for u in (u0, u1, u2, u3)]
    mine[...] = jnp.zeros_like(mine)
    mine[:, 0 : 2 * n] = block(seq_len, left[0], [stack(u0[w], v[w]) for w in range(2)])
    for slot in (1, 2, 3):
        at = 2 * n * slot
        mine[:, at : at + n] = block(seq_len, left[0], tok[slot])
    side[...] = jnp.zeros_like(side)
    for row, slot, other in ((0, 2, 3), (2 * per, 3, 2)):
        for column in (1, other):
            at = 2 * n * (column - 1)
            side[row : row + per, at : at + n] = block(seq_len, left[slot], tok[column])


def core_kernel(seq_len, per, terms, white, v1, mine, side, white1, mine_out, side_out):
    n = v1.shape[1]
    tok = [v1[w] for w in range(2)]
    for w in range(2):
        white1[w] = whiten(tok[w], terms.at[w])
    mine_out[...] = mine[...]
    mine_out[:, 3 * n : 4 * n] = block(seq_len, [white[w, : 2 * n] for w in range(2)], tok)
    side_out[...] = side[...]
    got = block(seq_len, [white[w, 2 * n : 4 * n] for w in range(2)], tok)
    for i, row in enumerate((0, 2 * per)):
        side_out[row : row + per, n : 2 * n] = got[i * per : (i + 1) * per]


def z_kernel(seq_len, per, terms, white, u2, u1, v1, v3, side, white3, side_out):
    n = v1.shape[1]
    tok = [v3[w] for w in range(2)]
    fresh = [whiten(tok[w], terms.at[w]) for w in range(2)]
    for w in range(2):
        white3[w] = fresh[w]
    side_out[...] = side[...]
    side_out[0:per, 5 * n : 6 * n] = block(
        seq_len, [white[w, 2 * n : 3 * n] for w in range(2)], tok
    )
    side_out[3 * per : 4 * per, 0 : 3 * n] = block(
        seq_len, fresh, [stack(u1[w], v1[w], u2[w]) for w in range(2)]
    )


def return_kernel(seq_len, per, white, white1, white3, pick, side, v2, by_x, by_z):
    n = v2.shape[1]
    tok = [v2[w] for w in range(2)]
    columns = [
        stack(white[w, 4 * n : 5 * n], white1[w], white[w, 3 * n : 4 * n], white3[w])
        for w in range(2)
    ]
    by_row = block(seq_len, tok, columns)
    by_column = block(
        seq_len, [stack(white[w, 3 * n : 4 * n], white3[w]) for w in range(2)], tok
    )
    zeros = jnp.zeros((per, 2 * n), jnp.float32)
    none = jnp.zeros((per, 6 * n), jnp.float32)
    row = jnp.concatenate([by_row[:, : 2 * n], zeros, by_row[:, 2 * n :]], axis=1)
    lead = jnp.zeros((2 * per, 3 * n), jnp.float32)
    both = jnp.concatenate([lead, by_column, lead[:, : 2 * n]], axis=1)
    picked = pick_columns(side[...] + stack(none, row, both), pick.at[2 * n :])
    by_x[...] = picked[: 2 * per]
    by_z[...] = picked[2 * per :]


def rows_kernel(seq_len, per, white, pick, mine, v3, v2, out):
    n = v2.shape[1]
    left = [white[w, : 2 * n] for w in range(2)]
    got = block(seq_len, left, [stack(v2[w], v3[w]) for w in range(2)])
    zeros = jnp.zeros((2 * per, n), jnp.float32)
    late = jnp.concatenate([zeros] * 5 + [got[:, :n], zeros, got[:, n:]], axis=1)
    out[...] = pick_columns(mine[...] + late, pick)


def call(kernel, name, flops, limit, operands, specs, out_shape, scratch=(), **more):
    vmem = pl.BlockSpec(memory_space=pltpu.VMEM)
    return pl.pallas_call(
        kernel,
        out_shape=out_shape,
        in_specs=specs + [vmem] * (len(operands) - len(specs)),
        out_specs=jax.tree.map(lambda _: vmem, out_shape),
        scratch_shapes=scratch,
        compiler_params=pltpu.CompilerParams(vmem_limit_bytes=int(limit * 1024 * 1024)),
        cost_estimate=pl.CostEstimate(flops=flops, bytes_accessed=10**6, transcendentals=0),
        name=name,
        **more,
    )(*operands)


def paired(activations, out_grads, lengths, layer_ids, flagged, act_factor, grad_factor):
    size = 16
    per = lengths.shape[0]
    tokens, rank = activations.shape[1:]
    seq_len = tokens // per
    f32, bf16 = jnp.float32, jnp.bfloat16

    def send(x, to):
        return lax.ppermute(x, "blk", [(d, to(d)) for d in range(size)])

    def opposite(d):
        return d ^ 8

    ways = (z_near, lambda d: d ^ 2, lambda d: d ^ 1)
    hbm = pl.BlockSpec(memory_space=pltpu.HBM)
    vmem = pl.BlockSpec(memory_space=pltpu.VMEM)
    shape = jax.ShapeDtypeStruct
    columns = flagged.shape[0]
    unit = shape((2, tokens, rank), bf16)
    data = (activations, out_grads)
    lens = lengths.reshape(1, -1)
    copies = [pltpu.SemaphoreType.DMA((2,))]
    away = call(away_kernel, "away", 3 * 10**9, 53.71, data, [hbm, hbm], unit, copies)
    away = call(
        functools.partial(away_mask_kernel, seq_len),
        "away_mask",
        10**4,
        40,
        (lens, away),
        [],
        unit,
        input_output_aliases={1: 0},
    )
    v = send(away, opposite)
    away, lens, *data = lax.optimization_barrier((away, lens, *data))
    own = call(
        functools.partial(own_kernel, seq_len), "own", 10**9, 40, (lens, *data), [], unit
    )
    near = [send(own, to) for to in ways]
    terms, pick = call(
        functools.partial(setup_kernel, seq_len, per),
        "factor_terms",
        10**9,
        51,
        (layer_ids, flagged.reshape(1, -1), act_factor, grad_factor),
        [pl.BlockSpec(memory_space=pltpu.SMEM), vmem, hbm, hbm],
        (shape((2, 3, rank, rank), bf16), shape((8 * tokens, columns), bf16)),
        [pltpu.VMEM((2, rank, rank), f32), pltpu.SemaphoreType.DMA((2,))],
    )
    v, terms, pick = lax.optimization_barrier((v, terms, pick))
    late = [send(v, to) for to in ways]
    whole = shape((2 * per, 8 * tokens), f32)
    sides = shape((4 * per, 6 * tokens), f32)
    rows = shape((2 * per, columns), f32)
    u3, u2, u1 = near
    v3, v2, v1 = late

    def kernel(body, name, operands, out_shape, **more):
        body = functools.partial(body, seq_len, per)
        return call(body, name, 10**9, 40, operands, [], out_shape, **more)

    white, mine, side = kernel(
        early_kernel,
        "early_pairs",
        (terms, own, v, u3, u2, u1),
        (shape((2, 5 * tokens, rank), bf16), whole, sides),
    )
    white1, mine, side = kernel(
        core_kernel,
        "core_pairs",
        (terms, white, v1, mine, side),
        (unit, whole, sides),
        input_output_aliases={3: 1, 4: 2},
    )
    white3, side = kernel(
        z_kernel,
        "z_pairs",
        (terms, white, u2, u1, v1, v3, side),
        (unit, sides),
        input_output_aliases={6: 1},
    )
    by_x, by_z = kernel(
        return_kernel, "return_rows", (white, white1, white3, pick, side, v2), (rows, rows)
    )
    mine = kernel(rows_kernel, "own_rows", (white, pick, mine, v3, v2), rows)
    half_sum = mine + send(by_x, lambda d: d ^ 2) + send(by_z, z_near)
    return half_sum[:per] + send(half_sum[per:], opposite)


def solution(mesh):
    in_specs = (
        P(None, ("grp", "blk"), None),
        P(None, ("grp", "blk"), None),
        P(("grp", "blk")),
        P("grp"),
        P("grp"),
        P(),
        P(),
    )
    out_specs = P(("grp", "blk"), None)
    shards = paired if mesh.shape["blk"] == 16 else gathered
    return jax.shard_map(shards, mesh=mesh, in_specs=in_specs, out_specs=out_specs, check_vma=False)
```

```python
import functools

import jax
import jax.numpy as jnp
from jax import lax
from jax.experimental import pallas as pl
from jax.experimental.pallas import tpu as pltpu
from jax.sharding import PartitionSpec as P

HIGHEST = lax.Precision.HIGHEST


def tile_scores(white_acts, white_grads, remote_acts, remote_grads, seq_len):
    gram_acts = jnp.einsum(
        "lqr,lkr->lqk", white_acts, remote_acts, preferred_element_type=jnp.float32
    )
    gram_grads = jnp.einsum(
        "lqr,lkr->lqk", white_grads, remote_grads, preferred_element_type=jnp.float32
    )
    pair = jnp.sum(gram_acts * gram_grads, axis=0)
    rows = pair.shape[0] // seq_len
    columns = pair.shape[1] // seq_len
    width = white_acts.shape[2]
    return pair.reshape(rows, seq_len, columns, seq_len).sum(axis=(1, 3)) * (
        1.0 / (width * seq_len)
    )


def gathered(activations, out_grads, lengths, layer_ids, flagged, act_factor, grad_factor):
    tok_rows = activations.shape[1]
    seq_count = lengths.shape[0]
    seq_len = tok_rows // seq_count
    slots = jnp.arange(tok_rows) % seq_len
    keep = (slots < jnp.repeat(lengths, seq_len)).astype(jnp.bfloat16)
    masked_acts = activations * keep[None, :, None]
    masked_grads = out_grads * keep[None, :, None]
    picked_act = jnp.take(act_factor, layer_ids, axis=0)
    picked_grad = jnp.take(grad_factor, layer_ids, axis=0)
    white_acts = jnp.einsum(
        "ltr,lrs->lts", masked_acts.astype(jnp.float32), picked_act, precision=HIGHEST
    ).astype(jnp.bfloat16)
    white_grads = jnp.einsum(
        "ltr,lrs->lts", masked_grads.astype(jnp.float32), picked_grad, precision=HIGHEST
    ).astype(jnp.bfloat16)
    part_scores = tile_scores(
        white_acts,
        white_grads,
        lax.all_gather(masked_acts, "blk", axis=1, tiled=True),
        lax.all_gather(masked_grads, "blk", axis=1, tiled=True),
        seq_len,
    )
    return jnp.take(part_scores, flagged, axis=1)


def z_near(d):
    return d ^ 4 ^ ((d >> 1) & 1)


def away_kernel(acts, grads, out, sems):
    layer = 1 - lax.axis_index("blk") // 8
    copies = [
        pltpu.make_async_copy(src.at[layer], out.at[i], sems.at[i])
        for i, src in enumerate((acts, grads))
    ]
    for copy in copies:
        copy.start()
    for copy in copies:
        copy.wait()


def masked_acts(x, lens, seq_len):
    row = lax.broadcasted_iota(jnp.int32, (x.shape[0], 1), 0)
    bound = jnp.zeros_like(row)
    for s in range(x.shape[0] // seq_len):
        bound = jnp.where(row // seq_len == s, lens[0:1, s : s + 1] + s * seq_len, bound)
    return jnp.where(row < bound, x, jnp.zeros_like(x))


def away_mask_kernel(seq_len, lens, unit, out):
    out[0] = masked_acts(unit[0], lens, seq_len)
    out[1] = unit[1]


def own_kernel(seq_len, lens, acts, grads, out):
    half = lax.axis_index("blk") // 8
    out[0] = masked_acts(acts[half], lens, seq_len)
    out[1] = grads[half]


def whiten(x, terms):
    total = jnp.dot(x, terms[0], preferred_element_type=jnp.float32)
    for n in (1, 2):
        total = total + jnp.dot(x, terms[n], preferred_element_type=jnp.float32)
    return total.astype(jnp.bfloat16)


def stack(*arrays):
    return jnp.concatenate(arrays, axis=0)


def block(seq_len, left, right):
    grams = [
        lax.dot_general(a, b, (((1,), (1,)), ((), ())), preferred_element_type=jnp.float32)
        for a, b in zip(left, right)
    ]
    rows, columns = grams[0].shape
    return (grams[0] * grams[1]).reshape(rows // seq_len, seq_len, columns).sum(axis=1)


def pick_columns(sums, pick):
    rest, terms = sums, []
    for _ in range(3):
        terms.append(rest.astype(jnp.bfloat16))
        rest = rest - terms[-1].astype(jnp.float32)
    n = sums.shape[0]
    out = jnp.dot(stack(*terms), pick[...], preferred_element_type=jnp.float32)
    return out[:n] + out[n : 2 * n] + out[2 * n :]


def setup_kernel(seq_len, per, layer_ids, flagged, act_f, grad_f, terms, pick, factor, sems):
    d = lax.axis_index("blk")
    layer = layer_ids[d // 8]
    copies = [
        pltpu.make_async_copy(src.at[layer], factor.at[i], sems.at[i])
        for i, src in enumerate((act_f, grad_f))
    ]
    for copy in copies:
        copy.start()
    token = lax.broadcasted_iota(jnp.int32, pick.shape, 0)
    spot = token // (seq_len * per)
    slot = spot // 2
    owner = jnp.where(
        slot == 0, d, jnp.where(slot == 1, d ^ 1, jnp.where(slot == 2, d ^ 2, z_near(d)))
    )
    owner = owner ^ (8 * (spot % 2))
    seq = owner * per + token // seq_len % per
    scale = 1.0 / (factor.shape[1] * seq_len)
    pick[...] = jnp.where(seq == flagged[...], scale, 0.0).astype(pick.dtype)
    for w, copy in enumerate(copies):
        copy.wait()
        rest = factor[w]
        for t in range(3):
            term = rest.astype(jnp.bfloat16)
            terms[w, t] = term
            rest = rest - term.astype(jnp.float32)


def early_kernel(seq_len, per, terms, u0, v, u3, u2, u1, white, mine, side):
    n = u0.shape[1]
    rows = []
    for w in range(2):
        white[w] = whiten(stack(u0[w], v[w], u2[w], u3[w], u1[w]), terms.at[w])
        rows.append(white[w])
    left = {
        0: [r[: 2 * n] for r in rows],
        2: [r[2 * n : 3 * n] for r in rows],
        3: [r[3 * n : 4 * n] for r in rows],
    }
    tok = [[u[w] for w in range(2)] for u in (u0, u1, u2, u3)]
    mine[...] = jnp.zeros_like(mine)
    mine[:, 0 : 2 * n] = block(seq_len, left[0], [stack(u0[w], v[w]) for w in range(2)])
    for slot in (1, 2, 3):
        at = 2 * n * slot
        mine[:, at : at + n] = block(seq_len, left[0], tok[slot])
    side[...] = jnp.zeros_like(side)
    for row, slot, other in ((0, 2, 3), (2 * per, 3, 2)):
        for column in (1, other):
            at = 2 * n * (column - 1)
            side[row : row + per, at : at + n] = block(seq_len, left[slot], tok[column])


def z_kernel(seq_len, per, terms, white, u2, u1, v3, side, white3, side_out):
    n = v3.shape[1]
    tok = [v3[w] for w in range(2)]
    fresh = [whiten(tok[w], terms.at[w]) for w in range(2)]
    for w in range(2):
        white3[w] = fresh[w]
    side_out[...] = side[...]
    side_out[0:per, 5 * n : 6 * n] = block(
        seq_len, [white[w, 2 * n : 3 * n] for w in range(2)], tok
    )
    got = block(seq_len, fresh, [stack(u1[w], u2[w]) for w in range(2)])
    side_out[3 * per : 4 * per, 0:n] = got[:, :n]
    side_out[3 * per : 4 * per, 2 * n : 3 * n] = got[:, n:]


def return_kernel(seq_len, per, terms, white, white3, pick, side, v2, v1, by_z, by_x):
    n = v2.shape[1]
    x = [v2[w] for w in range(2)]
    core = [v1[w] for w in range(2)]
    columns = [
        stack(white[w, 4 * n : 5 * n], white[w, 3 * n : 4 * n], white3[w]) for w in range(2)
    ]
    near = block(seq_len, x, columns)
    far = block(seq_len, x, [whiten(core[w], terms.at[w]) for w in range(2)])
    at_core = block(seq_len, [stack(white[w, 2 * n : 4 * n], white3[w]) for w in range(2)], core)
    at_x = block(seq_len, [stack(white[w, 3 * n : 4 * n], white3[w]) for w in range(2)], x)
    zeros = jnp.zeros((per, n), jnp.float32)

    def line(*blocks):
        return jnp.concatenate([zeros if x is None else x for x in blocks], axis=1)

    late = stack(
        line(None, at_core[:per], None, None, None, None),
        line(near[:, :n], far, None, None, near[:, n : 2 * n], near[:, 2 * n :]),
        line(None, at_core[per : 2 * per], None, at_x[:per], None, None),
        line(None, at_core[2 * per :], None, at_x[per:], None, None),
    )
    picked = pick_columns(side[...] + late, pick.at[2 * n :])
    by_x[...] = picked[: 2 * per]
    by_z[...] = picked[2 * per :]


def rows_kernel(seq_len, per, white, pick, mine, v3, v2, v1, out):
    n = v2.shape[1]
    left = [white[w, : 2 * n] for w in range(2)]
    got = block(seq_len, left, [stack(v1[w], v2[w], v3[w]) for w in range(2)])
    zeros = jnp.zeros((2 * per, n), jnp.float32)
    late = [zeros, zeros]
    for i in range(3):
        late += [zeros, got[:, i * n : (i + 1) * n]]
    out[...] = pick_columns(mine[...] + jnp.concatenate(late, axis=1), pick)


def call(kernel, name, flops, limit, operands, specs, out_shape, scratch=(), **more):
    vmem = pl.BlockSpec(memory_space=pltpu.VMEM)
    return pl.pallas_call(
        kernel,
        out_shape=out_shape,
        in_specs=specs + [vmem] * (len(operands) - len(specs)),
        out_specs=jax.tree.map(lambda _: vmem, out_shape),
        scratch_shapes=scratch,
        compiler_params=pltpu.CompilerParams(vmem_limit_bytes=int(limit * 1024 * 1024)),
        cost_estimate=pl.CostEstimate(flops=flops, bytes_accessed=10**6, transcendentals=0),
        name=name,
        **more,
    )(*operands)


def paired(activations, out_grads, lengths, layer_ids, flagged, act_factor, grad_factor):
    size = 16
    per = lengths.shape[0]
    tokens, rank = activations.shape[1:]
    seq_len = tokens // per
    f32, bf16 = jnp.float32, jnp.bfloat16

    def send(x, to):
        return lax.ppermute(x, "blk", [(d, to(d)) for d in range(size)])

    def opposite(d):
        return d ^ 8

    ways = (z_near, lambda d: d ^ 2, lambda d: d ^ 1)
    hbm = pl.BlockSpec(memory_space=pltpu.HBM)
    vmem = pl.BlockSpec(memory_space=pltpu.VMEM)
    shape = jax.ShapeDtypeStruct
    columns = flagged.shape[0]
    unit = shape((2, tokens, rank), bf16)
    data = (activations, out_grads)
    lens = lengths.reshape(1, -1)
    copies = [pltpu.SemaphoreType.DMA((2,))]
    away = call(away_kernel, "away", 3 * 10**9, 53.71, data, [hbm, hbm], unit, copies)
    away = call(
        functools.partial(away_mask_kernel, seq_len),
        "away_mask",
        10**4,
        40,
        (lens, away),
        [],
        unit,
        input_output_aliases={1: 0},
    )
    v = send(away, opposite)
    away, lens, *data = lax.optimization_barrier((away, lens, *data))
    own = call(
        functools.partial(own_kernel, seq_len), "own", 10**9, 40, (lens, *data), [], unit
    )
    near = [send(own, to) for to in ways]
    terms, pick = call(
        functools.partial(setup_kernel, seq_len, per),
        "factor_terms",
        10**9,
        51,
        (layer_ids, flagged.reshape(1, -1), act_factor, grad_factor),
        [pl.BlockSpec(memory_space=pltpu.SMEM), vmem, hbm, hbm],
        (shape((2, 3, rank, rank), bf16), shape((8 * tokens, columns), bf16)),
        [pltpu.VMEM((2, rank, rank), f32), pltpu.SemaphoreType.DMA((2,))],
    )
    v, terms, pick = lax.optimization_barrier((v, terms, pick))
    late = [send(v, to) for to in ways]
    whole = shape((2 * per, 8 * tokens), f32)
    sides = shape((4 * per, 6 * tokens), f32)
    rows = shape((2 * per, columns), f32)
    u3, u2, u1 = near
    v3, v2, v1 = late

    def kernel(body, name, operands, out_shape, **more):
        body = functools.partial(body, seq_len, per)
        return call(body, name, 10**9, 40, operands, [], out_shape, **more)

    white, mine, side = kernel(
        early_kernel,
        "early_pairs",
        (terms, own, v, u3, u2, u1),
        (shape((2, 5 * tokens, rank), bf16), whole, sides),
    )
    white3, side = kernel(
        z_kernel,
        "z_pairs",
        (terms, white, u2, u1, v3, side),
        (unit, sides),
        input_output_aliases={5: 1},
    )
    by_z, by_x = kernel(
        return_kernel, "return_rows", (terms, white, white3, pick, side, v2, v1), (rows, rows)
    )
    mine = kernel(rows_kernel, "own_rows", (white, pick, mine, v3, v2, v1), rows)
    half_sum = mine + send(by_x, lambda d: d ^ 2) + send(by_z, z_near)
    return half_sum[:per] + send(half_sum[per:], opposite)


def solution(mesh):
    in_specs = (
        P(None, ("grp", "blk"), None),
        P(None, ("grp", "blk"), None),
        P(("grp", "blk")),
        P("grp"),
        P("grp"),
        P(),
        P(),
    )
    out_specs = P(("grp", "blk"), None)
    shards = paired if mesh.shape["blk"] == 16 else gathered
    return jax.shard_map(shards, mesh=mesh, in_specs=in_specs, out_specs=out_specs, check_vma=False)
```

```python
import functools

import jax
import jax.numpy as jnp
from jax import lax
from jax.experimental import pallas as pl
from jax.experimental.pallas import tpu as pltpu
from jax.sharding import PartitionSpec as P

HIGHEST = lax.Precision.HIGHEST


def tile_scores(white_acts, white_grads, remote_acts, remote_grads, seq_len):
    gram_acts = jnp.einsum(
        "lqr,lkr->lqk", white_acts, remote_acts, preferred_element_type=jnp.float32
    )
    gram_grads = jnp.einsum(
        "lqr,lkr->lqk", white_grads, remote_grads, preferred_element_type=jnp.float32
    )
    pair = jnp.sum(gram_acts * gram_grads, axis=0)
    rows = pair.shape[0] // seq_len
    columns = pair.shape[1] // seq_len
    width = white_acts.shape[2]
    return pair.reshape(rows, seq_len, columns, seq_len).sum(axis=(1, 3)) * (
        1.0 / (width * seq_len)
    )


def gathered(activations, out_grads, lengths, layer_ids, flagged, act_factor, grad_factor):
    tok_rows = activations.shape[1]
    seq_count = lengths.shape[0]
    seq_len = tok_rows // seq_count
    slots = jnp.arange(tok_rows) % seq_len
    keep = (slots < jnp.repeat(lengths, seq_len)).astype(jnp.bfloat16)
    masked_acts = activations * keep[None, :, None]
    masked_grads = out_grads * keep[None, :, None]
    picked_act = jnp.take(act_factor, layer_ids, axis=0)
    picked_grad = jnp.take(grad_factor, layer_ids, axis=0)
    white_acts = jnp.einsum(
        "ltr,lrs->lts", masked_acts.astype(jnp.float32), picked_act, precision=HIGHEST
    ).astype(jnp.bfloat16)
    white_grads = jnp.einsum(
        "ltr,lrs->lts", masked_grads.astype(jnp.float32), picked_grad, precision=HIGHEST
    ).astype(jnp.bfloat16)
    part_scores = tile_scores(
        white_acts,
        white_grads,
        lax.all_gather(masked_acts, "blk", axis=1, tiled=True),
        lax.all_gather(masked_grads, "blk", axis=1, tiled=True),
        seq_len,
    )
    return jnp.take(part_scores, flagged, axis=1)


def z_near(d):
    return d ^ 4 ^ ((d >> 1) & 1)


def away_kernel(acts, grads, out, sems):
    layer = 1 - lax.axis_index("blk") // 8
    copies = [
        pltpu.make_async_copy(src.at[layer], out.at[i], sems.at[i])
        for i, src in enumerate((acts, grads))
    ]
    for copy in copies:
        copy.start()
    for copy in copies:
        copy.wait()


def masked_acts(x, lens, seq_len):
    row = lax.broadcasted_iota(jnp.int32, (x.shape[0], 1), 0)
    bound = jnp.zeros_like(row)
    for s in range(x.shape[0] // seq_len):
        bound = jnp.where(row // seq_len == s, lens[0:1, s : s + 1] + s * seq_len, bound)
    return jnp.where(row < bound, x, jnp.zeros_like(x))


def away_mask_kernel(seq_len, lens, unit, out):
    out[0] = masked_acts(unit[0], lens, seq_len)
    out[1] = unit[1]


def own_kernel(seq_len, lens, acts, grads, out):
    half = lax.axis_index("blk") // 8
    out[0] = masked_acts(acts[half], lens, seq_len)
    out[1] = grads[half]


def whiten(x, terms):
    total = jnp.dot(x, terms[0], preferred_element_type=jnp.float32)
    for n in (1, 2):
        total = total + jnp.dot(x, terms[n], preferred_element_type=jnp.float32)
    return total.astype(jnp.bfloat16)


def stack(*arrays):
    return jnp.concatenate(arrays, axis=0)


def block(seq_len, left, right):
    grams = [
        lax.dot_general(a, b, (((1,), (1,)), ((), ())), preferred_element_type=jnp.float32)
        for a, b in zip(left, right)
    ]
    rows, columns = grams[0].shape
    return (grams[0] * grams[1]).reshape(rows // seq_len, seq_len, columns).sum(axis=1)


def pick_columns(sums, pick):
    rest, terms = sums, []
    for _ in range(3):
        terms.append(rest.astype(jnp.bfloat16))
        rest = rest - terms[-1].astype(jnp.float32)
    n = sums.shape[0]
    out = jnp.dot(stack(*terms), pick[...], preferred_element_type=jnp.float32)
    return out[:n] + out[n : 2 * n] + out[2 * n :]


def setup_kernel(seq_len, per, layer_ids, flagged, act_f, grad_f, terms, pick, factor, sems):
    d = lax.axis_index("blk")
    layer = layer_ids[d // 8]
    copies = [
        pltpu.make_async_copy(src.at[layer], factor.at[i], sems.at[i])
        for i, src in enumerate((act_f, grad_f))
    ]
    for copy in copies:
        copy.start()
    token = lax.broadcasted_iota(jnp.int32, pick.shape, 0)
    spot = token // (seq_len * per)
    slot = spot // 2
    owner = jnp.where(
        slot == 0, d, jnp.where(slot == 1, d ^ 1, jnp.where(slot == 2, d ^ 2, z_near(d)))
    )
    owner = owner ^ (8 * (spot % 2))
    seq = owner * per + token // seq_len % per
    scale = 1.0 / (factor.shape[1] * seq_len)
    pick[...] = jnp.where(seq == flagged[...], scale, 0.0).astype(pick.dtype)
    for w, copy in enumerate(copies):
        copy.wait()
        rest = factor[w]
        for t in range(3):
            term = rest.astype(jnp.bfloat16)
            terms[w, t] = term
            rest = rest - term.astype(jnp.float32)


def early_kernel(seq_len, per, terms, u0, v, u3, u2, u1, white, mine, side):
    n = u0.shape[1]
    rows = []
    for w in range(2):
        white[w] = whiten(stack(u0[w], v[w], u2[w], u3[w], u1[w]), terms.at[w])
        rows.append(white[w])
    left = {
        0: [r[: 2 * n] for r in rows],
        2: [r[2 * n : 3 * n] for r in rows],
        3: [r[3 * n : 4 * n] for r in rows],
    }
    tok = [[u[w] for w in range(2)] for u in (u0, u1, u2, u3)]
    mine[...] = jnp.zeros_like(mine)
    mine[:, 0 : 2 * n] = block(seq_len, left[0], [stack(u0[w], v[w]) for w in range(2)])
    for slot in (1, 2, 3):
        at = 2 * n * slot
        mine[:, at : at + n] = block(seq_len, left[0], tok[slot])
    side[...] = jnp.zeros_like(side)
    for row, slot, other in ((0, 2, 3), (2 * per, 3, 2)):
        for column in (1, other):
            at = 2 * n * (column - 1)
            side[row : row + per, at : at + n] = block(seq_len, left[slot], tok[column])


def z_kernel(seq_len, per, terms, white, u2, u1, v3, side, white3, side_out):
    n = v3.shape[1]
    tok = [v3[w] for w in range(2)]
    fresh = [whiten(tok[w], terms.at[w]) for w in range(2)]
    for w in range(2):
        white3[w] = fresh[w]
    side_out[...] = side[...]
    side_out[0:per, 5 * n : 6 * n] = block(
        seq_len, [white[w, 2 * n : 3 * n] for w in range(2)], tok
    )
    got = block(seq_len, fresh, [stack(u1[w], u2[w]) for w in range(2)])
    side_out[3 * per : 4 * per, 0:n] = got[:, :n]
    side_out[3 * per : 4 * per, 2 * n : 3 * n] = got[:, n:]


def return_kernel(seq_len, per, terms, white, white3, pick, side, v2, v1, by_z, by_x):
    n = v2.shape[1]
    x = [v2[w] for w in range(2)]
    core = [v1[w] for w in range(2)]
    columns = [
        stack(white[w, 4 * n : 5 * n], white[w, 3 * n : 4 * n], white3[w]) for w in range(2)
    ]
    near = block(seq_len, x, columns)
    far = block(seq_len, x, [whiten(core[w], terms.at[w]) for w in range(2)])
    at_core = block(seq_len, [stack(white[w, 2 * n : 4 * n], white3[w]) for w in range(2)], core)
    at_x = block(seq_len, [stack(white[w, 3 * n : 4 * n], white3[w]) for w in range(2)], x)
    zeros = jnp.zeros((per, n), jnp.float32)

    def line(*blocks):
        return jnp.concatenate([zeros if x is None else x for x in blocks], axis=1)

    late = stack(
        line(None, at_core[:per], None, None, None, None),
        line(near[:, :n], far, None, None, near[:, n : 2 * n], near[:, 2 * n :]),
        line(None, at_core[per : 2 * per], None, at_x[:per], None, None),
        line(None, at_core[2 * per :], None, at_x[per:], None, None),
    )
    picked = pick_columns(side[...] + late, pick.at[2 * n :])
    by_x[...] = picked[: 2 * per]
    by_z[...] = picked[2 * per :]


def rows_kernel(seq_len, per, white, pick, mine, v3, v2, v1, out):
    n = v2.shape[1]
    left = [white[w, : 2 * n] for w in range(2)]
    got = block(seq_len, left, [stack(v1[w], v2[w], v3[w]) for w in range(2)])
    zeros = jnp.zeros((2 * per, n), jnp.float32)
    late = [zeros, zeros]
    for i in range(3):
        late += [zeros, got[:, i * n : (i + 1) * n]]
    out[...] = pick_columns(mine[...] + jnp.concatenate(late, axis=1), pick)


def call(kernel, name, flops, limit, operands, specs, out_shape, scratch=(), **more):
    vmem = pl.BlockSpec(memory_space=pltpu.VMEM)
    return pl.pallas_call(
        kernel,
        out_shape=out_shape,
        in_specs=specs + [vmem] * (len(operands) - len(specs)),
        out_specs=jax.tree.map(lambda _: vmem, out_shape),
        scratch_shapes=scratch,
        compiler_params=pltpu.CompilerParams(vmem_limit_bytes=int(limit * 1024 * 1024)),
        cost_estimate=pl.CostEstimate(flops=flops, bytes_accessed=10**6, transcendentals=0),
        name=name,
        **more,
    )(*operands)


def paired(activations, out_grads, lengths, layer_ids, flagged, act_factor, grad_factor):
    size = 16
    per = lengths.shape[0]
    tokens, rank = activations.shape[1:]
    seq_len = tokens // per
    f32, bf16 = jnp.float32, jnp.bfloat16

    def send(x, to):
        return lax.ppermute(x, "blk", [(d, to(d)) for d in range(size)])

    def opposite(d):
        return d ^ 8

    ways = (z_near, lambda d: d ^ 2, lambda d: d ^ 1)
    hbm = pl.BlockSpec(memory_space=pltpu.HBM)
    vmem = pl.BlockSpec(memory_space=pltpu.VMEM)
    shape = jax.ShapeDtypeStruct
    columns = flagged.shape[0]
    unit = shape((2, tokens, rank), bf16)
    data = (activations, out_grads)
    lens = lengths.reshape(1, -1)
    copies = [pltpu.SemaphoreType.DMA((2,))]
    away = call(away_kernel, "away", 3 * 10**9, 53.71, data, [hbm, hbm], unit, copies)
    away = call(
        functools.partial(away_mask_kernel, seq_len),
        "away_mask",
        10**4,
        40,
        (lens, away),
        [],
        unit,
        input_output_aliases={1: 0},
    )
    v = send(away, opposite)
    away, lens, *data = lax.optimization_barrier((away, lens, *data))
    own = call(
        functools.partial(own_kernel, seq_len), "own", 10**9, 40, (lens, *data), [], unit
    )
    near = [send(own, to) for to in ways]
    terms, pick = call(
        functools.partial(setup_kernel, seq_len, per),
        "factor_terms",
        10**9,
        51,
        (layer_ids, flagged.reshape(1, -1), act_factor, grad_factor),
        [pl.BlockSpec(memory_space=pltpu.SMEM), vmem, hbm, hbm],
        (shape((2, 3, rank, rank), bf16), shape((8 * tokens, columns), bf16)),
        [pltpu.VMEM((2, rank, rank), f32), pltpu.SemaphoreType.DMA((2,))],
    )
    v, terms, pick = lax.optimization_barrier((v, terms, pick))
    late = [send(v, to) for to in ways[:2]]
    whole = shape((2 * per, 8 * tokens), f32)
    sides = shape((4 * per, 6 * tokens), f32)
    rows = shape((2 * per, columns), f32)
    u3, u2, u1 = near
    v3, v2 = late

    def kernel(body, name, operands, out_shape, **more):
        body = functools.partial(body, seq_len, per)
        return call(body, name, 10**9, 40, operands, [], out_shape, **more)

    white, mine, side = kernel(
        early_kernel,
        "early_pairs",
        (terms, own, v, u3, u2, u1),
        (shape((2, 5 * tokens, rank), bf16), whole, sides),
    )
    v, white = lax.optimization_barrier((v, white))
    v1 = send(v, ways[2])
    white3, side = kernel(
        z_kernel,
        "z_pairs",
        (terms, white, u2, u1, v3, side),
        (unit, sides),
        input_output_aliases={5: 1},
    )
    by_z, by_x = kernel(
        return_kernel, "return_rows", (terms, white, white3, pick, side, v2, v1), (rows, rows)
    )
    mine = kernel(rows_kernel, "own_rows", (white, pick, mine, v3, v2, v1), rows)
    half_sum = mine + send(by_x, lambda d: d ^ 2) + send(by_z, z_near)
    return half_sum[:per] + send(half_sum[per:], opposite)


def solution(mesh):
    in_specs = (
        P(None, ("grp", "blk"), None),
        P(None, ("grp", "blk"), None),
        P(("grp", "blk")),
        P("grp"),
        P("grp"),
        P(),
        P(),
    )
    out_specs = P(("grp", "blk"), None)
    shards = paired if mesh.shape["blk"] == 16 else gathered
    return jax.shard_map(shards, mesh=mesh, in_specs=in_specs, out_specs=out_specs, check_vma=False)
```

```python
import functools

import jax
import jax.numpy as jnp
from jax import lax
from jax.experimental import pallas as pl
from jax.experimental.pallas import tpu as pltpu
from jax.sharding import PartitionSpec as P

HIGHEST = lax.Precision.HIGHEST


def tile_scores(white_acts, white_grads, remote_acts, remote_grads, seq_len):
    gram_acts = jnp.einsum(
        "lqr,lkr->lqk", white_acts, remote_acts, preferred_element_type=jnp.float32
    )
    gram_grads = jnp.einsum(
        "lqr,lkr->lqk", white_grads, remote_grads, preferred_element_type=jnp.float32
    )
    pair = jnp.sum(gram_acts * gram_grads, axis=0)
    rows = pair.shape[0] // seq_len
    columns = pair.shape[1] // seq_len
    width = white_acts.shape[2]
    return pair.reshape(rows, seq_len, columns, seq_len).sum(axis=(1, 3)) * (
        1.0 / (width * seq_len)
    )


def gathered(activations, out_grads, lengths, layer_ids, flagged, act_factor, grad_factor):
    tok_rows = activations.shape[1]
    seq_count = lengths.shape[0]
    seq_len = tok_rows // seq_count
    slots = jnp.arange(tok_rows) % seq_len
    keep = (slots < jnp.repeat(lengths, seq_len)).astype(jnp.bfloat16)
    masked_acts = activations * keep[None, :, None]
    masked_grads = out_grads * keep[None, :, None]
    picked_act = jnp.take(act_factor, layer_ids, axis=0)
    picked_grad = jnp.take(grad_factor, layer_ids, axis=0)
    white_acts = jnp.einsum(
        "ltr,lrs->lts", masked_acts.astype(jnp.float32), picked_act, precision=HIGHEST
    ).astype(jnp.bfloat16)
    white_grads = jnp.einsum(
        "ltr,lrs->lts", masked_grads.astype(jnp.float32), picked_grad, precision=HIGHEST
    ).astype(jnp.bfloat16)
    part_scores = tile_scores(
        white_acts,
        white_grads,
        lax.all_gather(masked_acts, "blk", axis=1, tiled=True),
        lax.all_gather(masked_grads, "blk", axis=1, tiled=True),
        seq_len,
    )
    return jnp.take(part_scores, flagged, axis=1)


def z_near(d):
    return d ^ 4 ^ ((d >> 1) & 1)


def away_kernel(acts, grads, out, sems):
    layer = 1 - lax.axis_index("blk") // 8
    copies = [
        pltpu.make_async_copy(src.at[layer], out.at[i], sems.at[i])
        for i, src in enumerate((acts, grads))
    ]
    for copy in copies:
        copy.start()
    for copy in copies:
        copy.wait()


def masked_acts(x, lens, seq_len):
    row = lax.broadcasted_iota(jnp.int32, (x.shape[0], 1), 0)
    bound = jnp.zeros_like(row)
    for s in range(x.shape[0] // seq_len):
        bound = jnp.where(row // seq_len == s, lens[0:1, s : s + 1] + s * seq_len, bound)
    return jnp.where(row < bound, x, jnp.zeros_like(x))


def away_mask_kernel(seq_len, lens, unit, out):
    out[0] = masked_acts(unit[0], lens, seq_len)
    out[1] = unit[1]


def own_kernel(seq_len, lens, acts, grads, out):
    half = lax.axis_index("blk") // 8
    out[0] = masked_acts(acts[half], lens, seq_len)
    out[1] = grads[half]


def whiten(x, terms):
    total = jnp.dot(x, terms[0], preferred_element_type=jnp.float32)
    for n in (1, 2):
        total = total + jnp.dot(x, terms[n], preferred_element_type=jnp.float32)
    return total.astype(jnp.bfloat16)


def stack(*arrays):
    return jnp.concatenate(arrays, axis=0)


def block(seq_len, left, right):
    grams = [
        lax.dot_general(a, b, (((1,), (1,)), ((), ())), preferred_element_type=jnp.float32)
        for a, b in zip(left, right)
    ]
    rows, columns = grams[0].shape
    return (grams[0] * grams[1]).reshape(rows // seq_len, seq_len, columns).sum(axis=1)


def pick_columns(sums, pick):
    rest, terms = sums, []
    for _ in range(3):
        terms.append(rest.astype(jnp.bfloat16))
        rest = rest - terms[-1].astype(jnp.float32)
    n = sums.shape[0]
    out = jnp.dot(stack(*terms), pick[...], preferred_element_type=jnp.float32)
    return out[:n] + out[n : 2 * n] + out[2 * n :]


def setup_kernel(seq_len, per, layer_ids, flagged, act_f, grad_f, terms, pick, factor, sems):
    d = lax.axis_index("blk")
    layer = layer_ids[d // 8]
    copies = [
        pltpu.make_async_copy(src.at[layer], factor.at[i], sems.at[i])
        for i, src in enumerate((act_f, grad_f))
    ]
    for copy in copies:
        copy.start()
    token = lax.broadcasted_iota(jnp.int32, pick.shape, 0)
    spot = token // (seq_len * per)
    slot = spot // 2
    owner = jnp.where(
        slot == 0, d, jnp.where(slot == 1, d ^ 1, jnp.where(slot == 2, d ^ 2, z_near(d)))
    )
    owner = owner ^ (8 * (spot % 2))
    seq = owner * per + token // seq_len % per
    scale = 1.0 / (factor.shape[1] * seq_len)
    pick[...] = jnp.where(seq == flagged[...], scale, 0.0).astype(pick.dtype)
    for w, copy in enumerate(copies):
        copy.wait()
        rest = factor[w]
        for t in range(3):
            term = rest.astype(jnp.bfloat16)
            terms[w, t] = term
            rest = rest - term.astype(jnp.float32)


def early_kernel(seq_len, per, terms, u0, v, u3, u2, u1, white, mine, side):
    n = u0.shape[1]
    rows = []
    for w in range(2):
        white[w] = whiten(stack(u0[w], v[w], u2[w], u3[w], u1[w]), terms.at[w])
        rows.append(white[w])
    left = {
        0: [r[: 2 * n] for r in rows],
        2: [r[2 * n : 3 * n] for r in rows],
        3: [r[3 * n : 4 * n] for r in rows],
    }
    tok = [[u[w] for w in range(2)] for u in (u0, u1, u2, u3)]
    mine[...] = jnp.zeros_like(mine)
    mine[:, 0 : 2 * n] = block(seq_len, left[0], [stack(u0[w], v[w]) for w in range(2)])
    for slot in (1, 2, 3):
        at = 2 * n * slot
        mine[:, at : at + n] = block(seq_len, left[0], tok[slot])
    side[...] = jnp.zeros_like(side)
    for row, slot, other in ((0, 2, 3), (2 * per, 3, 2)):
        for column in (1, other):
            at = 2 * n * (column - 1)
            side[row : row + per, at : at + n] = block(seq_len, left[slot], tok[column])


def z_kernel(seq_len, per, terms, white, u2, u1, v3, side, white3, side_out):
    n = v3.shape[1]
    tok = [v3[w] for w in range(2)]
    fresh = [whiten(tok[w], terms.at[w]) for w in range(2)]
    for w in range(2):
        white3[w] = fresh[w]
    side_out[...] = side[...]
    side_out[0:per, 5 * n : 6 * n] = block(
        seq_len, [white[w, 2 * n : 3 * n] for w in range(2)], tok
    )
    got = block(seq_len, fresh, [stack(u1[w], u2[w]) for w in range(2)])
    side_out[3 * per : 4 * per, 0:n] = got[:, :n]
    side_out[3 * per : 4 * per, 2 * n : 3 * n] = got[:, n:]


def core_kernel(
    seq_len, per, terms, white, white3, acts, grads, mine, side, white1, mine_out, side_out
):
    n = acts.shape[0]
    tok = [acts[...], grads[...]]
    for w in range(2):
        white1[w] = whiten(tok[w], terms.at[w])
    mine_out[...] = mine[...]
    mine_out[:, 3 * n : 4 * n] = block(seq_len, [white[w, : 2 * n] for w in range(2)], tok)
    side_out[...] = side[...]
    left = [stack(white[w, 2 * n : 4 * n], white3[w]) for w in range(2)]
    got = block(seq_len, left, tok)
    for i, row in enumerate((0, 2 * per, 3 * per)):
        side_out[row : row + per, n : 2 * n] = got[i * per : (i + 1) * per]


def return_kernel(seq_len, per, white, white1, white3, pick, side, v2, by_z, by_x):
    n = v2.shape[1]
    tok = [v2[w] for w in range(2)]
    columns = [
        stack(white[w, 4 * n : 5 * n], white1[w], white[w, 3 * n : 4 * n], white3[w])
        for w in range(2)
    ]
    by_row = block(seq_len, tok, columns)
    by_column = block(
        seq_len, [stack(white[w, 3 * n : 4 * n], white3[w]) for w in range(2)], tok
    )
    zeros = jnp.zeros((per, 2 * n), jnp.float32)
    none = jnp.zeros((per, 6 * n), jnp.float32)
    row = jnp.concatenate([by_row[:, : 2 * n], zeros, by_row[:, 2 * n :]], axis=1)
    lead = jnp.zeros((2 * per, 3 * n), jnp.float32)
    both = jnp.concatenate([lead, by_column, lead[:, : 2 * n]], axis=1)
    picked = pick_columns(side[...] + stack(none, row, both), pick.at[2 * n :])
    by_x[...] = picked[: 2 * per]
    by_z[...] = picked[2 * per :]


def rows_kernel(seq_len, per, white, pick, mine, v3, v2, out):
    n = v2.shape[1]
    left = [white[w, : 2 * n] for w in range(2)]
    got = block(seq_len, left, [stack(v2[w], v3[w]) for w in range(2)])
    zeros = jnp.zeros((2 * per, n), jnp.float32)
    late = jnp.concatenate([zeros] * 5 + [got[:, :n], zeros, got[:, n:]], axis=1)
    out[...] = pick_columns(mine[...] + late, pick)


def call(kernel, name, flops, limit, operands, specs, out_shape, scratch=(), **more):
    vmem = pl.BlockSpec(memory_space=pltpu.VMEM)
    return pl.pallas_call(
        kernel,
        out_shape=out_shape,
        in_specs=specs + [vmem] * (len(operands) - len(specs)),
        out_specs=jax.tree.map(lambda _: vmem, out_shape),
        scratch_shapes=scratch,
        compiler_params=pltpu.CompilerParams(vmem_limit_bytes=int(limit * 1024 * 1024)),
        cost_estimate=pl.CostEstimate(flops=flops, bytes_accessed=10**6, transcendentals=0),
        name=name,
        **more,
    )(*operands)


def paired(activations, out_grads, lengths, layer_ids, flagged, act_factor, grad_factor):
    size = 16
    per = lengths.shape[0]
    tokens, rank = activations.shape[1:]
    seq_len = tokens // per
    f32, bf16 = jnp.float32, jnp.bfloat16

    def send(x, to):
        return lax.ppermute(x, "blk", [(d, to(d)) for d in range(size)])

    def opposite(d):
        return d ^ 8

    ways = (z_near, lambda d: d ^ 2, lambda d: d ^ 1)
    hbm = pl.BlockSpec(memory_space=pltpu.HBM)
    vmem = pl.BlockSpec(memory_space=pltpu.VMEM)
    shape = jax.ShapeDtypeStruct
    columns = flagged.shape[0]
    unit = shape((2, tokens, rank), bf16)
    data = (activations, out_grads)
    lens = lengths.reshape(1, -1)
    copies = [pltpu.SemaphoreType.DMA((2,))]
    away = call(away_kernel, "away", 3 * 10**9, 53.71, data, [hbm, hbm], unit, copies)
    away = call(
        functools.partial(away_mask_kernel, seq_len),
        "away_mask",
        10**4,
        40,
        (lens, away),
        [],
        unit,
        input_output_aliases={1: 0},
    )
    v = send(away, opposite)
    away, lens, *data = lax.optimization_barrier((away, lens, *data))
    own = call(
        functools.partial(own_kernel, seq_len), "own", 10**9, 40, (lens, *data), [], unit
    )
    near = [send(own, to) for to in ways]
    terms, pick = call(
        functools.partial(setup_kernel, seq_len, per),
        "factor_terms",
        10**9,
        51,
        (layer_ids, flagged.reshape(1, -1), act_factor, grad_factor),
        [pl.BlockSpec(memory_space=pltpu.SMEM), vmem, hbm, hbm],
        (shape((2, 3, rank, rank), bf16), shape((8 * tokens, columns), bf16)),
        [pltpu.VMEM((2, rank, rank), f32), pltpu.SemaphoreType.DMA((2,))],
    )
    v, terms, pick = lax.optimization_barrier((v, terms, pick))
    late = [send(v, to) for to in ways[:2]]
    whole = shape((2 * per, 8 * tokens), f32)
    sides = shape((4 * per, 6 * tokens), f32)
    rows = shape((2 * per, columns), f32)
    u3, u2, u1 = near
    v3, v2 = late

    def kernel(body, name, operands, out_shape, flops=10**9, **more):
        body = functools.partial(body, seq_len, per)
        return call(body, name, flops, 40, operands, [], out_shape, **more)

    white, mine, side = kernel(
        early_kernel,
        "early_pairs",
        (terms, own, v, u3, u2, u1),
        (shape((2, 5 * tokens, rank), bf16), whole, sides),
    )
    v, white = lax.optimization_barrier((v, white))
    v1 = [send(v[w], ways[2]) for w in range(2)]
    white3, side = kernel(
        z_kernel,
        "z_pairs",
        (terms, white, u2, u1, v3, side),
        (unit, sides),
        flops=10**4,
        input_output_aliases={5: 1},
    )
    white1, mine, side = kernel(
        core_kernel,
        "core_pairs",
        (terms, white, white3, *v1, mine, side),
        (unit, whole, sides),
        flops=10**4,
        input_output_aliases={5: 1, 6: 2},
    )
    by_z, by_x = kernel(
        return_kernel, "return_rows", (white, white1, white3, pick, side, v2), (rows, rows)
    )
    mine = kernel(rows_kernel, "own_rows", (white, pick, mine, v3, v2), rows)
    half_sum = mine + send(by_z, z_near) + send(by_x, lambda d: d ^ 2)
    return half_sum[:per] + send(half_sum[per:], opposite)


def solution(mesh):
    in_specs = (
        P(None, ("grp", "blk"), None),
        P(None, ("grp", "blk"), None),
        P(("grp", "blk")),
        P("grp"),
        P("grp"),
        P(),
        P(),
    )
    out_specs = P(("grp", "blk"), None)
    shards = paired if mesh.shape["blk"] == 16 else gathered
    return jax.shard_map(shards, mesh=mesh, in_specs=in_specs, out_specs=out_specs, check_vma=False)
```

```python
import functools

import jax
import jax.numpy as jnp
from jax import lax
from jax.experimental import pallas as pl
from jax.experimental.pallas import tpu as pltpu
from jax.sharding import PartitionSpec as P

HIGHEST = lax.Precision.HIGHEST


def tile_scores(white_acts, white_grads, remote_acts, remote_grads, seq_len):
    gram_acts = jnp.einsum(
        "lqr,lkr->lqk", white_acts, remote_acts, preferred_element_type=jnp.float32
    )
    gram_grads = jnp.einsum(
        "lqr,lkr->lqk", white_grads, remote_grads, preferred_element_type=jnp.float32
    )
    pair = jnp.sum(gram_acts * gram_grads, axis=0)
    rows = pair.shape[0] // seq_len
    columns = pair.shape[1] // seq_len
    width = white_acts.shape[2]
    return pair.reshape(rows, seq_len, columns, seq_len).sum(axis=(1, 3)) * (
        1.0 / (width * seq_len)
    )


def gathered(activations, out_grads, lengths, layer_ids, flagged, act_factor, grad_factor):
    tok_rows = activations.shape[1]
    seq_count = lengths.shape[0]
    seq_len = tok_rows // seq_count
    slots = jnp.arange(tok_rows) % seq_len
    keep = (slots < jnp.repeat(lengths, seq_len)).astype(jnp.bfloat16)
    masked_acts = activations * keep[None, :, None]
    masked_grads = out_grads * keep[None, :, None]
    picked_act = jnp.take(act_factor, layer_ids, axis=0)
    picked_grad = jnp.take(grad_factor, layer_ids, axis=0)
    white_acts = jnp.einsum(
        "ltr,lrs->lts", masked_acts.astype(jnp.float32), picked_act, precision=HIGHEST
    ).astype(jnp.bfloat16)
    white_grads = jnp.einsum(
        "ltr,lrs->lts", masked_grads.astype(jnp.float32), picked_grad, precision=HIGHEST
    ).astype(jnp.bfloat16)
    part_scores = tile_scores(
        white_acts,
        white_grads,
        lax.all_gather(masked_acts, "blk", axis=1, tiled=True),
        lax.all_gather(masked_grads, "blk", axis=1, tiled=True),
        seq_len,
    )
    return jnp.take(part_scores, flagged, axis=1)


def z_near(d):
    return d ^ 4 ^ ((d >> 1) & 1)


def away_kernel(acts, grads, out, sems):
    layer = 1 - lax.axis_index("blk") // 8
    copies = [
        pltpu.make_async_copy(src.at[layer], out.at[i], sems.at[i])
        for i, src in enumerate((acts, grads))
    ]
    for copy in copies:
        copy.start()
    for copy in copies:
        copy.wait()


def masked_acts(x, lens, seq_len):
    row = lax.broadcasted_iota(jnp.int32, (x.shape[0], 1), 0)
    bound = jnp.zeros_like(row)
    for s in range(x.shape[0] // seq_len):
        bound = jnp.where(row // seq_len == s, lens[0:1, s : s + 1] + s * seq_len, bound)
    return jnp.where(row < bound, x, jnp.zeros_like(x))


def away_mask_kernel(seq_len, lens, unit, out):
    out[0] = masked_acts(unit[0], lens, seq_len)
    out[1] = unit[1]


def own_kernel(seq_len, lens, acts, grads, out):
    half = lax.axis_index("blk") // 8
    out[0] = masked_acts(acts[half], lens, seq_len)
    out[1] = grads[half]


def whiten(x, terms):
    total = jnp.dot(x, terms[0], preferred_element_type=jnp.float32)
    for n in (1, 2):
        total = total + jnp.dot(x, terms[n], preferred_element_type=jnp.float32)
    return total.astype(jnp.bfloat16)


def stack(*arrays):
    return jnp.concatenate(arrays, axis=0)


def block(seq_len, left, right):
    grams = [
        lax.dot_general(a, b, (((1,), (1,)), ((), ())), preferred_element_type=jnp.float32)
        for a, b in zip(left, right)
    ]
    rows, columns = grams[0].shape
    return (grams[0] * grams[1]).reshape(rows // seq_len, seq_len, columns).sum(axis=1)


def pick_columns(sums, pick):
    rest, terms = sums, []
    for _ in range(3):
        terms.append(rest.astype(jnp.bfloat16))
        rest = rest - terms[-1].astype(jnp.float32)
    n = sums.shape[0]
    out = jnp.dot(stack(*terms), pick[...], preferred_element_type=jnp.float32)
    return out[:n] + out[n : 2 * n] + out[2 * n :]


def setup_kernel(seq_len, per, layer_ids, flagged, act_f, grad_f, terms, pick, factor, sems):
    d = lax.axis_index("blk")
    layer = layer_ids[d // 8]
    copies = [
        pltpu.make_async_copy(src.at[layer], factor.at[i], sems.at[i])
        for i, src in enumerate((act_f, grad_f))
    ]
    for copy in copies:
        copy.start()
    token = lax.broadcasted_iota(jnp.int32, pick.shape, 0)
    spot = token // (seq_len * per)
    slot = spot // 2
    owner = jnp.where(
        slot == 0, d, jnp.where(slot == 1, d ^ 1, jnp.where(slot == 2, d ^ 2, z_near(d)))
    )
    owner = owner ^ (8 * (spot % 2))
    seq = owner * per + token // seq_len % per
    scale = 1.0 / (factor.shape[1] * seq_len)
    pick[...] = jnp.where(seq == flagged[...], scale, 0.0).astype(pick.dtype)
    for w, copy in enumerate(copies):
        copy.wait()
        rest = factor[w]
        for t in range(3):
            term = rest.astype(jnp.bfloat16)
            terms[w, t] = term
            rest = rest - term.astype(jnp.float32)


def early_kernel(seq_len, per, terms, u0, v, u3, u2, u1, white, mine, side):
    n = u0.shape[1]
    rows = []
    for w in range(2):
        white[w] = whiten(stack(u0[w], v[w], u2[w], u3[w]), terms.at[w])
        rows.append(white[w])
    left = {
        0: [r[: 2 * n] for r in rows],
        2: [r[2 * n : 3 * n] for r in rows],
        3: [r[3 * n : 4 * n] for r in rows],
    }
    tok = [[u[w] for w in range(2)] for u in (u0, u1, u2, u3)]
    mine[...] = jnp.zeros_like(mine)
    mine[:, 0 : 2 * n] = block(seq_len, left[0], [stack(u0[w], v[w]) for w in range(2)])
    for slot in (1, 2, 3):
        at = 2 * n * slot
        mine[:, at : at + n] = block(seq_len, left[0], tok[slot])
    side[...] = jnp.zeros_like(side)
    for row, slot, other in ((0, 2, 3), (2 * per, 3, 2)):
        for column in (1, other):
            at = 2 * n * (column - 1)
            side[row : row + per, at : at + n] = block(seq_len, left[slot], tok[column])


def z_kernel(seq_len, per, terms, white, u2, u1, v3, side, white3, side_out):
    n = v3.shape[1]
    tok = [v3[w] for w in range(2)]
    fresh = [whiten(tok[w], terms.at[w]) for w in range(2)]
    for w in range(2):
        white3[w] = fresh[w]
    side_out[...] = side[...]
    side_out[0:per, 5 * n : 6 * n] = block(
        seq_len, [white[w, 2 * n : 3 * n] for w in range(2)], tok
    )
    got = block(seq_len, fresh, [stack(u1[w], u2[w]) for w in range(2)])
    side_out[3 * per : 4 * per, 0:n] = got[:, :n]
    side_out[3 * per : 4 * per, 2 * n : 3 * n] = got[:, n:]


def core_kernel(seq_len, per, white, white3, acts, grads, mine, side, mine_out, side_out):
    n = acts.shape[0]
    tok = [acts[...], grads[...]]
    mine_out[...] = mine[...]
    mine_out[:, 3 * n : 4 * n] = block(seq_len, [white[w, : 2 * n] for w in range(2)], tok)
    side_out[...] = side[...]
    left = [stack(white[w, 2 * n : 4 * n], white3[w]) for w in range(2)]
    got = block(seq_len, left, tok)
    for i, row in enumerate((0, 2 * per, 3 * per)):
        side_out[row : row + per, n : 2 * n] = got[i * per : (i + 1) * per]


def return_kernel(
    seq_len, per, terms, white, white3, pick, side, u3, u1, v3, acts, grads, v2, by_z, by_x
):
    n = v2.shape[1]
    tok = [v2[w] for w in range(2)]
    core = (acts[...], grads[...])
    by_row = block(
        seq_len,
        [whiten(tok[w], terms.at[w]) for w in range(2)],
        [stack(u1[w], core[w], u3[w], v3[w]) for w in range(2)],
    )
    by_column = block(
        seq_len, [stack(white[w, 3 * n : 4 * n], white3[w]) for w in range(2)], tok
    )
    zeros = jnp.zeros((per, 2 * n), jnp.float32)
    none = jnp.zeros((per, 6 * n), jnp.float32)
    row = jnp.concatenate([by_row[:, : 2 * n], zeros, by_row[:, 2 * n :]], axis=1)
    lead = jnp.zeros((2 * per, 3 * n), jnp.float32)
    both = jnp.concatenate([lead, by_column, lead[:, : 2 * n]], axis=1)
    picked = pick_columns(side[...] + stack(none, row, both), pick.at[2 * n :])
    by_x[...] = picked[: 2 * per]
    by_z[...] = picked[2 * per :]


def rows_kernel(seq_len, per, white, pick, mine, v3, v2, out):
    n = v2.shape[1]
    left = [white[w, : 2 * n] for w in range(2)]
    got = block(seq_len, left, [stack(v2[w], v3[w]) for w in range(2)])
    zeros = jnp.zeros((2 * per, n), jnp.float32)
    late = jnp.concatenate([zeros] * 5 + [got[:, :n], zeros, got[:, n:]], axis=1)
    out[...] = pick_columns(mine[...] + late, pick)


def call(kernel, name, flops, limit, operands, specs, out_shape, scratch=(), **more):
    vmem = pl.BlockSpec(memory_space=pltpu.VMEM)
    return pl.pallas_call(
        kernel,
        out_shape=out_shape,
        in_specs=specs + [vmem] * (len(operands) - len(specs)),
        out_specs=jax.tree.map(lambda _: vmem, out_shape),
        scratch_shapes=scratch,
        compiler_params=pltpu.CompilerParams(vmem_limit_bytes=int(limit * 1024 * 1024)),
        cost_estimate=pl.CostEstimate(flops=flops, bytes_accessed=10**6, transcendentals=0),
        name=name,
        **more,
    )(*operands)


def paired(activations, out_grads, lengths, layer_ids, flagged, act_factor, grad_factor):
    size = 16
    per = lengths.shape[0]
    tokens, rank = activations.shape[1:]
    seq_len = tokens // per
    f32, bf16 = jnp.float32, jnp.bfloat16

    def send(x, to):
        return lax.ppermute(x, "blk", [(d, to(d)) for d in range(size)])

    def opposite(d):
        return d ^ 8

    ways = (z_near, lambda d: d ^ 2, lambda d: d ^ 1)
    hbm = pl.BlockSpec(memory_space=pltpu.HBM)
    vmem = pl.BlockSpec(memory_space=pltpu.VMEM)
    shape = jax.ShapeDtypeStruct
    columns = flagged.shape[0]
    unit = shape((2, tokens, rank), bf16)
    data = (activations, out_grads)
    lens = lengths.reshape(1, -1)
    copies = [pltpu.SemaphoreType.DMA((2,))]
    away = call(away_kernel, "away", 3 * 10**9, 53.71, data, [hbm, hbm], unit, copies)
    away = call(
        functools.partial(away_mask_kernel, seq_len),
        "away_mask",
        10**4,
        40,
        (lens, away),
        [],
        unit,
        input_output_aliases={1: 0},
    )
    v = send(away, opposite)
    away, lens, *data = lax.optimization_barrier((away, lens, *data))
    own = call(
        functools.partial(own_kernel, seq_len), "own", 10**9, 40, (lens, *data), [], unit
    )
    near = [send(own, to) for to in ways]
    terms, pick = call(
        functools.partial(setup_kernel, seq_len, per),
        "factor_terms",
        10**9,
        51,
        (layer_ids, flagged.reshape(1, -1), act_factor, grad_factor),
        [pl.BlockSpec(memory_space=pltpu.SMEM), vmem, hbm, hbm],
        (shape((2, 3, rank, rank), bf16), shape((8 * tokens, columns), bf16)),
        [pltpu.VMEM((2, rank, rank), f32), pltpu.SemaphoreType.DMA((2,))],
    )
    v, terms, pick = lax.optimization_barrier((v, terms, pick))
    late = [send(v, to) for to in ways[:2]]
    whole = shape((2 * per, 8 * tokens), f32)
    sides = shape((4 * per, 6 * tokens), f32)
    rows = shape((2 * per, columns), f32)
    u3, u2, u1 = near
    v3, v2 = late

    def kernel(body, name, operands, out_shape, flops=10**9, **more):
        body = functools.partial(body, seq_len, per)
        return call(body, name, flops, 40, operands, [], out_shape, **more)

    white, mine, side = kernel(
        early_kernel,
        "early_pairs",
        (terms, own, v, u3, u2, u1),
        (shape((2, 4 * tokens, rank), bf16), whole, sides),
    )
    v, white = lax.optimization_barrier((v, white))
    v1 = [send(v[w], ways[2]) for w in range(2)]
    white3, side = kernel(
        z_kernel,
        "z_pairs",
        (terms, white, u2, u1, v3, side),
        (unit, sides),
        flops=10**4,
        input_output_aliases={5: 1},
    )
    mine, side = kernel(
        core_kernel,
        "core_pairs",
        (white, white3, *v1, mine, side),
        (whole, sides),
        flops=10**4,
        input_output_aliases={4: 0, 5: 1},
    )
    by_z, by_x = kernel(
        return_kernel,
        "return_rows",
        (terms, white, white3, pick, side, u3, u1, v3, *v1, v2),
        (rows, rows),
    )
    mine = kernel(rows_kernel, "own_rows", (white, pick, mine, v3, v2), rows)
    half_sum = mine + send(by_x, lambda d: d ^ 2) + send(by_z, z_near)
    return half_sum[:per] + send(half_sum[per:], opposite)


def solution(mesh):
    in_specs = (
        P(None, ("grp", "blk"), None),
        P(None, ("grp", "blk"), None),
        P(("grp", "blk")),
        P("grp"),
        P("grp"),
        P(),
        P(),
    )
    out_specs = P(("grp", "blk"), None)
    shards = paired if mesh.shape["blk"] == 16 else gathered
    return jax.shard_map(shards, mesh=mesh, in_specs=in_specs, out_specs=out_specs, check_vma=False)
```

```python
import functools

import jax
import jax.numpy as jnp
from jax import lax
from jax.experimental import pallas as pl
from jax.experimental.pallas import tpu as pltpu
from jax.sharding import PartitionSpec as P

HIGHEST = lax.Precision.HIGHEST


def tile_scores(white_acts, white_grads, remote_acts, remote_grads, seq_len):
    gram_acts = jnp.einsum(
        "lqr,lkr->lqk", white_acts, remote_acts, preferred_element_type=jnp.float32
    )
    gram_grads = jnp.einsum(
        "lqr,lkr->lqk", white_grads, remote_grads, preferred_element_type=jnp.float32
    )
    pair = jnp.sum(gram_acts * gram_grads, axis=0)
    rows = pair.shape[0] // seq_len
    columns = pair.shape[1] // seq_len
    width = white_acts.shape[2]
    return pair.reshape(rows, seq_len, columns, seq_len).sum(axis=(1, 3)) * (
        1.0 / (width * seq_len)
    )


def gathered(activations, out_grads, lengths, layer_ids, flagged, act_factor, grad_factor):
    tok_rows = activations.shape[1]
    seq_count = lengths.shape[0]
    seq_len = tok_rows // seq_count
    slots = jnp.arange(tok_rows) % seq_len
    keep = (slots < jnp.repeat(lengths, seq_len)).astype(jnp.bfloat16)
    masked_acts = activations * keep[None, :, None]
    masked_grads = out_grads * keep[None, :, None]
    picked_act = jnp.take(act_factor, layer_ids, axis=0)
    picked_grad = jnp.take(grad_factor, layer_ids, axis=0)
    white_acts = jnp.einsum(
        "ltr,lrs->lts", masked_acts.astype(jnp.float32), picked_act, precision=HIGHEST
    ).astype(jnp.bfloat16)
    white_grads = jnp.einsum(
        "ltr,lrs->lts", masked_grads.astype(jnp.float32), picked_grad, precision=HIGHEST
    ).astype(jnp.bfloat16)
    part_scores = tile_scores(
        white_acts,
        white_grads,
        lax.all_gather(masked_acts, "blk", axis=1, tiled=True),
        lax.all_gather(masked_grads, "blk", axis=1, tiled=True),
        seq_len,
    )
    return jnp.take(part_scores, flagged, axis=1)


def z_near(d):
    return d ^ 4 ^ ((d >> 1) & 1)


def is_inner(d):
    return (d >= 4) & (d < 12)


def away_kernel(acts, grads, out, sems):
    layer = 1 - lax.axis_index("blk") // 8
    copies = [
        pltpu.make_async_copy(src.at[layer], out.at[i], sems.at[i])
        for i, src in enumerate((acts, grads))
    ]
    for copy in copies:
        copy.start()
    for copy in copies:
        copy.wait()


def masked_acts(x, lens, seq_len):
    row = lax.broadcasted_iota(jnp.int32, (x.shape[0], 1), 0)
    bound = jnp.zeros_like(row)
    for s in range(x.shape[0] // seq_len):
        bound = jnp.where(row // seq_len == s, lens[0:1, s : s + 1] + s * seq_len, bound)
    return jnp.where(row < bound, x, jnp.zeros_like(x))


def away_mask_kernel(seq_len, lens, unit, out):
    out[0] = masked_acts(unit[0], lens, seq_len)
    out[1] = unit[1]


def own_kernel(seq_len, lens, acts, grads, out):
    half = lax.axis_index("blk") // 8
    out[0] = masked_acts(acts[half], lens, seq_len)
    out[1] = grads[half]


def whiten(x, terms):
    total = jnp.dot(x, terms[0], preferred_element_type=jnp.float32)
    for n in (1, 2):
        total = total + jnp.dot(x, terms[n], preferred_element_type=jnp.float32)
    return total.astype(jnp.bfloat16)


def stack(*arrays):
    return jnp.concatenate(arrays, axis=0)


def block(seq_len, left, right):
    grams = [
        lax.dot_general(a, b, (((1,), (1,)), ((), ())), preferred_element_type=jnp.float32)
        for a, b in zip(left, right)
    ]
    rows, columns = grams[0].shape
    return (grams[0] * grams[1]).reshape(rows // seq_len, seq_len, columns).sum(axis=1)


def pick_columns(sums, pick):
    rest, terms = sums, []
    for _ in range(3):
        terms.append(rest.astype(jnp.bfloat16))
        rest = rest - terms[-1].astype(jnp.float32)
    n = sums.shape[0]
    out = jnp.dot(stack(*terms), pick[...], preferred_element_type=jnp.float32)
    return out[:n] + out[n : 2 * n] + out[2 * n :]


def setup_kernel(seq_len, per, layer_ids, flagged, act_f, grad_f, terms, pick, factor, sems):
    d = lax.axis_index("blk")
    layer = layer_ids[d // 8]
    copies = [
        pltpu.make_async_copy(src.at[layer], factor.at[i], sems.at[i])
        for i, src in enumerate((act_f, grad_f))
    ]
    for copy in copies:
        copy.start()
    token = lax.broadcasted_iota(jnp.int32, pick.shape, 0)
    spot = token // (seq_len * per)
    slot = spot // 2
    owner = jnp.where(
        slot == 0, d, jnp.where(slot == 1, d ^ 1, jnp.where(slot == 2, d ^ 2, z_near(d)))
    )
    owner = owner ^ (8 * (spot % 2))
    seq = owner * per + token // seq_len % per
    scale = 1.0 / (factor.shape[1] * seq_len)
    pick[...] = jnp.where(seq == flagged[...], scale, 0.0).astype(pick.dtype)
    for w, copy in enumerate(copies):
        copy.wait()
        rest = factor[w]
        for t in range(3):
            term = rest.astype(jnp.bfloat16)
            terms[w, t] = term
            rest = rest - term.astype(jnp.float32)


def early_kernel(seq_len, per, terms, u0, v, u3, u2, u1, white, mine, side):
    n = u0.shape[1]
    rows = []
    for w in range(2):
        white[w] = whiten(stack(u0[w], v[w], u2[w], u3[w]), terms.at[w])
        rows.append(white[w])
    left = {
        0: [r[: 2 * n] for r in rows],
        2: [r[2 * n : 3 * n] for r in rows],
        3: [r[3 * n : 4 * n] for r in rows],
    }
    tok = [[u[w] for w in range(2)] for u in (u0, u1, u2, u3)]
    mine[...] = jnp.zeros_like(mine)
    mine[:, 0 : 2 * n] = block(seq_len, left[0], [stack(u0[w], v[w]) for w in range(2)])
    for slot in (1, 2, 3):
        at = 2 * n * slot
        mine[:, at : at + n] = block(seq_len, left[0], tok[slot])
    side[...] = jnp.zeros_like(side)
    for row, slot, other in ((0, 2, 3), (2 * per, 3, 2)):
        for column in (1, other):
            at = 2 * n * (column - 1)
            side[row : row + per, at : at + n] = block(seq_len, left[slot], tok[column])


def z_kernel(seq_len, per, terms, white, u2, u1, first, v3, side, white3, side_out):
    n = v3.shape[1]
    tok = [v3[w] for w in range(2)]
    fresh = [whiten(tok[w], terms.at[w]) for w in range(2)]
    for w in range(2):
        white3[w] = fresh[w]
    side_out[...] = side[...]
    side_out[0:per, 5 * n : 6 * n] = block(
        seq_len, [white[w, 2 * n : 3 * n] for w in range(2)], tok
    )
    got = block(seq_len, fresh, [stack(u1[w], u2[w]) for w in range(2)])
    side_out[3 * per : 4 * per, 0:n] = got[:, :n]
    side_out[3 * per : 4 * per, 2 * n : 3 * n] = got[:, n:]


def core_kernel(seq_len, per, white, white3, acts, grads, mine, side, mine_out, side_out):
    n = acts.shape[0]
    tok = [acts[...], grads[...]]
    mine_out[...] = mine[...]
    mine_out[:, 3 * n : 4 * n] = block(seq_len, [white[w, : 2 * n] for w in range(2)], tok)
    side_out[...] = side[...]
    left = [stack(white[w, 2 * n : 4 * n], white3[w]) for w in range(2)]
    got = block(seq_len, left, tok)
    for i, row in enumerate((0, 2 * per, 3 * per)):
        side_out[row : row + per, n : 2 * n] = got[i * per : (i + 1) * per]


def x_unit(first, last):
    inner = is_inner(lax.axis_index("blk"))
    return [jnp.where(inner, first[w], last[w]) for w in range(2)]


def return_kernel(
    seq_len, per, terms, white, white3, pick, side, u3, u1, v3, acts, grads, first, last, by_z, by_x
):
    n = first.shape[1]
    tok = x_unit(first, last)
    core = (acts[...], grads[...])
    by_row = block(
        seq_len,
        [whiten(tok[w], terms.at[w]) for w in range(2)],
        [stack(u1[w], core[w], u3[w], v3[w]) for w in range(2)],
    )
    by_column = block(
        seq_len, [stack(white[w, 3 * n : 4 * n], white3[w]) for w in range(2)], tok
    )
    zeros = jnp.zeros((per, 2 * n), jnp.float32)
    none = jnp.zeros((per, 6 * n), jnp.float32)
    row = jnp.concatenate([by_row[:, : 2 * n], zeros, by_row[:, 2 * n :]], axis=1)
    lead = jnp.zeros((2 * per, 3 * n), jnp.float32)
    both = jnp.concatenate([lead, by_column, lead[:, : 2 * n]], axis=1)
    picked = pick_columns(side[...] + stack(none, row, both), pick.at[2 * n :])
    by_x[...] = picked[: 2 * per]
    by_z[...] = picked[2 * per :]


def rows_kernel(seq_len, per, white, pick, mine, v3, first, last, out):
    n = v3.shape[1]
    v2 = x_unit(first, last)
    left = [white[w, : 2 * n] for w in range(2)]
    got = block(seq_len, left, [stack(v2[w], v3[w]) for w in range(2)])
    zeros = jnp.zeros((2 * per, n), jnp.float32)
    late = jnp.concatenate([zeros] * 5 + [got[:, :n], zeros, got[:, n:]], axis=1)
    out[...] = pick_columns(mine[...] + late, pick)


def call(kernel, name, flops, limit, operands, specs, out_shape, scratch=(), **more):
    vmem = pl.BlockSpec(memory_space=pltpu.VMEM)
    return pl.pallas_call(
        kernel,
        out_shape=out_shape,
        in_specs=specs + [vmem] * (len(operands) - len(specs)),
        out_specs=jax.tree.map(lambda _: vmem, out_shape),
        scratch_shapes=scratch,
        compiler_params=pltpu.CompilerParams(vmem_limit_bytes=int(limit * 1024 * 1024)),
        cost_estimate=pl.CostEstimate(flops=flops, bytes_accessed=10**6, transcendentals=0),
        name=name,
        **more,
    )(*operands)


def paired(activations, out_grads, lengths, layer_ids, flagged, act_factor, grad_factor):
    size = 16
    per = lengths.shape[0]
    tokens, rank = activations.shape[1:]
    seq_len = tokens // per
    f32, bf16 = jnp.float32, jnp.bfloat16

    def send(x, to):
        return lax.ppermute(x, "blk", [(d, to(d)) for d in range(size)])

    def opposite(d):
        return d ^ 8

    ways = (z_near, lambda d: d ^ 2, lambda d: d ^ 1)
    hbm = pl.BlockSpec(memory_space=pltpu.HBM)
    vmem = pl.BlockSpec(memory_space=pltpu.VMEM)
    shape = jax.ShapeDtypeStruct
    columns = flagged.shape[0]
    unit = shape((2, tokens, rank), bf16)
    data = (activations, out_grads)
    lens = lengths.reshape(1, -1)
    copies = [pltpu.SemaphoreType.DMA((2,))]
    away = call(away_kernel, "away", 3 * 10**9, 53.71, data, [hbm, hbm], unit, copies)
    away = call(
        functools.partial(away_mask_kernel, seq_len),
        "away_mask",
        10**4,
        40,
        (lens, away),
        [],
        unit,
        input_output_aliases={1: 0},
    )
    v = send(away, opposite)
    away, lens, *data = lax.optimization_barrier((away, lens, *data))
    own = call(
        functools.partial(own_kernel, seq_len), "own", 10**9, 40, (lens, *data), [], unit
    )
    near = [send(own, to) for to in ways]
    terms, pick = call(
        functools.partial(setup_kernel, seq_len, per),
        "factor_terms",
        10**9,
        51,
        (layer_ids, flagged.reshape(1, -1), act_factor, grad_factor),
        [pl.BlockSpec(memory_space=pltpu.SMEM), vmem, hbm, hbm],
        (shape((2, 3, rank, rank), bf16), shape((8 * tokens, columns), bf16)),
        [pltpu.VMEM((2, rank, rank), f32), pltpu.SemaphoreType.DMA((2,))],
    )
    v, terms, pick = lax.optimization_barrier((v, terms, pick))
    first = send(v, lambda d: d ^ 2 if is_inner(d) else d)
    v3 = send(v, z_near)
    last = send(v, lambda d: d if is_inner(d) else d ^ 2)
    whole = shape((2 * per, 8 * tokens), f32)
    sides = shape((4 * per, 6 * tokens), f32)
    rows = shape((2 * per, columns), f32)
    u3, u2, u1 = near

    def kernel(body, name, operands, out_shape, flops=10**9, **more):
        body = functools.partial(body, seq_len, per)
        return call(body, name, flops, 40, operands, [], out_shape, **more)

    white, mine, side = kernel(
        early_kernel,
        "early_pairs",
        (terms, own, v, u3, u2, u1),
        (shape((2, 4 * tokens, rank), bf16), whole, sides),
    )
    v, white = lax.optimization_barrier((v, white))
    v1 = [send(v[w], ways[2]) for w in range(2)]
    white3, side = kernel(
        z_kernel,
        "z_pairs",
        (terms, white, u2, u1, first, v3, side),
        (unit, sides),
        flops=10**4,
        input_output_aliases={6: 1},
    )
    mine, side = kernel(
        core_kernel,
        "core_pairs",
        (white, white3, *v1, mine, side),
        (whole, sides),
        flops=10**4,
        input_output_aliases={4: 0, 5: 1},
    )
    by_z, by_x = kernel(
        return_kernel,
        "return_rows",
        (terms, white, white3, pick, side, u3, u1, v3, *v1, first, last),
        (rows, rows),
    )
    mine = kernel(rows_kernel, "own_rows", (white, pick, mine, v3, first, last), rows)
    half_sum = mine + send(by_x, lambda d: d ^ 2) + send(by_z, z_near)
    return half_sum[:per] + send(half_sum[per:], opposite)


def solution(mesh):
    in_specs = (
        P(None, ("grp", "blk"), None),
        P(None, ("grp", "blk"), None),
        P(("grp", "blk")),
        P("grp"),
        P("grp"),
        P(),
        P(),
    )
    out_specs = P(("grp", "blk"), None)
    shards = paired if mesh.shape["blk"] == 16 else gathered
    return jax.shard_map(shards, mesh=mesh, in_specs=in_specs, out_specs=out_specs, check_vma=False)
```

```python
import functools

import jax
import jax.numpy as jnp
from jax import lax
from jax.experimental import pallas as pl
from jax.experimental.pallas import tpu as pltpu
from jax.sharding import PartitionSpec as P

HIGHEST = lax.Precision.HIGHEST


def tile_scores(white_acts, white_grads, remote_acts, remote_grads, seq_len):
    gram_acts = jnp.einsum(
        "lqr,lkr->lqk", white_acts, remote_acts, preferred_element_type=jnp.float32
    )
    gram_grads = jnp.einsum(
        "lqr,lkr->lqk", white_grads, remote_grads, preferred_element_type=jnp.float32
    )
    pair = jnp.sum(gram_acts * gram_grads, axis=0)
    rows = pair.shape[0] // seq_len
    columns = pair.shape[1] // seq_len
    width = white_acts.shape[2]
    return pair.reshape(rows, seq_len, columns, seq_len).sum(axis=(1, 3)) * (
        1.0 / (width * seq_len)
    )


def gathered(activations, out_grads, lengths, layer_ids, flagged, act_factor, grad_factor):
    tok_rows = activations.shape[1]
    seq_count = lengths.shape[0]
    seq_len = tok_rows // seq_count
    slots = jnp.arange(tok_rows) % seq_len
    keep = (slots < jnp.repeat(lengths, seq_len)).astype(jnp.bfloat16)
    masked_acts = activations * keep[None, :, None]
    masked_grads = out_grads * keep[None, :, None]
    picked_act = jnp.take(act_factor, layer_ids, axis=0)
    picked_grad = jnp.take(grad_factor, layer_ids, axis=0)
    white_acts = jnp.einsum(
        "ltr,lrs->lts", masked_acts.astype(jnp.float32), picked_act, precision=HIGHEST
    ).astype(jnp.bfloat16)
    white_grads = jnp.einsum(
        "ltr,lrs->lts", masked_grads.astype(jnp.float32), picked_grad, precision=HIGHEST
    ).astype(jnp.bfloat16)
    part_scores = tile_scores(
        white_acts,
        white_grads,
        lax.all_gather(masked_acts, "blk", axis=1, tiled=True),
        lax.all_gather(masked_grads, "blk", axis=1, tiled=True),
        seq_len,
    )
    return jnp.take(part_scores, flagged, axis=1)


def z_near(d):
    return d ^ 4 ^ ((d >> 1) & 1)


def away_kernel(acts, grads, out, sems):
    layer = 1 - lax.axis_index("blk") // 8
    copies = [
        pltpu.make_async_copy(src.at[layer], out.at[i], sems.at[i])
        for i, src in enumerate((acts, grads))
    ]
    for copy in copies:
        copy.start()
    for copy in copies:
        copy.wait()


def masked_acts(x, lens, seq_len):
    row = lax.broadcasted_iota(jnp.int32, (x.shape[0], 1), 0)
    bound = jnp.zeros_like(row)
    for s in range(x.shape[0] // seq_len):
        bound = jnp.where(row // seq_len == s, lens[0:1, s : s + 1] + s * seq_len, bound)
    return jnp.where(row < bound, x, jnp.zeros_like(x))


def away_mask_kernel(seq_len, lens, unit, out):
    out[0] = masked_acts(unit[0], lens, seq_len)
    out[1] = unit[1]


def own_kernel(seq_len, lens, acts, grads, out):
    half = lax.axis_index("blk") // 8
    out[0] = masked_acts(acts[half], lens, seq_len)
    out[1] = grads[half]


def whiten(x, terms):
    total = jnp.dot(x, terms[0], preferred_element_type=jnp.float32)
    for n in (1, 2):
        total = total + jnp.dot(x, terms[n], preferred_element_type=jnp.float32)
    return total.astype(jnp.bfloat16)


def stack(*arrays):
    return jnp.concatenate(arrays, axis=0)


def block(seq_len, left, right):
    grams = [
        lax.dot_general(a, b, (((1,), (1,)), ((), ())), preferred_element_type=jnp.float32)
        for a, b in zip(left, right)
    ]
    rows, columns = grams[0].shape
    return (grams[0] * grams[1]).reshape(rows // seq_len, seq_len, columns).sum(axis=1)


def pick_columns(sums, pick):
    rest, terms = sums, []
    for _ in range(3):
        terms.append(rest.astype(jnp.bfloat16))
        rest = rest - terms[-1].astype(jnp.float32)
    n = sums.shape[0]
    out = jnp.dot(stack(*terms), pick[...], preferred_element_type=jnp.float32)
    return out[:n] + out[n : 2 * n] + out[2 * n :]


def setup_kernel(seq_len, per, layer_ids, flagged, act_f, grad_f, terms, pick, factor, sems):
    d = lax.axis_index("blk")
    layer = layer_ids[d // 8]
    copies = [
        pltpu.make_async_copy(src.at[layer], factor.at[i], sems.at[i])
        for i, src in enumerate((act_f, grad_f))
    ]
    for copy in copies:
        copy.start()
    token = lax.broadcasted_iota(jnp.int32, pick.shape, 0)
    spot = token // (seq_len * per)
    slot = spot // 2
    owner = jnp.where(
        slot == 0, d, jnp.where(slot == 1, d ^ 1, jnp.where(slot == 2, d ^ 2, z_near(d)))
    )
    owner = owner ^ (8 * (spot % 2))
    seq = owner * per + token // seq_len % per
    scale = 1.0 / (factor.shape[1] * seq_len)
    pick[...] = jnp.where(seq == flagged[...], scale, 0.0).astype(pick.dtype)
    for w, copy in enumerate(copies):
        copy.wait()
        rest = factor[w]
        for t in range(3):
            term = rest.astype(jnp.bfloat16)
            terms[w, t] = term
            rest = rest - term.astype(jnp.float32)


def early_kernel(seq_len, per, terms, u0, v, u3, u2, u1, white, mine, side):
    n = u0.shape[1]
    rows = []
    for w in range(2):
        white[w] = whiten(stack(u0[w], v[w], u2[w], u3[w]), terms.at[w])
        rows.append(white[w])
    left = {
        0: [r[: 2 * n] for r in rows],
        2: [r[2 * n : 3 * n] for r in rows],
        3: [r[3 * n : 4 * n] for r in rows],
    }
    tok = [[u[w] for w in range(2)] for u in (u0, u1, u2, u3)]
    mine[...] = jnp.zeros_like(mine)
    mine[:, 0 : 2 * n] = block(seq_len, left[0], [stack(u0[w], v[w]) for w in range(2)])
    for slot in (1, 2, 3):
        at = 2 * n * slot
        mine[:, at : at + n] = block(seq_len, left[0], tok[slot])
    side[...] = jnp.zeros_like(side)
    for row, slot, other in ((0, 2, 3), (2 * per, 3, 2)):
        for column in (1, other):
            at = 2 * n * (column - 1)
            side[row : row + per, at : at + n] = block(seq_len, left[slot], tok[column])


def z_kernel(seq_len, per, terms, white, u2, u1, v3, side, white3, side_out):
    n = v3.shape[1]
    tok = [v3[w] for w in range(2)]
    fresh = [whiten(tok[w], terms.at[w]) for w in range(2)]
    for w in range(2):
        white3[w] = fresh[w]
    side_out[...] = side[...]
    side_out[0:per, 5 * n : 6 * n] = block(
        seq_len, [white[w, 2 * n : 3 * n] for w in range(2)], tok
    )
    got = block(seq_len, fresh, [stack(u1[w], u2[w]) for w in range(2)])
    side_out[3 * per : 4 * per, 0:n] = got[:, :n]
    side_out[3 * per : 4 * per, 2 * n : 3 * n] = got[:, n:]


def core_kernel(seq_len, per, white, white3, acts, grads, mine, side, mine_out, side_out):
    n = acts.shape[0]
    tok = [acts[...], grads[...]]
    mine_out[...] = mine[...]
    mine_out[:, 3 * n : 4 * n] = block(seq_len, [white[w, : 2 * n] for w in range(2)], tok)
    side_out[...] = side[...]
    left = [stack(white[w, 2 * n : 4 * n], white3[w]) for w in range(2)]
    got = block(seq_len, left, tok)
    for i, row in enumerate((0, 2 * per, 3 * per)):
        side_out[row : row + per, n : 2 * n] = got[i * per : (i + 1) * per]


def return_kernel(
    seq_len, per, terms, white, white3, pick, side, u3, u1, v3, acts, grads, v2, by_z, by_x
):
    n = v2.shape[1]
    tok = [v2[w] for w in range(2)]
    core = (acts[...], grads[...])
    by_row = block(
        seq_len,
        [whiten(tok[w], terms.at[w]) for w in range(2)],
        [stack(u1[w], core[w], u3[w], v3[w]) for w in range(2)],
    )
    by_column = block(
        seq_len, [stack(white[w, 3 * n : 4 * n], white3[w]) for w in range(2)], tok
    )
    zeros = jnp.zeros((per, 2 * n), jnp.float32)
    none = jnp.zeros((per, 6 * n), jnp.float32)
    row = jnp.concatenate([by_row[:, : 2 * n], zeros, by_row[:, 2 * n :]], axis=1)
    lead = jnp.zeros((2 * per, 3 * n), jnp.float32)
    both = jnp.concatenate([lead, by_column, lead[:, : 2 * n]], axis=1)
    picked = pick_columns(side[...] + stack(none, row, both), pick.at[2 * n :])
    by_x[...] = picked[: 2 * per]
    by_z[...] = picked[2 * per :]


def rows_kernel(seq_len, per, white, pick, mine, v3, v2, out):
    n = v2.shape[1]
    left = [white[w, : 2 * n] for w in range(2)]
    got = block(seq_len, left, [stack(v2[w], v3[w]) for w in range(2)])
    zeros = jnp.zeros((2 * per, n), jnp.float32)
    late = jnp.concatenate([zeros] * 5 + [got[:, :n], zeros, got[:, n:]], axis=1)
    out[...] = pick_columns(mine[...] + late, pick)


def call(kernel, name, flops, limit, operands, specs, out_shape, scratch=(), **more):
    vmem = pl.BlockSpec(memory_space=pltpu.VMEM)
    return pl.pallas_call(
        kernel,
        out_shape=out_shape,
        in_specs=specs + [vmem] * (len(operands) - len(specs)),
        out_specs=jax.tree.map(lambda _: vmem, out_shape),
        scratch_shapes=scratch,
        compiler_params=pltpu.CompilerParams(vmem_limit_bytes=int(limit * 1024 * 1024)),
        cost_estimate=pl.CostEstimate(flops=flops, bytes_accessed=10**6, transcendentals=0),
        name=name,
        **more,
    )(*operands)


def paired(activations, out_grads, lengths, layer_ids, flagged, act_factor, grad_factor):
    size = 16
    per = lengths.shape[0]
    tokens, rank = activations.shape[1:]
    seq_len = tokens // per
    f32, bf16 = jnp.float32, jnp.bfloat16

    def send(x, to):
        return lax.ppermute(x, "blk", [(d, to(d)) for d in range(size)])

    def opposite(d):
        return d ^ 8

    ways = (z_near, lambda d: d ^ 2, lambda d: d ^ 1)
    hbm = pl.BlockSpec(memory_space=pltpu.HBM)
    vmem = pl.BlockSpec(memory_space=pltpu.VMEM)
    shape = jax.ShapeDtypeStruct
    columns = flagged.shape[0]
    unit = shape((2, tokens, rank), bf16)
    data = (activations, out_grads)
    lens = lengths.reshape(1, -1)
    copies = [pltpu.SemaphoreType.DMA((2,))]
    away = call(away_kernel, "away", 3 * 10**9, 53.71, data, [hbm, hbm], unit, copies)
    away = call(
        functools.partial(away_mask_kernel, seq_len),
        "away_mask",
        10**4,
        40,
        (lens, away),
        [],
        unit,
        input_output_aliases={1: 0},
    )
    v = send(away, opposite)
    away, ids = lax.optimization_barrier((away, layer_ids))
    terms, pick = call(
        functools.partial(setup_kernel, seq_len, per),
        "factor_terms",
        10**9,
        51,
        (ids, flagged.reshape(1, -1), act_factor, grad_factor),
        [pl.BlockSpec(memory_space=pltpu.SMEM), vmem, hbm, hbm],
        (shape((2, 3, rank, rank), bf16), shape((8 * tokens, columns), bf16)),
        [pltpu.VMEM((2, rank, rank), f32), pltpu.SemaphoreType.DMA((2,))],
    )
    away, terms, lens, *data = lax.optimization_barrier((away, terms, lens, *data))
    own = call(
        functools.partial(own_kernel, seq_len), "own", 10**9, 40, (lens, *data), [], unit
    )
    near = [send(own, to) for to in ways]
    v, terms, pick = lax.optimization_barrier((v, terms, pick))
    late = [send(v, to) for to in ways[:2]]
    whole = shape((2 * per, 8 * tokens), f32)
    sides = shape((4 * per, 6 * tokens), f32)
    rows = shape((2 * per, columns), f32)
    u3, u2, u1 = near
    v3, v2 = late

    def kernel(body, name, operands, out_shape, flops=10**9, **more):
        body = functools.partial(body, seq_len, per)
        return call(body, name, flops, 40, operands, [], out_shape, **more)

    white, mine, side = kernel(
        early_kernel,
        "early_pairs",
        (terms, own, v, u3, u2, u1),
        (shape((2, 4 * tokens, rank), bf16), whole, sides),
    )
    v, white = lax.optimization_barrier((v, white))
    v1 = [send(v[w], ways[2]) for w in range(2)]
    white3, side = kernel(
        z_kernel,
        "z_pairs",
        (terms, white, u2, u1, v3, side),
        (unit, sides),
        flops=10**4,
        input_output_aliases={5: 1},
    )
    mine, side = kernel(
        core_kernel,
        "core_pairs",
        (white, white3, *v1, mine, side),
        (whole, sides),
        flops=10**4,
        input_output_aliases={4: 0, 5: 1},
    )
    by_z, by_x = kernel(
        return_kernel,
        "return_rows",
        (terms, white, white3, pick, side, u3, u1, v3, *v1, v2),
        (rows, rows),
    )
    mine = kernel(rows_kernel, "own_rows", (white, pick, mine, v3, v2), rows)
    half_sum = mine + send(by_x, lambda d: d ^ 2) + send(by_z, z_near)
    return half_sum[:per] + send(half_sum[per:], opposite)


def solution(mesh):
    in_specs = (
        P(None, ("grp", "blk"), None),
        P(None, ("grp", "blk"), None),
        P(("grp", "blk")),
        P("grp"),
        P("grp"),
        P(),
        P(),
    )
    out_specs = P(("grp", "blk"), None)
    shards = paired if mesh.shape["blk"] == 16 else gathered
    return jax.shard_map(shards, mesh=mesh, in_specs=in_specs, out_specs=out_specs, check_vma=False)
```

```python
import functools

import jax
import jax.numpy as jnp
from jax import lax
from jax.experimental import pallas as pl
from jax.experimental.pallas import tpu as pltpu
from jax.sharding import PartitionSpec as P

HIGHEST = lax.Precision.HIGHEST


def tile_scores(white_acts, white_grads, remote_acts, remote_grads, seq_len):
    gram_acts = jnp.einsum(
        "lqr,lkr->lqk", white_acts, remote_acts, preferred_element_type=jnp.float32
    )
    gram_grads = jnp.einsum(
        "lqr,lkr->lqk", white_grads, remote_grads, preferred_element_type=jnp.float32
    )
    pair = jnp.sum(gram_acts * gram_grads, axis=0)
    rows = pair.shape[0] // seq_len
    columns = pair.shape[1] // seq_len
    width = white_acts.shape[2]
    return pair.reshape(rows, seq_len, columns, seq_len).sum(axis=(1, 3)) * (
        1.0 / (width * seq_len)
    )


def gathered(activations, out_grads, lengths, layer_ids, flagged, act_factor, grad_factor):
    tok_rows = activations.shape[1]
    seq_count = lengths.shape[0]
    seq_len = tok_rows // seq_count
    slots = jnp.arange(tok_rows) % seq_len
    keep = (slots < jnp.repeat(lengths, seq_len)).astype(jnp.bfloat16)
    masked_acts = activations * keep[None, :, None]
    masked_grads = out_grads * keep[None, :, None]
    picked_act = jnp.take(act_factor, layer_ids, axis=0)
    picked_grad = jnp.take(grad_factor, layer_ids, axis=0)
    white_acts = jnp.einsum(
        "ltr,lrs->lts", masked_acts.astype(jnp.float32), picked_act, precision=HIGHEST
    ).astype(jnp.bfloat16)
    white_grads = jnp.einsum(
        "ltr,lrs->lts", masked_grads.astype(jnp.float32), picked_grad, precision=HIGHEST
    ).astype(jnp.bfloat16)
    part_scores = tile_scores(
        white_acts,
        white_grads,
        lax.all_gather(masked_acts, "blk", axis=1, tiled=True),
        lax.all_gather(masked_grads, "blk", axis=1, tiled=True),
        seq_len,
    )
    return jnp.take(part_scores, flagged, axis=1)


def z_near(d):
    return d ^ 4 ^ ((d >> 1) & 1)


def away_kernel(acts, grads, out, sems):
    layer = 1 - lax.axis_index("blk") // 8
    copies = [
        pltpu.make_async_copy(src.at[layer], out.at[i], sems.at[i])
        for i, src in enumerate((acts, grads))
    ]
    for copy in copies:
        copy.start()
    for copy in copies:
        copy.wait()


def masked_acts(x, lens, seq_len):
    row = lax.broadcasted_iota(jnp.int32, (x.shape[0], 1), 0)
    bound = jnp.zeros_like(row)
    for s in range(x.shape[0] // seq_len):
        bound = jnp.where(row // seq_len == s, lens[0:1, s : s + 1] + s * seq_len, bound)
    return jnp.where(row < bound, x, jnp.zeros_like(x))


def away_mask_kernel(seq_len, lens, unit, out):
    out[0] = masked_acts(unit[0], lens, seq_len)
    out[1] = unit[1]


def own_kernel(seq_len, lens, acts, grads, out):
    half = lax.axis_index("blk") // 8
    out[0] = masked_acts(acts[half], lens, seq_len)
    out[1] = grads[half]


def whiten(x, terms):
    total = jnp.dot(x, terms[0], preferred_element_type=jnp.float32)
    for n in (1, 2):
        total = total + jnp.dot(x, terms[n], preferred_element_type=jnp.float32)
    return total.astype(jnp.bfloat16)


def stack(*arrays):
    return jnp.concatenate(arrays, axis=0)


def block(seq_len, left, right):
    grams = [
        lax.dot_general(a, b, (((1,), (1,)), ((), ())), preferred_element_type=jnp.float32)
        for a, b in zip(left, right)
    ]
    rows, columns = grams[0].shape
    return (grams[0] * grams[1]).reshape(rows // seq_len, seq_len, columns).sum(axis=1)


def pick_columns(sums, pick):
    rest, terms = sums, []
    for _ in range(3):
        terms.append(rest.astype(jnp.bfloat16))
        rest = rest - terms[-1].astype(jnp.float32)
    n = sums.shape[0]
    out = jnp.dot(stack(*terms), pick[...], preferred_element_type=jnp.float32)
    return out[:n] + out[n : 2 * n] + out[2 * n :]


def setup_kernel(seq_len, per, layer_ids, flagged, act_f, grad_f, terms, pick, factor, sems):
    d = lax.axis_index("blk")
    layer = layer_ids[d // 8]
    copies = [
        pltpu.make_async_copy(src.at[layer], factor.at[i], sems.at[i])
        for i, src in enumerate((act_f, grad_f))
    ]
    for copy in copies:
        copy.start()
    token = lax.broadcasted_iota(jnp.int32, pick.shape, 0)
    spot = token // (seq_len * per)
    slot = spot // 2
    owner = jnp.where(
        slot == 0, d, jnp.where(slot == 1, d ^ 1, jnp.where(slot == 2, d ^ 2, z_near(d)))
    )
    owner = owner ^ (8 * (spot % 2))
    seq = owner * per + token // seq_len % per
    scale = 1.0 / (factor.shape[1] * seq_len)
    pick[...] = jnp.where(seq == flagged[...], scale, 0.0).astype(pick.dtype)
    for w, copy in enumerate(copies):
        copy.wait()
        rest = factor[w]
        for t in range(3):
            term = rest.astype(jnp.bfloat16)
            terms[w, t] = term
            rest = rest - term.astype(jnp.float32)


def early_kernel(seq_len, per, terms, u0, v, u3, u2, u1, white, mine, side):
    n = u0.shape[1]
    rows = []
    for w in range(2):
        white[w] = whiten(stack(u0[w], v[w], u2[w], u3[w]), terms.at[w])
        rows.append(white[w])
    left = {
        0: [r[: 2 * n] for r in rows],
        2: [r[2 * n : 3 * n] for r in rows],
        3: [r[3 * n : 4 * n] for r in rows],
    }
    tok = [[u[w] for w in range(2)] for u in (u0, u1, u2, u3)]
    mine[...] = jnp.zeros_like(mine)
    mine[:, 0 : 2 * n] = block(seq_len, left[0], [stack(u0[w], v[w]) for w in range(2)])
    for slot in (1, 2, 3):
        at = 2 * n * slot
        mine[:, at : at + n] = block(seq_len, left[0], tok[slot])
    side[...] = jnp.zeros_like(side)
    for row, slot, other in ((0, 2, 3), (2 * per, 3, 2)):
        for column in (1, other):
            at = 2 * n * (column - 1)
            side[row : row + per, at : at + n] = block(seq_len, left[slot], tok[column])


def core_kernel(seq_len, per, white, acts, grads, mine, side, mine_out, side_out):
    n = acts.shape[0]
    tok = [acts[...], grads[...]]
    mine_out[...] = mine[...]
    mine_out[:, 3 * n : 4 * n] = block(seq_len, [white[w, : 2 * n] for w in range(2)], tok)
    side_out[...] = side[...]
    got = block(seq_len, [white[w, 2 * n : 4 * n] for w in range(2)], tok)
    for i, row in enumerate((0, 2 * per)):
        side_out[row : row + per, n : 2 * n] = got[i * per : (i + 1) * per]


def z_kernel(
    seq_len, per, terms, white, u2, u1, acts, grads, v3, side, white3, side_out
):
    n = v3.shape[1]
    tok = [v3[w] for w in range(2)]
    core = (acts[...], grads[...])
    fresh = [whiten(tok[w], terms.at[w]) for w in range(2)]
    for w in range(2):
        white3[w] = fresh[w]
    side_out[...] = side[...]
    side_out[0:per, 5 * n : 6 * n] = block(
        seq_len, [white[w, 2 * n : 3 * n] for w in range(2)], tok
    )
    side_out[3 * per : 4 * per, 0 : 3 * n] = block(
        seq_len, fresh, [stack(u1[w], core[w], u2[w]) for w in range(2)]
    )


def return_kernel(
    seq_len, per, terms, white, white3, pick, side, u3, u1, v3, acts, grads, v2, by_z, by_x
):
    n = v2.shape[1]
    tok = [v2[w] for w in range(2)]
    core = (acts[...], grads[...])
    by_row = block(
        seq_len,
        [whiten(tok[w], terms.at[w]) for w in range(2)],
        [stack(u1[w], core[w], u3[w], v3[w]) for w in range(2)],
    )
    by_column = block(
        seq_len, [stack(white[w, 3 * n : 4 * n], white3[w]) for w in range(2)], tok
    )
    zeros = jnp.zeros((per, 2 * n), jnp.float32)
    none = jnp.zeros((per, 6 * n), jnp.float32)
    row = jnp.concatenate([by_row[:, : 2 * n], zeros, by_row[:, 2 * n :]], axis=1)
    lead = jnp.zeros((2 * per, 3 * n), jnp.float32)
    both = jnp.concatenate([lead, by_column, lead[:, : 2 * n]], axis=1)
    picked = pick_columns(side[...] + stack(none, row, both), pick.at[2 * n :])
    by_x[...] = picked[: 2 * per]
    by_z[...] = picked[2 * per :]


def rows_kernel(seq_len, per, white, pick, mine, v3, v2, out):
    n = v2.shape[1]
    left = [white[w, : 2 * n] for w in range(2)]
    got = block(seq_len, left, [stack(v2[w], v3[w]) for w in range(2)])
    zeros = jnp.zeros((2 * per, n), jnp.float32)
    late = jnp.concatenate([zeros] * 5 + [got[:, :n], zeros, got[:, n:]], axis=1)
    out[...] = pick_columns(mine[...] + late, pick)


def call(kernel, name, flops, limit, operands, specs, out_shape, scratch=(), **more):
    vmem = pl.BlockSpec(memory_space=pltpu.VMEM)
    return pl.pallas_call(
        kernel,
        out_shape=out_shape,
        in_specs=specs + [vmem] * (len(operands) - len(specs)),
        out_specs=jax.tree.map(lambda _: vmem, out_shape),
        scratch_shapes=scratch,
        compiler_params=pltpu.CompilerParams(vmem_limit_bytes=int(limit * 1024 * 1024)),
        cost_estimate=pl.CostEstimate(flops=flops, bytes_accessed=10**6, transcendentals=0),
        name=name,
        **more,
    )(*operands)


def paired(activations, out_grads, lengths, layer_ids, flagged, act_factor, grad_factor):
    size = 16
    per = lengths.shape[0]
    tokens, rank = activations.shape[1:]
    seq_len = tokens // per
    f32, bf16 = jnp.float32, jnp.bfloat16

    def send(x, to):
        return lax.ppermute(x, "blk", [(d, to(d)) for d in range(size)])

    def opposite(d):
        return d ^ 8

    ways = (z_near, lambda d: d ^ 2, lambda d: d ^ 1)
    hbm = pl.BlockSpec(memory_space=pltpu.HBM)
    vmem = pl.BlockSpec(memory_space=pltpu.VMEM)
    shape = jax.ShapeDtypeStruct
    columns = flagged.shape[0]
    unit = shape((2, tokens, rank), bf16)
    data = (activations, out_grads)
    lens = lengths.reshape(1, -1)
    copies = [pltpu.SemaphoreType.DMA((2,))]
    away = call(away_kernel, "away", 3 * 10**9, 53.71, data, [hbm, hbm], unit, copies)
    away = call(
        functools.partial(away_mask_kernel, seq_len),
        "away_mask",
        10**4,
        40,
        (lens, away),
        [],
        unit,
        input_output_aliases={1: 0},
    )
    v = send(away, opposite)
    away, lens, *data = lax.optimization_barrier((away, lens, *data))
    own = call(
        functools.partial(own_kernel, seq_len), "own", 10**9, 40, (lens, *data), [], unit
    )
    near = [send(own, to) for to in ways]
    terms, pick = call(
        functools.partial(setup_kernel, seq_len, per),
        "factor_terms",
        10**9,
        51,
        (layer_ids, flagged.reshape(1, -1), act_factor, grad_factor),
        [pl.BlockSpec(memory_space=pltpu.SMEM), vmem, hbm, hbm],
        (shape((2, 3, rank, rank), bf16), shape((8 * tokens, columns), bf16)),
        [pltpu.VMEM((2, rank, rank), f32), pltpu.SemaphoreType.DMA((2,))],
    )
    v, terms, pick = lax.optimization_barrier((v, terms, pick))
    v3 = send(v, ways[0])
    v, near[2], near[1], near[0] = lax.optimization_barrier((v, near[2], near[1], near[0]))
    v2 = send(v, ways[1])
    whole = shape((2 * per, 8 * tokens), f32)
    sides = shape((4 * per, 6 * tokens), f32)
    rows = shape((2 * per, columns), f32)
    u3, u2, u1 = near

    def kernel(body, name, operands, out_shape, flops=10**9, **more):
        body = functools.partial(body, seq_len, per)
        return call(body, name, flops, 40, operands, [], out_shape, **more)

    white, mine, side = kernel(
        early_kernel,
        "early_pairs",
        (terms, own, v, u3, u2, u1),
        (shape((2, 4 * tokens, rank), bf16), whole, sides),
    )
    v, white = lax.optimization_barrier((v, white))
    v1 = [send(v[w], ways[2]) for w in range(2)]
    mine, side = kernel(
        core_kernel,
        "core_pairs",
        (white, *v1, mine, side),
        (whole, sides),
        flops=10**4,
        input_output_aliases={3: 0, 4: 1},
    )
    white3, side = kernel(
        z_kernel,
        "z_pairs",
        (terms, white, u2, u1, *v1, v3, side),
        (unit, sides),
        flops=10**4,
        input_output_aliases={7: 1},
    )
    by_z, by_x = kernel(
        return_kernel,
        "return_rows",
        (terms, white, white3, pick, side, u3, u1, v3, *v1, v2),
        (rows, rows),
    )
    mine = kernel(rows_kernel, "own_rows", (white, pick, mine, v3, v2), rows)
    half_sum = mine + send(by_z, z_near) + send(by_x, lambda d: d ^ 2)
    return half_sum[:per] + send(half_sum[per:], opposite)


def solution(mesh):
    in_specs = (
        P(None, ("grp", "blk"), None),
        P(None, ("grp", "blk"), None),
        P(("grp", "blk")),
        P("grp"),
        P("grp"),
        P(),
        P(),
    )
    out_specs = P(("grp", "blk"), None)
    shards = paired if mesh.shape["blk"] == 16 else gathered
    return jax.shard_map(shards, mesh=mesh, in_specs=in_specs, out_specs=out_specs, check_vma=False)
```

```python
import functools

import jax
import jax.numpy as jnp
from jax import lax
from jax.experimental import pallas as pl
from jax.experimental.pallas import tpu as pltpu
from jax.sharding import PartitionSpec as P

HIGHEST = lax.Precision.HIGHEST


def tile_scores(white_acts, white_grads, remote_acts, remote_grads, seq_len):
    gram_acts = jnp.einsum(
        "lqr,lkr->lqk", white_acts, remote_acts, preferred_element_type=jnp.float32
    )
    gram_grads = jnp.einsum(
        "lqr,lkr->lqk", white_grads, remote_grads, preferred_element_type=jnp.float32
    )
    pair = jnp.sum(gram_acts * gram_grads, axis=0)
    rows = pair.shape[0] // seq_len
    columns = pair.shape[1] // seq_len
    width = white_acts.shape[2]
    return pair.reshape(rows, seq_len, columns, seq_len).sum(axis=(1, 3)) * (
        1.0 / (width * seq_len)
    )


def gathered(activations, out_grads, lengths, layer_ids, flagged, act_factor, grad_factor):
    tok_rows = activations.shape[1]
    seq_count = lengths.shape[0]
    seq_len = tok_rows // seq_count
    slots = jnp.arange(tok_rows) % seq_len
    keep = (slots < jnp.repeat(lengths, seq_len)).astype(jnp.bfloat16)
    masked_acts = activations * keep[None, :, None]
    masked_grads = out_grads * keep[None, :, None]
    picked_act = jnp.take(act_factor, layer_ids, axis=0)
    picked_grad = jnp.take(grad_factor, layer_ids, axis=0)
    white_acts = jnp.einsum(
        "ltr,lrs->lts", masked_acts.astype(jnp.float32), picked_act, precision=HIGHEST
    ).astype(jnp.bfloat16)
    white_grads = jnp.einsum(
        "ltr,lrs->lts", masked_grads.astype(jnp.float32), picked_grad, precision=HIGHEST
    ).astype(jnp.bfloat16)
    part_scores = tile_scores(
        white_acts,
        white_grads,
        lax.all_gather(masked_acts, "blk", axis=1, tiled=True),
        lax.all_gather(masked_grads, "blk", axis=1, tiled=True),
        seq_len,
    )
    return jnp.take(part_scores, flagged, axis=1)


def z_near(d):
    return d ^ 4 ^ ((d >> 1) & 1)


def away_kernel(acts, grads, out, sems):
    layer = 1 - lax.axis_index("blk") // 8
    copies = [
        pltpu.make_async_copy(src.at[layer], out.at[i], sems.at[i])
        for i, src in enumerate((acts, grads))
    ]
    for copy in copies:
        copy.start()
    for copy in copies:
        copy.wait()


def masked_acts(x, lens, seq_len):
    row = lax.broadcasted_iota(jnp.int32, (x.shape[0], 1), 0)
    bound = jnp.zeros_like(row)
    for s in range(x.shape[0] // seq_len):
        bound = jnp.where(row // seq_len == s, lens[0:1, s : s + 1] + s * seq_len, bound)
    return jnp.where(row < bound, x, jnp.zeros_like(x))


def away_mask_kernel(seq_len, lens, unit, out):
    out[0] = masked_acts(unit[0], lens, seq_len)
    out[1] = unit[1]


def own_kernel(seq_len, lens, acts, grads, out):
    half = lax.axis_index("blk") // 8
    out[0] = masked_acts(acts[half], lens, seq_len)
    out[1] = grads[half]


def whiten(x, terms):
    total = jnp.dot(x, terms[0], preferred_element_type=jnp.float32)
    for n in (1, 2):
        total = total + jnp.dot(x, terms[n], preferred_element_type=jnp.float32)
    return total.astype(jnp.bfloat16)


def stack(*arrays):
    return jnp.concatenate(arrays, axis=0)


def block(seq_len, left, right):
    grams = [
        lax.dot_general(a, b, (((1,), (1,)), ((), ())), preferred_element_type=jnp.float32)
        for a, b in zip(left, right)
    ]
    rows, columns = grams[0].shape
    return (grams[0] * grams[1]).reshape(rows // seq_len, seq_len, columns).sum(axis=1)


def pick_columns(sums, pick):
    rest, terms = sums, []
    for _ in range(3):
        terms.append(rest.astype(jnp.bfloat16))
        rest = rest - terms[-1].astype(jnp.float32)
    n = sums.shape[0]
    out = jnp.dot(stack(*terms), pick[...], preferred_element_type=jnp.float32)
    return out[:n] + out[n : 2 * n] + out[2 * n :]


def setup_kernel(seq_len, per, layer_ids, flagged, act_f, grad_f, terms, pick, factor, sems):
    d = lax.axis_index("blk")
    layer = layer_ids[d // 8]
    copies = [
        pltpu.make_async_copy(src.at[layer], factor.at[i], sems.at[i])
        for i, src in enumerate((act_f, grad_f))
    ]
    for copy in copies:
        copy.start()
    token = lax.broadcasted_iota(jnp.int32, pick.shape, 0)
    spot = token // (seq_len * per)
    slot = spot // 2
    owner = jnp.where(
        slot == 0, d, jnp.where(slot == 1, d ^ 1, jnp.where(slot == 2, d ^ 2, z_near(d)))
    )
    owner = owner ^ (8 * (spot % 2))
    seq = owner * per + token // seq_len % per
    scale = 1.0 / (factor.shape[1] * seq_len)
    pick[...] = jnp.where(seq == flagged[...], scale, 0.0).astype(pick.dtype)
    for w, copy in enumerate(copies):
        copy.wait()
        rest = factor[w]
        for t in range(3):
            term = rest.astype(jnp.bfloat16)
            terms[w, t] = term
            rest = rest - term.astype(jnp.float32)


def early_kernel(seq_len, per, terms, u0, v, u1, u2, u3, white, mine, side):
    n = u0.shape[1]
    rows = []
    for w in range(2):
        white[w] = whiten(stack(u0[w], v[w], u2[w], u3[w]), terms.at[w])
        rows.append(white[w])
    left = {
        0: [r[: 2 * n] for r in rows],
        2: [r[2 * n : 3 * n] for r in rows],
        3: [r[3 * n : 4 * n] for r in rows],
    }
    tok = [[u[w] for w in range(2)] for u in (u0, u1, u2, u3)]
    mine[...] = jnp.zeros_like(mine)
    mine[:, 0 : 2 * n] = block(seq_len, left[0], [stack(u0[w], v[w]) for w in range(2)])
    for slot in (1, 2, 3):
        at = 2 * n * slot
        mine[:, at : at + n] = block(seq_len, left[0], tok[slot])
    side[...] = jnp.zeros_like(side)
    for row, slot, other in ((0, 2, 3), (2 * per, 3, 2)):
        for column in (1, other):
            at = 2 * n * (column - 1)
            side[row : row + per, at : at + n] = block(seq_len, left[slot], tok[column])


def core_kernel(seq_len, per, white, acts, grads, mine, side, mine_out, side_out):
    n = acts.shape[0]
    tok = [acts[...], grads[...]]
    mine_out[...] = mine[...]
    mine_out[:, 3 * n : 4 * n] = block(seq_len, [white[w, : 2 * n] for w in range(2)], tok)
    side_out[...] = side[...]
    got = block(seq_len, [white[w, 2 * n : 4 * n] for w in range(2)], tok)
    for i, row in enumerate((0, 2 * per)):
        side_out[row : row + per, n : 2 * n] = got[i * per : (i + 1) * per]


def z_kernel(
    seq_len, per, terms, white, u2, u1, acts, grads, v3, side, white3, side_out
):
    n = v3.shape[1]
    tok = [v3[w] for w in range(2)]
    core = (acts[...], grads[...])
    fresh = [whiten(tok[w], terms.at[w]) for w in range(2)]
    for w in range(2):
        white3[w] = fresh[w]
    side_out[...] = side[...]
    side_out[0:per, 5 * n : 6 * n] = block(
        seq_len, [white[w, 2 * n : 3 * n] for w in range(2)], tok
    )
    side_out[3 * per : 4 * per, 0 : 3 * n] = block(
        seq_len, fresh, [stack(u1[w], core[w], u2[w]) for w in range(2)]
    )


def return_kernel(
    seq_len, per, terms, white, white3, pick, side, u3, u1, v3, acts, grads, v2, by_z, by_x
):
    n = v2.shape[1]
    tok = [v2[w] for w in range(2)]
    core = (acts[...], grads[...])
    by_row = block(
        seq_len,
        [whiten(tok[w], terms.at[w]) for w in range(2)],
        [stack(u1[w], core[w], u3[w], v3[w]) for w in range(2)],
    )
    by_column = block(
        seq_len, [stack(white[w, 3 * n : 4 * n], white3[w]) for w in range(2)], tok
    )
    zeros = jnp.zeros((per, 2 * n), jnp.float32)
    none = jnp.zeros((per, 6 * n), jnp.float32)
    row = jnp.concatenate([by_row[:, : 2 * n], zeros, by_row[:, 2 * n :]], axis=1)
    lead = jnp.zeros((2 * per, 3 * n), jnp.float32)
    both = jnp.concatenate([lead, by_column, lead[:, : 2 * n]], axis=1)
    picked = pick_columns(side[...] + stack(none, row, both), pick.at[2 * n :])
    by_x[...] = picked[: 2 * per]
    by_z[...] = picked[2 * per :]


def rows_kernel(seq_len, per, white, pick, mine, v3, v2, out):
    n = v2.shape[1]
    left = [white[w, : 2 * n] for w in range(2)]
    got = block(seq_len, left, [stack(v2[w], v3[w]) for w in range(2)])
    zeros = jnp.zeros((2 * per, n), jnp.float32)
    late = jnp.concatenate([zeros] * 5 + [got[:, :n], zeros, got[:, n:]], axis=1)
    out[...] = pick_columns(mine[...] + late, pick)


def call(kernel, name, flops, limit, operands, specs, out_shape, scratch=(), **more):
    vmem = pl.BlockSpec(memory_space=pltpu.VMEM)
    return pl.pallas_call(
        kernel,
        out_shape=out_shape,
        in_specs=specs + [vmem] * (len(operands) - len(specs)),
        out_specs=jax.tree.map(lambda _: vmem, out_shape),
        scratch_shapes=scratch,
        compiler_params=pltpu.CompilerParams(vmem_limit_bytes=int(limit * 1024 * 1024)),
        cost_estimate=pl.CostEstimate(flops=flops, bytes_accessed=10**6, transcendentals=0),
        name=name,
        **more,
    )(*operands)


def paired(activations, out_grads, lengths, layer_ids, flagged, act_factor, grad_factor):
    size = 16
    per = lengths.shape[0]
    tokens, rank = activations.shape[1:]
    seq_len = tokens // per
    f32, bf16 = jnp.float32, jnp.bfloat16

    def send(x, to):
        return lax.ppermute(x, "blk", [(d, to(d)) for d in range(size)])

    def opposite(d):
        return d ^ 8

    ways = (z_near, lambda d: d ^ 2, lambda d: d ^ 1)
    hbm = pl.BlockSpec(memory_space=pltpu.HBM)
    vmem = pl.BlockSpec(memory_space=pltpu.VMEM)
    shape = jax.ShapeDtypeStruct
    columns = flagged.shape[0]
    unit = shape((2, tokens, rank), bf16)
    data = (activations, out_grads)
    lens = lengths.reshape(1, -1)
    copies = [pltpu.SemaphoreType.DMA((2,))]
    away = call(away_kernel, "away", 3 * 10**9, 53.71, data, [hbm, hbm], unit, copies)
    away = call(
        functools.partial(away_mask_kernel, seq_len),
        "away_mask",
        10**4,
        40,
        (lens, away),
        [],
        unit,
        input_output_aliases={1: 0},
    )
    v = send(away, opposite)
    away, lens, *data = lax.optimization_barrier((away, lens, *data))
    own = call(
        functools.partial(own_kernel, seq_len), "own", 10**9, 40, (lens, *data), [], unit
    )
    near = [send(own, to) for to in ways]
    terms, pick = call(
        functools.partial(setup_kernel, seq_len, per),
        "factor_terms",
        10**9,
        51,
        (layer_ids, flagged.reshape(1, -1), act_factor, grad_factor),
        [pl.BlockSpec(memory_space=pltpu.SMEM), vmem, hbm, hbm],
        (shape((2, 3, rank, rank), bf16), shape((8 * tokens, columns), bf16)),
        [pltpu.VMEM((2, rank, rank), f32), pltpu.SemaphoreType.DMA((2,))],
    )
    v, terms, pick = lax.optimization_barrier((v, terms, pick))
    v3 = send(v, ways[0])
    v, near[0] = lax.optimization_barrier((v, near[0]))
    v2 = send(v, ways[1])
    whole = shape((2 * per, 8 * tokens), f32)
    sides = shape((4 * per, 6 * tokens), f32)
    rows = shape((2 * per, columns), f32)
    u3, u2, u1 = near

    def kernel(body, name, operands, out_shape, flops=10**9, **more):
        body = functools.partial(body, seq_len, per)
        return call(body, name, flops, 40, operands, [], out_shape, **more)

    white, mine, side = kernel(
        early_kernel,
        "early_pairs",
        (terms, own, v, u1, u2, u3),
        (shape((2, 4 * tokens, rank), bf16), whole, sides),
    )
    v, white = lax.optimization_barrier((v, white))
    v1 = [send(v[w], ways[2]) for w in range(2)]
    mine, side = kernel(
        core_kernel,
        "core_pairs",
        (white, *v1, mine, side),
        (whole, sides),
        flops=10**4,
        input_output_aliases={3: 0, 4: 1},
    )
    white3, side = kernel(
        z_kernel,
        "z_pairs",
        (terms, white, u2, u1, *v1, v3, side),
        (unit, sides),
        flops=10**4,
        input_output_aliases={7: 1},
    )
    by_z, by_x = kernel(
        return_kernel,
        "return_rows",
        (terms, white, white3, pick, side, u3, u1, v3, *v1, v2),
        (rows, rows),
    )
    mine = kernel(rows_kernel, "own_rows", (white, pick, mine, v3, v2), rows)
    half_sum = mine + send(by_z, z_near) + send(by_x, lambda d: d ^ 2)
    return half_sum[:per] + send(half_sum[per:], opposite)


def solution(mesh):
    in_specs = (
        P(None, ("grp", "blk"), None),
        P(None, ("grp", "blk"), None),
        P(("grp", "blk")),
        P("grp"),
        P("grp"),
        P(),
        P(),
    )
    out_specs = P(("grp", "blk"), None)
    shards = paired if mesh.shape["blk"] == 16 else gathered
    return jax.shard_map(shards, mesh=mesh, in_specs=in_specs, out_specs=out_specs, check_vma=False)
```

```python
import functools

import jax
import jax.numpy as jnp
from jax import lax
from jax.experimental import pallas as pl
from jax.experimental.pallas import tpu as pltpu
from jax.sharding import PartitionSpec as P

HIGHEST = lax.Precision.HIGHEST


def tile_scores(white_acts, white_grads, remote_acts, remote_grads, seq_len):
    gram_acts = jnp.einsum(
        "lqr,lkr->lqk", white_acts, remote_acts, preferred_element_type=jnp.float32
    )
    gram_grads = jnp.einsum(
        "lqr,lkr->lqk", white_grads, remote_grads, preferred_element_type=jnp.float32
    )
    pair = jnp.sum(gram_acts * gram_grads, axis=0)
    rows = pair.shape[0] // seq_len
    columns = pair.shape[1] // seq_len
    width = white_acts.shape[2]
    return pair.reshape(rows, seq_len, columns, seq_len).sum(axis=(1, 3)) * (
        1.0 / (width * seq_len)
    )


def gathered(activations, out_grads, lengths, layer_ids, flagged, act_factor, grad_factor):
    tok_rows = activations.shape[1]
    seq_count = lengths.shape[0]
    seq_len = tok_rows // seq_count
    slots = jnp.arange(tok_rows) % seq_len
    keep = (slots < jnp.repeat(lengths, seq_len)).astype(jnp.bfloat16)
    masked_acts = activations * keep[None, :, None]
    masked_grads = out_grads * keep[None, :, None]
    picked_act = jnp.take(act_factor, layer_ids, axis=0)
    picked_grad = jnp.take(grad_factor, layer_ids, axis=0)
    white_acts = jnp.einsum(
        "ltr,lrs->lts", masked_acts.astype(jnp.float32), picked_act, precision=HIGHEST
    ).astype(jnp.bfloat16)
    white_grads = jnp.einsum(
        "ltr,lrs->lts", masked_grads.astype(jnp.float32), picked_grad, precision=HIGHEST
    ).astype(jnp.bfloat16)
    part_scores = tile_scores(
        white_acts,
        white_grads,
        lax.all_gather(masked_acts, "blk", axis=1, tiled=True),
        lax.all_gather(masked_grads, "blk", axis=1, tiled=True),
        seq_len,
    )
    return jnp.take(part_scores, flagged, axis=1)


def z_near(d):
    return d ^ 4 ^ ((d >> 1) & 1)


def away_kernel(acts, grads, out, sems):
    layer = 1 - lax.axis_index("blk") // 8
    copies = [
        pltpu.make_async_copy(src.at[layer], out.at[i], sems.at[i])
        for i, src in enumerate((acts, grads))
    ]
    for copy in copies:
        copy.start()
    for copy in copies:
        copy.wait()


def masked_acts(x, lens, seq_len):
    row = lax.broadcasted_iota(jnp.int32, (x.shape[0], 1), 0)
    bound = jnp.zeros_like(row)
    for s in range(x.shape[0] // seq_len):
        bound = jnp.where(row // seq_len == s, lens[0:1, s : s + 1] + s * seq_len, bound)
    return jnp.where(row < bound, x, jnp.zeros_like(x))


def away_mask_kernel(seq_len, lens, unit, out):
    out[0] = masked_acts(unit[0], lens, seq_len)
    out[1] = unit[1]


def own_kernel(seq_len, lens, acts, grads, out):
    half = lax.axis_index("blk") // 8
    out[0] = masked_acts(acts[half], lens, seq_len)
    out[1] = grads[half]


def whiten(x, terms):
    total = jnp.dot(x, terms[0], preferred_element_type=jnp.float32)
    for n in (1, 2):
        total = total + jnp.dot(x, terms[n], preferred_element_type=jnp.float32)
    return total.astype(jnp.bfloat16)


def stack(*arrays):
    return jnp.concatenate(arrays, axis=0)


def block(seq_len, left, right):
    grams = [
        lax.dot_general(a, b, (((1,), (1,)), ((), ())), preferred_element_type=jnp.float32)
        for a, b in zip(left, right)
    ]
    rows, columns = grams[0].shape
    return (grams[0] * grams[1]).reshape(rows // seq_len, seq_len, columns).sum(axis=1)


def pick_columns(sums, pick):
    rest, terms = sums, []
    for _ in range(3):
        terms.append(rest.astype(jnp.bfloat16))
        rest = rest - terms[-1].astype(jnp.float32)
    n = sums.shape[0]
    out = jnp.dot(stack(*terms), pick[...], preferred_element_type=jnp.float32)
    return out[:n] + out[n : 2 * n] + out[2 * n :]


def setup_kernel(seq_len, per, layer_ids, flagged, act_f, grad_f, terms, pick, factor, sems):
    d = lax.axis_index("blk")
    layer = layer_ids[d // 8]
    copies = [
        pltpu.make_async_copy(src.at[layer], factor.at[i], sems.at[i])
        for i, src in enumerate((act_f, grad_f))
    ]
    for copy in copies:
        copy.start()
    token = lax.broadcasted_iota(jnp.int32, pick.shape, 0)
    spot = token // (seq_len * per)
    slot = spot // 2
    owner = jnp.where(
        slot == 0, d, jnp.where(slot == 1, d ^ 1, jnp.where(slot == 2, d ^ 2, z_near(d)))
    )
    owner = owner ^ (8 * (spot % 2))
    seq = owner * per + token // seq_len % per
    scale = 1.0 / (factor.shape[1] * seq_len)
    pick[...] = jnp.where(seq == flagged[...], scale, 0.0).astype(pick.dtype)
    for w, copy in enumerate(copies):
        copy.wait()
        rest = factor[w]
        for t in range(3):
            term = rest.astype(jnp.bfloat16)
            terms[w, t] = term
            rest = rest - term.astype(jnp.float32)


def early_kernel(seq_len, per, terms, u0, v, u1, u2, u3, white, mine, side):
    n = u0.shape[1]
    rows = []
    for w in range(2):
        white[w] = whiten(stack(u0[w], v[w], u2[w], u3[w]), terms.at[w])
        rows.append(white[w])
    left = {
        0: [r[: 2 * n] for r in rows],
        2: [r[2 * n : 3 * n] for r in rows],
        3: [r[3 * n : 4 * n] for r in rows],
    }
    tok = [[u[w] for w in range(2)] for u in (u0, u1, u2, u3)]
    mine[...] = jnp.zeros_like(mine)
    mine[:, 0 : 2 * n] = block(seq_len, left[0], [stack(u0[w], v[w]) for w in range(2)])
    for slot in (1, 2, 3):
        at = 2 * n * slot
        mine[:, at : at + n] = block(seq_len, left[0], tok[slot])
    side[...] = jnp.zeros_like(side)
    for row, slot, other in ((0, 2, 3), (2 * per, 3, 2)):
        for column in (1, other):
            at = 2 * n * (column - 1)
            side[row : row + per, at : at + n] = block(seq_len, left[slot], tok[column])


def core_kernel(seq_len, per, white, acts, grads, mine, side, mine_out, side_out):
    n = acts.shape[0]
    tok = [acts[...], grads[...]]
    mine_out[...] = mine[...]
    mine_out[:, 3 * n : 4 * n] = block(seq_len, [white[w, : 2 * n] for w in range(2)], tok)
    side_out[...] = side[...]
    got = block(seq_len, [white[w, 2 * n : 4 * n] for w in range(2)], tok)
    for i, row in enumerate((0, 2 * per)):
        side_out[row : row + per, n : 2 * n] = got[i * per : (i + 1) * per]


def z_kernel(
    seq_len, per, terms, white, u2, u1, acts, grads, v3, side, white3, side_out
):
    n = v3.shape[1]
    tok = [v3[w] for w in range(2)]
    core = (acts[...], grads[...])
    fresh = [whiten(tok[w], terms.at[w]) for w in range(2)]
    for w in range(2):
        white3[w] = fresh[w]
    side_out[...] = side[...]
    side_out[0:per, 5 * n : 6 * n] = block(
        seq_len, [white[w, 2 * n : 3 * n] for w in range(2)], tok
    )
    side_out[3 * per : 4 * per, 0 : 3 * n] = block(
        seq_len, fresh, [stack(u1[w], core[w], u2[w]) for w in range(2)]
    )


def return_kernel(
    seq_len, per, terms, white, white3, pick, side, u3, u1, v3, acts, grads, v2, by_z, by_x
):
    n = v2.shape[1]
    tok = [v2[w] for w in range(2)]
    core = (acts[...], grads[...])
    by_row = block(
        seq_len,
        [whiten(tok[w], terms.at[w]) for w in range(2)],
        [stack(u1[w], core[w], u3[w], v3[w]) for w in range(2)],
    )
    by_column = block(
        seq_len, [stack(white[w, 3 * n : 4 * n], white3[w]) for w in range(2)], tok
    )
    zeros = jnp.zeros((per, 2 * n), jnp.float32)
    none = jnp.zeros((per, 6 * n), jnp.float32)
    row = jnp.concatenate([by_row[:, : 2 * n], zeros, by_row[:, 2 * n :]], axis=1)
    lead = jnp.zeros((2 * per, 3 * n), jnp.float32)
    both = jnp.concatenate([lead, by_column, lead[:, : 2 * n]], axis=1)
    picked = pick_columns(side[...] + stack(none, row, both), pick.at[2 * n :])
    by_x[...] = picked[: 2 * per]
    by_z[...] = picked[2 * per :]


def rows_kernel(seq_len, per, white, pick, mine, v3, v2, out):
    n = v2.shape[1]
    left = [white[w, : 2 * n] for w in range(2)]
    got = block(seq_len, left, [stack(v2[w], v3[w]) for w in range(2)])
    zeros = jnp.zeros((2 * per, n), jnp.float32)
    late = jnp.concatenate([zeros] * 5 + [got[:, :n], zeros, got[:, n:]], axis=1)
    out[...] = pick_columns(mine[...] + late, pick)


def call(kernel, name, flops, limit, operands, specs, out_shape, scratch=(), **more):
    vmem = pl.BlockSpec(memory_space=pltpu.VMEM)
    return pl.pallas_call(
        kernel,
        out_shape=out_shape,
        in_specs=specs + [vmem] * (len(operands) - len(specs)),
        out_specs=jax.tree.map(lambda _: vmem, out_shape),
        scratch_shapes=scratch,
        compiler_params=pltpu.CompilerParams(vmem_limit_bytes=int(limit * 1024 * 1024)),
        cost_estimate=pl.CostEstimate(flops=flops, bytes_accessed=10**6, transcendentals=0),
        name=name,
        **more,
    )(*operands)


def paired(activations, out_grads, lengths, layer_ids, flagged, act_factor, grad_factor):
    size = 16
    per = lengths.shape[0]
    tokens, rank = activations.shape[1:]
    seq_len = tokens // per
    f32, bf16 = jnp.float32, jnp.bfloat16

    def send(x, to):
        return lax.ppermute(x, "blk", [(d, to(d)) for d in range(size)])

    def opposite(d):
        return d ^ 8

    ways = (z_near, lambda d: d ^ 2, lambda d: d ^ 1)
    hbm = pl.BlockSpec(memory_space=pltpu.HBM)
    vmem = pl.BlockSpec(memory_space=pltpu.VMEM)
    shape = jax.ShapeDtypeStruct
    columns = flagged.shape[0]
    unit = shape((2, tokens, rank), bf16)
    data = (activations, out_grads)
    lens = lengths.reshape(1, -1)
    copies = [pltpu.SemaphoreType.DMA((2,))]
    away = call(away_kernel, "away", 3 * 10**9, 53.71, data, [hbm, hbm], unit, copies)
    away = call(
        functools.partial(away_mask_kernel, seq_len),
        "away_mask",
        10**4,
        40,
        (lens, away),
        [],
        unit,
        input_output_aliases={1: 0},
    )
    v = send(away, opposite)
    away, lens, *data = lax.optimization_barrier((away, lens, *data))
    own = call(
        functools.partial(own_kernel, seq_len), "own", 10**9, 40, (lens, *data), [], unit
    )
    near = [send(own, to) for to in ways]
    terms, pick = call(
        functools.partial(setup_kernel, seq_len, per),
        "factor_terms",
        10**9,
        51,
        (layer_ids, flagged.reshape(1, -1), act_factor, grad_factor),
        [pl.BlockSpec(memory_space=pltpu.SMEM), vmem, hbm, hbm],
        (shape((2, 3, rank, rank), bf16), shape((8 * tokens, columns), bf16)),
        [pltpu.VMEM((2, rank, rank), f32), pltpu.SemaphoreType.DMA((2,))],
    )
    v, terms, pick = lax.optimization_barrier((v, terms, pick))
    v3 = send(v, ways[0])
    v, near[2] = lax.optimization_barrier((v, near[2]))
    v2 = send(v, ways[1])
    whole = shape((2 * per, 8 * tokens), f32)
    sides = shape((4 * per, 6 * tokens), f32)
    rows = shape((2 * per, columns), f32)
    u3, u2, u1 = near

    def kernel(body, name, operands, out_shape, flops=10**9, **more):
        body = functools.partial(body, seq_len, per)
        return call(body, name, flops, 40, operands, [], out_shape, **more)

    white, mine, side = kernel(
        early_kernel,
        "early_pairs",
        (terms, own, v, u1, u2, u3),
        (shape((2, 4 * tokens, rank), bf16), whole, sides),
    )
    v, white = lax.optimization_barrier((v, white))
    v1 = [send(v[w], ways[2]) for w in range(2)]
    mine, side = kernel(
        core_kernel,
        "core_pairs",
        (white, *v1, mine, side),
        (whole, sides),
        flops=10**4,
        input_output_aliases={3: 0, 4: 1},
    )
    white3, side = kernel(
        z_kernel,
        "z_pairs",
        (terms, white, u2, u1, *v1, v3, side),
        (unit, sides),
        flops=10**4,
        input_output_aliases={7: 1},
    )
    by_z, by_x = kernel(
        return_kernel,
        "return_rows",
        (terms, white, white3, pick, side, u3, u1, v3, *v1, v2),
        (rows, rows),
    )
    mine = kernel(rows_kernel, "own_rows", (white, pick, mine, v3, v2), rows)
    half_sum = mine + send(by_z, z_near) + send(by_x, lambda d: d ^ 2)
    return half_sum[:per] + send(half_sum[per:], opposite)


def solution(mesh):
    in_specs = (
        P(None, ("grp", "blk"), None),
        P(None, ("grp", "blk"), None),
        P(("grp", "blk")),
        P("grp"),
        P("grp"),
        P(),
        P(),
    )
    out_specs = P(("grp", "blk"), None)
    shards = paired if mesh.shape["blk"] == 16 else gathered
    return jax.shard_map(shards, mesh=mesh, in_specs=in_specs, out_specs=out_specs, check_vma=False)
```

```python
import functools

import jax
import jax.numpy as jnp
from jax import lax
from jax.experimental import pallas as pl
from jax.experimental.pallas import tpu as pltpu
from jax.sharding import PartitionSpec as P

HIGHEST = lax.Precision.HIGHEST


def tile_scores(white_acts, white_grads, remote_acts, remote_grads, seq_len):
    gram_acts = jnp.einsum(
        "lqr,lkr->lqk", white_acts, remote_acts, preferred_element_type=jnp.float32
    )
    gram_grads = jnp.einsum(
        "lqr,lkr->lqk", white_grads, remote_grads, preferred_element_type=jnp.float32
    )
    pair = jnp.sum(gram_acts * gram_grads, axis=0)
    rows = pair.shape[0] // seq_len
    columns = pair.shape[1] // seq_len
    width = white_acts.shape[2]
    return pair.reshape(rows, seq_len, columns, seq_len).sum(axis=(1, 3)) * (
        1.0 / (width * seq_len)
    )


def gathered(activations, out_grads, lengths, layer_ids, flagged, act_factor, grad_factor):
    tok_rows = activations.shape[1]
    seq_count = lengths.shape[0]
    seq_len = tok_rows // seq_count
    slots = jnp.arange(tok_rows) % seq_len
    keep = (slots < jnp.repeat(lengths, seq_len)).astype(jnp.bfloat16)
    masked_acts = activations * keep[None, :, None]
    masked_grads = out_grads * keep[None, :, None]
    picked_act = jnp.take(act_factor, layer_ids, axis=0)
    picked_grad = jnp.take(grad_factor, layer_ids, axis=0)
    white_acts = jnp.einsum(
        "ltr,lrs->lts", masked_acts.astype(jnp.float32), picked_act, precision=HIGHEST
    ).astype(jnp.bfloat16)
    white_grads = jnp.einsum(
        "ltr,lrs->lts", masked_grads.astype(jnp.float32), picked_grad, precision=HIGHEST
    ).astype(jnp.bfloat16)
    part_scores = tile_scores(
        white_acts,
        white_grads,
        lax.all_gather(masked_acts, "blk", axis=1, tiled=True),
        lax.all_gather(masked_grads, "blk", axis=1, tiled=True),
        seq_len,
    )
    return jnp.take(part_scores, flagged, axis=1)


def z_near(d):
    return d ^ 4 ^ ((d >> 1) & 1)


def away_kernel(acts, grads, out, sems):
    layer = 1 - lax.axis_index("blk") // 8
    copies = [
        pltpu.make_async_copy(src.at[layer], out.at[i], sems.at[i])
        for i, src in enumerate((acts, grads))
    ]
    for copy in copies:
        copy.start()
    for copy in copies:
        copy.wait()


def masked_acts(x, lens, seq_len):
    row = lax.broadcasted_iota(jnp.int32, (x.shape[0], 1), 0)
    bound = jnp.zeros_like(row)
    for s in range(x.shape[0] // seq_len):
        bound = jnp.where(row // seq_len == s, lens[0:1, s : s + 1] + s * seq_len, bound)
    return jnp.where(row < bound, x, jnp.zeros_like(x))


def away_mask_kernel(seq_len, lens, unit, out):
    out[0] = masked_acts(unit[0], lens, seq_len)
    out[1] = unit[1]


def own_kernel(seq_len, lens, acts, grads, out):
    half = lax.axis_index("blk") // 8
    out[0] = masked_acts(acts[half], lens, seq_len)
    out[1] = grads[half]


def whiten(x, terms):
    wide = jnp.concatenate([x] * 3, axis=1)
    return jnp.dot(wide, terms[...], preferred_element_type=jnp.float32).astype(jnp.bfloat16)


def stack(*arrays):
    return jnp.concatenate(arrays, axis=0)


def block(seq_len, left, right):
    grams = [
        lax.dot_general(a, b, (((1,), (1,)), ((), ())), preferred_element_type=jnp.float32)
        for a, b in zip(left, right)
    ]
    rows, columns = grams[0].shape
    return (grams[0] * grams[1]).reshape(rows // seq_len, seq_len, columns).sum(axis=1)


def pick_columns(sums, pick):
    rest, terms = sums, []
    for _ in range(3):
        terms.append(rest.astype(jnp.bfloat16))
        rest = rest - terms[-1].astype(jnp.float32)
    n = sums.shape[0]
    out = jnp.dot(stack(*terms), pick[...], preferred_element_type=jnp.float32)
    return out[:n] + out[n : 2 * n] + out[2 * n :]


def setup_kernel(seq_len, per, layer_ids, flagged, act_f, grad_f, terms, pick, factor, sems):
    d = lax.axis_index("blk")
    layer = layer_ids[d // 8]
    copies = [
        pltpu.make_async_copy(src.at[layer], factor.at[i], sems.at[i])
        for i, src in enumerate((act_f, grad_f))
    ]
    for copy in copies:
        copy.start()
    token = lax.broadcasted_iota(jnp.int32, pick.shape, 0)
    spot = token // (seq_len * per)
    slot = spot // 2
    owner = jnp.where(
        slot == 0, d, jnp.where(slot == 1, d ^ 1, jnp.where(slot == 2, d ^ 2, z_near(d)))
    )
    owner = owner ^ (8 * (spot % 2))
    seq = owner * per + token // seq_len % per
    scale = 1.0 / (factor.shape[1] * seq_len)
    pick[...] = jnp.where(seq == flagged[...], scale, 0.0).astype(pick.dtype)
    for w, copy in enumerate(copies):
        copy.wait()
        rest = factor[w]
        for t in range(3):
            term = rest.astype(jnp.bfloat16)
            terms[w, t * rest.shape[0] : (t + 1) * rest.shape[0]] = term
            rest = rest - term.astype(jnp.float32)


def early_kernel(seq_len, per, terms, u0, v, u1, u2, u3, white, mine, side):
    n = u0.shape[1]
    rows = []
    for w in range(2):
        white[w] = whiten(stack(u0[w], v[w], u2[w], u3[w]), terms.at[w])
        rows.append(white[w])
    left = {
        0: [r[: 2 * n] for r in rows],
        2: [r[2 * n : 3 * n] for r in rows],
        3: [r[3 * n : 4 * n] for r in rows],
    }
    tok = [[u[w] for w in range(2)] for u in (u0, u1, u2, u3)]
    mine[...] = jnp.zeros_like(mine)
    mine[:, 0 : 2 * n] = block(seq_len, left[0], [stack(u0[w], v[w]) for w in range(2)])
    for slot in (1, 2, 3):
        at = 2 * n * slot
        mine[:, at : at + n] = block(seq_len, left[0], tok[slot])
    side[...] = jnp.zeros_like(side)
    for row, slot, other in ((0, 2, 3), (2 * per, 3, 2)):
        for column in (1, other):
            at = 2 * n * (column - 1)
            side[row : row + per, at : at + n] = block(seq_len, left[slot], tok[column])


def core_kernel(seq_len, per, white, acts, grads, mine, side, mine_out, side_out):
    n = acts.shape[0]
    tok = [acts[...], grads[...]]
    mine_out[...] = mine[...]
    mine_out[:, 3 * n : 4 * n] = block(seq_len, [white[w, : 2 * n] for w in range(2)], tok)
    side_out[...] = side[...]
    got = block(seq_len, [white[w, 2 * n : 4 * n] for w in range(2)], tok)
    for i, row in enumerate((0, 2 * per)):
        side_out[row : row + per, n : 2 * n] = got[i * per : (i + 1) * per]


def z_kernel(
    seq_len, per, terms, white, u2, u1, acts, grads, v3, side, white3, side_out
):
    n = v3.shape[1]
    tok = [v3[w] for w in range(2)]
    core = (acts[...], grads[...])
    fresh = [whiten(tok[w], terms.at[w]) for w in range(2)]
    for w in range(2):
        white3[w] = fresh[w]
    side_out[...] = side[...]
    side_out[0:per, 5 * n : 6 * n] = block(
        seq_len, [white[w, 2 * n : 3 * n] for w in range(2)], tok
    )
    side_out[3 * per : 4 * per, 0 : 3 * n] = block(
        seq_len, fresh, [stack(u1[w], core[w], u2[w]) for w in range(2)]
    )


def return_kernel(
    seq_len, per, terms, white, white3, pick, side, u3, u1, v3, acts, grads, v2, by_z, by_x
):
    n = v2.shape[1]
    tok = [v2[w] for w in range(2)]
    core = (acts[...], grads[...])
    by_row = block(
        seq_len,
        [whiten(tok[w], terms.at[w]) for w in range(2)],
        [stack(u1[w], core[w], u3[w], v3[w]) for w in range(2)],
    )
    by_column = block(
        seq_len, [stack(white[w, 3 * n : 4 * n], white3[w]) for w in range(2)], tok
    )
    zeros = jnp.zeros((per, 2 * n), jnp.float32)
    none = jnp.zeros((per, 6 * n), jnp.float32)
    row = jnp.concatenate([by_row[:, : 2 * n], zeros, by_row[:, 2 * n :]], axis=1)
    lead = jnp.zeros((2 * per, 3 * n), jnp.float32)
    both = jnp.concatenate([lead, by_column, lead[:, : 2 * n]], axis=1)
    picked = pick_columns(side[...] + stack(none, row, both), pick.at[2 * n :])
    by_x[...] = picked[: 2 * per]
    by_z[...] = picked[2 * per :]


def rows_kernel(seq_len, per, white, pick, mine, v3, v2, out):
    n = v2.shape[1]
    left = [white[w, : 2 * n] for w in range(2)]
    got = block(seq_len, left, [stack(v2[w], v3[w]) for w in range(2)])
    zeros = jnp.zeros((2 * per, n), jnp.float32)
    late = jnp.concatenate([zeros] * 5 + [got[:, :n], zeros, got[:, n:]], axis=1)
    out[...] = pick_columns(mine[...] + late, pick)


def call(kernel, name, flops, limit, operands, specs, out_shape, scratch=(), **more):
    vmem = pl.BlockSpec(memory_space=pltpu.VMEM)
    return pl.pallas_call(
        kernel,
        out_shape=out_shape,
        in_specs=specs + [vmem] * (len(operands) - len(specs)),
        out_specs=jax.tree.map(lambda _: vmem, out_shape),
        scratch_shapes=scratch,
        compiler_params=pltpu.CompilerParams(vmem_limit_bytes=int(limit * 1024 * 1024)),
        cost_estimate=pl.CostEstimate(flops=flops, bytes_accessed=10**6, transcendentals=0),
        name=name,
        **more,
    )(*operands)


def paired(activations, out_grads, lengths, layer_ids, flagged, act_factor, grad_factor):
    size = 16
    per = lengths.shape[0]
    tokens, rank = activations.shape[1:]
    seq_len = tokens // per
    f32, bf16 = jnp.float32, jnp.bfloat16

    def send(x, to):
        return lax.ppermute(x, "blk", [(d, to(d)) for d in range(size)])

    def opposite(d):
        return d ^ 8

    ways = (z_near, lambda d: d ^ 2, lambda d: d ^ 1)
    hbm = pl.BlockSpec(memory_space=pltpu.HBM)
    vmem = pl.BlockSpec(memory_space=pltpu.VMEM)
    shape = jax.ShapeDtypeStruct
    columns = flagged.shape[0]
    unit = shape((2, tokens, rank), bf16)
    data = (activations, out_grads)
    lens = lengths.reshape(1, -1)
    copies = [pltpu.SemaphoreType.DMA((2,))]
    away = call(away_kernel, "away", 3 * 10**9, 53.71, data, [hbm, hbm], unit, copies)
    away = call(
        functools.partial(away_mask_kernel, seq_len),
        "away_mask",
        10**4,
        40,
        (lens, away),
        [],
        unit,
        input_output_aliases={1: 0},
    )
    v = send(away, opposite)
    away, lens, *data = lax.optimization_barrier((away, lens, *data))
    own = call(
        functools.partial(own_kernel, seq_len), "own", 10**9, 40, (lens, *data), [], unit
    )
    near = [send(own, to) for to in ways]
    terms, pick = call(
        functools.partial(setup_kernel, seq_len, per),
        "factor_terms",
        10**9,
        51,
        (layer_ids, flagged.reshape(1, -1), act_factor, grad_factor),
        [pl.BlockSpec(memory_space=pltpu.SMEM), vmem, hbm, hbm],
        (shape((2, 3 * rank, rank), bf16), shape((8 * tokens, columns), bf16)),
        [pltpu.VMEM((2, rank, rank), f32), pltpu.SemaphoreType.DMA((2,))],
    )
    v, terms, pick = lax.optimization_barrier((v, terms, pick))
    v3 = send(v, ways[0])
    v, near[0] = lax.optimization_barrier((v, near[0]))
    v2 = send(v, ways[1])
    whole = shape((2 * per, 8 * tokens), f32)
    sides = shape((4 * per, 6 * tokens), f32)
    rows = shape((2 * per, columns), f32)
    u3, u2, u1 = near

    def kernel(body, name, operands, out_shape, flops=10**9, **more):
        body = functools.partial(body, seq_len, per)
        return call(body, name, flops, 40, operands, [], out_shape, **more)

    white, mine, side = kernel(
        early_kernel,
        "early_pairs",
        (terms, own, v, u1, u2, u3),
        (shape((2, 4 * tokens, rank), bf16), whole, sides),
    )
    v, white = lax.optimization_barrier((v, white))
    v1 = [send(v[w], ways[2]) for w in range(2)]
    mine, side = kernel(
        core_kernel,
        "core_pairs",
        (white, *v1, mine, side),
        (whole, sides),
        flops=10**4,
        input_output_aliases={3: 0, 4: 1},
    )
    white3, side = kernel(
        z_kernel,
        "z_pairs",
        (terms, white, u2, u1, *v1, v3, side),
        (unit, sides),
        flops=10**4,
        input_output_aliases={7: 1},
    )
    by_z, by_x = kernel(
        return_kernel,
        "return_rows",
        (terms, white, white3, pick, side, u3, u1, v3, *v1, v2),
        (rows, rows),
    )
    mine = kernel(rows_kernel, "own_rows", (white, pick, mine, v3, v2), rows)
    half_sum = mine + send(by_z, z_near) + send(by_x, lambda d: d ^ 2)
    return half_sum[:per] + send(half_sum[per:], opposite)


def solution(mesh):
    in_specs = (
        P(None, ("grp", "blk"), None),
        P(None, ("grp", "blk"), None),
        P(("grp", "blk")),
        P("grp"),
        P("grp"),
        P(),
        P(),
    )
    out_specs = P(("grp", "blk"), None)
    shards = paired if mesh.shape["blk"] == 16 else gathered
    return jax.shard_map(shards, mesh=mesh, in_specs=in_specs, out_specs=out_specs, check_vma=False)
```

```python
import functools

import jax
import jax.numpy as jnp
from jax import lax
from jax.experimental import pallas as pl
from jax.experimental.pallas import tpu as pltpu
from jax.sharding import PartitionSpec as P

HIGHEST = lax.Precision.HIGHEST


def tile_scores(white_acts, white_grads, remote_acts, remote_grads, seq_len):
    gram_acts = jnp.einsum(
        "lqr,lkr->lqk", white_acts, remote_acts, preferred_element_type=jnp.float32
    )
    gram_grads = jnp.einsum(
        "lqr,lkr->lqk", white_grads, remote_grads, preferred_element_type=jnp.float32
    )
    pair = jnp.sum(gram_acts * gram_grads, axis=0)
    rows = pair.shape[0] // seq_len
    columns = pair.shape[1] // seq_len
    width = white_acts.shape[2]
    return pair.reshape(rows, seq_len, columns, seq_len).sum(axis=(1, 3)) * (
        1.0 / (width * seq_len)
    )


def gathered(activations, out_grads, lengths, layer_ids, flagged, act_factor, grad_factor):
    tok_rows = activations.shape[1]
    seq_count = lengths.shape[0]
    seq_len = tok_rows // seq_count
    slots = jnp.arange(tok_rows) % seq_len
    keep = (slots < jnp.repeat(lengths, seq_len)).astype(jnp.bfloat16)
    masked_acts = activations * keep[None, :, None]
    masked_grads = out_grads * keep[None, :, None]
    picked_act = jnp.take(act_factor, layer_ids, axis=0)
    picked_grad = jnp.take(grad_factor, layer_ids, axis=0)
    white_acts = jnp.einsum(
        "ltr,lrs->lts", masked_acts.astype(jnp.float32), picked_act, precision=HIGHEST
    ).astype(jnp.bfloat16)
    white_grads = jnp.einsum(
        "ltr,lrs->lts", masked_grads.astype(jnp.float32), picked_grad, precision=HIGHEST
    ).astype(jnp.bfloat16)
    part_scores = tile_scores(
        white_acts,
        white_grads,
        lax.all_gather(masked_acts, "blk", axis=1, tiled=True),
        lax.all_gather(masked_grads, "blk", axis=1, tiled=True),
        seq_len,
    )
    return jnp.take(part_scores, flagged, axis=1)


def z_near(d):
    return d ^ 4 ^ ((d >> 1) & 1)


def away_kernel(acts, grads, out, sems):
    layer = 1 - lax.axis_index("blk") // 8
    copies = [
        pltpu.make_async_copy(src.at[layer], out.at[i], sems.at[i])
        for i, src in enumerate((acts, grads))
    ]
    for copy in copies:
        copy.start()
    for copy in copies:
        copy.wait()


def masked_acts(x, lens, seq_len):
    row = lax.broadcasted_iota(jnp.int32, (x.shape[0], 1), 0)
    bound = jnp.zeros_like(row)
    for s in range(x.shape[0] // seq_len):
        bound = jnp.where(row // seq_len == s, lens[0:1, s : s + 1] + s * seq_len, bound)
    return jnp.where(row < bound, x, jnp.zeros_like(x))


def away_mask_kernel(seq_len, lens, unit, out):
    out[0] = masked_acts(unit[0], lens, seq_len)
    out[1] = unit[1]


def own_kernel(seq_len, lens, acts, grads, out):
    half = lax.axis_index("blk") // 8
    out[0] = masked_acts(acts[half], lens, seq_len)
    out[1] = grads[half]


def whiten(x, terms):
    total = jnp.dot(x, terms[0], preferred_element_type=jnp.float32)
    for n in (1, 2):
        total = total + jnp.dot(x, terms[n], preferred_element_type=jnp.float32)
    return total.astype(jnp.bfloat16)


def stack(*arrays):
    return jnp.concatenate(arrays, axis=0)


def block(seq_len, left, right):
    grams = [
        lax.dot_general(a, b, (((1,), (1,)), ((), ())), preferred_element_type=jnp.float32)
        for a, b in zip(left, right)
    ]
    rows, columns = grams[0].shape
    return (grams[0] * grams[1]).reshape(rows // seq_len, seq_len, columns).sum(axis=1)


def pick_columns(sums, pick):
    rest, terms = sums, []
    for _ in range(3):
        terms.append(rest.astype(jnp.bfloat16))
        rest = rest - terms[-1].astype(jnp.float32)
    n = sums.shape[0]
    out = jnp.dot(stack(*terms), pick[...], preferred_element_type=jnp.float32)
    return out[:n] + out[n : 2 * n] + out[2 * n :]


def setup_kernel(seq_len, per, layer_ids, flagged, act_f, grad_f, terms, pick, factor, sems):
    d = lax.axis_index("blk")
    layer = layer_ids[d // 8]
    copies = [
        pltpu.make_async_copy(src.at[layer], factor.at[i], sems.at[i])
        for i, src in enumerate((act_f, grad_f))
    ]
    for copy in copies:
        copy.start()
    token = lax.broadcasted_iota(jnp.int32, pick.shape, 0)
    spot = token // (seq_len * per)
    slot = spot // 2
    owner = jnp.where(
        slot == 0, d, jnp.where(slot == 1, d ^ 1, jnp.where(slot == 2, d ^ 2, z_near(d)))
    )
    owner = owner ^ (8 * (spot % 2))
    seq = owner * per + token // seq_len % per
    scale = 1.0 / (factor.shape[1] * seq_len)
    pick[...] = jnp.where(seq == flagged[...], scale, 0.0).astype(pick.dtype)
    for w, copy in enumerate(copies):
        copy.wait()
        rest = factor[w]
        for t in range(3):
            term = rest.astype(jnp.bfloat16)
            terms[w, t] = term
            rest = rest - term.astype(jnp.float32)


def early_kernel(seq_len, per, terms, u0, v, u1, u2, u3, white, mine, side):
    n = u0.shape[1]
    rows = []
    for w in range(2):
        white[w] = whiten(stack(u0[w], v[w], u2[w], u3[w]), terms.at[w])
        rows.append(white[w])
    left = {
        0: [r[: 2 * n] for r in rows],
        2: [r[2 * n : 3 * n] for r in rows],
        3: [r[3 * n : 4 * n] for r in rows],
    }
    tok = [[u[w] for w in range(2)] for u in (u0, u1, u2, u3)]
    mine[...] = jnp.zeros_like(mine)
    mine[:, 0 : 2 * n] = block(seq_len, left[0], [stack(u0[w], v[w]) for w in range(2)])
    for slot in (1, 2, 3):
        at = 2 * n * slot
        mine[:, at : at + n] = block(seq_len, left[0], tok[slot])
    side[...] = jnp.zeros_like(side)
    for row, slot, other in ((0, 2, 3), (2 * per, 3, 2)):
        for column in (1, other):
            at = 2 * n * (column - 1)
            side[row : row + per, at : at + n] = block(seq_len, left[slot], tok[column])


def core_kernel(seq_len, per, white, acts, grads, mine, side, mine_out, side_out):
    n = acts.shape[0]
    tok = [acts[...], grads[...]]
    mine_out[...] = mine[...]
    mine_out[:, 3 * n : 4 * n] = block(seq_len, [white[w, : 2 * n] for w in range(2)], tok)
    side_out[...] = side[...]
    got = block(seq_len, [white[w, 2 * n : 4 * n] for w in range(2)], tok)
    for i, row in enumerate((0, 2 * per)):
        side_out[row : row + per, n : 2 * n] = got[i * per : (i + 1) * per]


def z_kernel(
    seq_len, per, terms, white, u2, u1, acts, grads, v3, side, white3, side_out
):
    n = v3.shape[1]
    tok = [v3[w] for w in range(2)]
    core = (acts[...], grads[...])
    fresh = [whiten(tok[w], terms.at[w]) for w in range(2)]
    for w in range(2):
        white3[w] = fresh[w]
    side_out[...] = side[...]
    side_out[0:per, 5 * n : 6 * n] = block(
        seq_len, [white[w, 2 * n : 3 * n] for w in range(2)], tok
    )
    side_out[3 * per : 4 * per, 0 : 3 * n] = block(
        seq_len, fresh, [stack(u1[w], core[w], u2[w]) for w in range(2)]
    )


def return_kernel(
    seq_len, per, terms, white, white3, pick, side, u3, u1, v3, acts, grads, v2, by_z, by_x
):
    n = v2.shape[1]
    tok = [v2[w] for w in range(2)]
    core = (acts[...], grads[...])
    by_row = block(
        seq_len,
        [whiten(tok[w], terms.at[w]) for w in range(2)],
        [stack(u1[w], core[w], u3[w], v3[w]) for w in range(2)],
    )
    by_column = block(
        seq_len, [stack(white[w, 3 * n : 4 * n], white3[w]) for w in range(2)], tok
    )
    zeros = jnp.zeros((per, 2 * n), jnp.float32)
    none = jnp.zeros((per, 6 * n), jnp.float32)
    row = jnp.concatenate([by_row[:, : 2 * n], zeros, by_row[:, 2 * n :]], axis=1)
    lead = jnp.zeros((2 * per, 3 * n), jnp.float32)
    both = jnp.concatenate([lead, by_column, lead[:, : 2 * n]], axis=1)
    picked = pick_columns(side[...] + stack(none, row, both), pick.at[2 * n :])
    by_x[...] = picked[: 2 * per]
    by_z[...] = picked[2 * per :]


def rows_kernel(seq_len, per, white, pick, mine, v3, v2, out):
    n = v2.shape[1]
    left = [white[w, : 2 * n] for w in range(2)]
    got = block(seq_len, left, [stack(v2[w], v3[w]) for w in range(2)])
    zeros = jnp.zeros((2 * per, n), jnp.float32)
    late = jnp.concatenate([zeros] * 5 + [got[:, :n], zeros, got[:, n:]], axis=1)
    out[...] = pick_columns(mine[...] + late, pick)


def call(kernel, name, flops, limit, operands, specs, out_shape, scratch=(), **more):
    vmem = pl.BlockSpec(memory_space=pltpu.VMEM)
    return pl.pallas_call(
        kernel,
        out_shape=out_shape,
        in_specs=specs + [vmem] * (len(operands) - len(specs)),
        out_specs=jax.tree.map(lambda _: vmem, out_shape),
        scratch_shapes=scratch,
        compiler_params=pltpu.CompilerParams(vmem_limit_bytes=int(limit * 1024 * 1024)),
        cost_estimate=pl.CostEstimate(flops=flops, bytes_accessed=10**6, transcendentals=0),
        name=name,
        **more,
    )(*operands)


def paired(activations, out_grads, lengths, layer_ids, flagged, act_factor, grad_factor):
    size = 16
    per = lengths.shape[0]
    tokens, rank = activations.shape[1:]
    seq_len = tokens // per
    f32, bf16 = jnp.float32, jnp.bfloat16

    def send(x, to):
        return lax.ppermute(x, "blk", [(d, to(d)) for d in range(size)])

    def opposite(d):
        return d ^ 8

    ways = (z_near, lambda d: d ^ 2, lambda d: d ^ 1)
    hbm = pl.BlockSpec(memory_space=pltpu.HBM)
    vmem = pl.BlockSpec(memory_space=pltpu.VMEM)
    shape = jax.ShapeDtypeStruct
    columns = flagged.shape[0]
    unit = shape((2, tokens, rank), bf16)
    data = (activations, out_grads)
    lens = lengths.reshape(1, -1)
    copies = [pltpu.SemaphoreType.DMA((2,))]
    away = call(away_kernel, "away", 3 * 10**9, 53.71, data, [hbm, hbm], unit, copies)
    away = call(
        functools.partial(away_mask_kernel, seq_len),
        "away_mask",
        10**4,
        40,
        (lens, away),
        [],
        unit,
        input_output_aliases={1: 0},
    )
    v = send(away, opposite)
    away, lens, *data = lax.optimization_barrier((away, lens, *data))
    own = call(
        functools.partial(own_kernel, seq_len), "own", 10**9, 40, (lens, *data), [], unit
    )
    near = [send(own, to) for to in ways]
    terms, pick = call(
        functools.partial(setup_kernel, seq_len, per),
        "factor_terms",
        10**9,
        51,
        (layer_ids, flagged.reshape(1, -1), act_factor, grad_factor),
        [pl.BlockSpec(memory_space=pltpu.SMEM), vmem, hbm, hbm],
        (shape((2, 3, rank, rank), bf16), shape((8 * tokens, columns), bf16)),
        [pltpu.VMEM((2, rank, rank), f32), pltpu.SemaphoreType.DMA((2,))],
    )
    v, terms, pick = lax.optimization_barrier((v, terms, pick))
    v3 = send(v, ways[0])
    v, near[0] = lax.optimization_barrier((v, near[0]))
    v2 = send(v, ways[1])
    whole = shape((2 * per, 8 * tokens), f32)
    sides = shape((4 * per, 6 * tokens), f32)
    rows = shape((2 * per, columns), f32)
    u3, u2, u1 = near

    def kernel(body, name, operands, out_shape, flops=10**9, **more):
        body = functools.partial(body, seq_len, per)
        return call(body, name, flops, 40, operands, [], out_shape, **more)

    white, mine, side = kernel(
        early_kernel,
        "early_pairs",
        (terms, own, v, u1, u2, u3),
        (shape((2, 4 * tokens, rank), bf16), whole, sides),
    )
    v, white = lax.optimization_barrier((v, white))
    v1 = [send(v[w], ways[2]) for w in range(2)]
    mine, side = kernel(
        core_kernel,
        "core_pairs",
        (white, *v1, mine, side),
        (whole, sides),
        flops=10**4,
        input_output_aliases={3: 0, 4: 1},
    )
    white3, side = kernel(
        z_kernel,
        "z_pairs",
        (terms, white, u2, u1, *v1, v3, side),
        (unit, sides),
        flops=10**4,
        input_output_aliases={7: 1},
    )
    by_z, by_x = kernel(
        return_kernel,
        "return_rows",
        (terms, white, white3, pick, side, u3, u1, v3, *v1, v2),
        (rows, rows),
    )
    mine = kernel(rows_kernel, "own_rows", (white, pick, mine, v3, v2), rows)
    half_sum = mine + send(by_x, lambda d: d ^ 2) + send(by_z, z_near)
    return half_sum[:per] + send(half_sum[per:], opposite)


def solution(mesh):
    in_specs = (
        P(None, ("grp", "blk"), None),
        P(None, ("grp", "blk"), None),
        P(("grp", "blk")),
        P("grp"),
        P("grp"),
        P(),
        P(),
    )
    out_specs = P(("grp", "blk"), None)
    shards = paired if mesh.shape["blk"] == 16 else gathered
    return jax.shard_map(shards, mesh=mesh, in_specs=in_specs, out_specs=out_specs, check_vma=False)
```

```python
import functools

import jax
import jax.numpy as jnp
from jax import lax
from jax.experimental import pallas as pl
from jax.experimental.pallas import tpu as pltpu
from jax.sharding import PartitionSpec as P

HIGHEST = lax.Precision.HIGHEST


def tile_scores(white_acts, white_grads, remote_acts, remote_grads, seq_len):
    gram_acts = jnp.einsum(
        "lqr,lkr->lqk", white_acts, remote_acts, preferred_element_type=jnp.float32
    )
    gram_grads = jnp.einsum(
        "lqr,lkr->lqk", white_grads, remote_grads, preferred_element_type=jnp.float32
    )
    pair = jnp.sum(gram_acts * gram_grads, axis=0)
    rows = pair.shape[0] // seq_len
    columns = pair.shape[1] // seq_len
    width = white_acts.shape[2]
    return pair.reshape(rows, seq_len, columns, seq_len).sum(axis=(1, 3)) * (
        1.0 / (width * seq_len)
    )


def gathered(activations, out_grads, lengths, layer_ids, flagged, act_factor, grad_factor):
    tok_rows = activations.shape[1]
    seq_count = lengths.shape[0]
    seq_len = tok_rows // seq_count
    slots = jnp.arange(tok_rows) % seq_len
    keep = (slots < jnp.repeat(lengths, seq_len)).astype(jnp.bfloat16)
    masked_acts = activations * keep[None, :, None]
    masked_grads = out_grads * keep[None, :, None]
    picked_act = jnp.take(act_factor, layer_ids, axis=0)
    picked_grad = jnp.take(grad_factor, layer_ids, axis=0)
    white_acts = jnp.einsum(
        "ltr,lrs->lts", masked_acts.astype(jnp.float32), picked_act, precision=HIGHEST
    ).astype(jnp.bfloat16)
    white_grads = jnp.einsum(
        "ltr,lrs->lts", masked_grads.astype(jnp.float32), picked_grad, precision=HIGHEST
    ).astype(jnp.bfloat16)
    part_scores = tile_scores(
        white_acts,
        white_grads,
        lax.all_gather(masked_acts, "blk", axis=1, tiled=True),
        lax.all_gather(masked_grads, "blk", axis=1, tiled=True),
        seq_len,
    )
    return jnp.take(part_scores, flagged, axis=1)


def z_near(d):
    return d ^ 4 ^ ((d >> 1) & 1)


def away_kernel(acts, grads, out, sems):
    layer = 1 - lax.axis_index("blk") // 8
    copies = [
        pltpu.make_async_copy(src.at[layer], out.at[i], sems.at[i])
        for i, src in enumerate((acts, grads))
    ]
    for copy in copies:
        copy.start()
    for copy in copies:
        copy.wait()


def masked_acts(x, lens, seq_len):
    row = lax.broadcasted_iota(jnp.int32, (x.shape[0], 1), 0)
    bound = jnp.zeros_like(row)
    for s in range(x.shape[0] // seq_len):
        bound = jnp.where(row // seq_len == s, lens[0:1, s : s + 1] + s * seq_len, bound)
    return jnp.where(row < bound, x, jnp.zeros_like(x))


def away_mask_kernel(seq_len, lens, unit, out):
    out[0] = masked_acts(unit[0], lens, seq_len)
    out[1] = unit[1]


def own_kernel(seq_len, lens, acts, grads, out):
    half = lax.axis_index("blk") // 8
    out[0] = masked_acts(acts[half], lens, seq_len)
    out[1] = grads[half]


def whiten(x, terms):
    total = jnp.dot(x, terms[0], preferred_element_type=jnp.float32)
    for n in (1, 2):
        total = total + jnp.dot(x, terms[n], preferred_element_type=jnp.float32)
    return total.astype(jnp.bfloat16)


def stack(*arrays):
    return jnp.concatenate(arrays, axis=0)


def block(seq_len, left, right):
    grams = [
        lax.dot_general(a, b, (((1,), (1,)), ((), ())), preferred_element_type=jnp.float32)
        for a, b in zip(left, right)
    ]
    rows, columns = grams[0].shape
    return (grams[0] * grams[1]).reshape(rows // seq_len, seq_len, columns).sum(axis=1)


def pick_columns(sums, pick):
    rest, terms = sums, []
    for _ in range(3):
        terms.append(rest.astype(jnp.bfloat16))
        rest = rest - terms[-1].astype(jnp.float32)
    n = sums.shape[0]
    out = jnp.dot(stack(*terms), pick[...], preferred_element_type=jnp.float32)
    return out[:n] + out[n : 2 * n] + out[2 * n :]


def setup_kernel(seq_len, per, layer_ids, flagged, act_f, grad_f, terms, pick, factor, sems):
    d = lax.axis_index("blk")
    layer = layer_ids[d // 8]
    copies = [
        pltpu.make_async_copy(src.at[layer], factor.at[i], sems.at[i])
        for i, src in enumerate((act_f, grad_f))
    ]
    for copy in copies:
        copy.start()
    token = lax.broadcasted_iota(jnp.int32, pick.shape, 0)
    spot = token // (seq_len * per)
    slot = spot // 2
    owner = jnp.where(
        slot == 0, d, jnp.where(slot == 1, d ^ 1, jnp.where(slot == 2, d ^ 2, z_near(d)))
    )
    owner = owner ^ (8 * (spot % 2))
    seq = owner * per + token // seq_len % per
    scale = 1.0 / (factor.shape[1] * seq_len)
    pick[...] = jnp.where(seq == flagged[...], scale, 0.0).astype(pick.dtype)
    for w, copy in enumerate(copies):
        copy.wait()
        rest = factor[w]
        for t in range(3):
            term = rest.astype(jnp.bfloat16)
            terms[w, t] = term
            rest = rest - term.astype(jnp.float32)


def early_kernel(seq_len, per, terms, u0, v, u1, u2, u3, white, mine, side):
    n = u0.shape[1]
    rows = []
    for w in range(2):
        white[w] = whiten(stack(u0[w], v[w], u2[w], u3[w]), terms.at[w])
        rows.append(white[w])
    left = {
        0: [r[: 2 * n] for r in rows],
        2: [r[2 * n : 3 * n] for r in rows],
        3: [r[3 * n : 4 * n] for r in rows],
    }
    tok = [[u[w] for w in range(2)] for u in (u0, u1, u2, u3)]
    mine[...] = jnp.zeros_like(mine)
    mine[:, 0 : 2 * n] = block(seq_len, left[0], [stack(u0[w], v[w]) for w in range(2)])
    for slot in (1, 2, 3):
        at = 2 * n * slot
        mine[:, at : at + n] = block(seq_len, left[0], tok[slot])
    side[...] = jnp.zeros_like(side)
    for row, slot, other in ((0, 2, 3), (2 * per, 3, 2)):
        for column in (1, other):
            at = 2 * n * (column - 1)
            side[row : row + per, at : at + n] = block(seq_len, left[slot], tok[column])


def core_kernel(seq_len, per, white, acts, grads, mine, side, mine_out, side_out):
    n = acts.shape[0]
    tok = [acts[...], grads[...]]
    mine_out[...] = mine[...]
    mine_out[:, 3 * n : 4 * n] = block(seq_len, [white[w, : 2 * n] for w in range(2)], tok)
    side_out[...] = side[...]
    got = block(seq_len, [white[w, 2 * n : 4 * n] for w in range(2)], tok)
    for i, row in enumerate((0, 2 * per)):
        side_out[row : row + per, n : 2 * n] = got[i * per : (i + 1) * per]


def z_kernel(
    seq_len, per, terms, white, u2, u1, acts, grads, v3, side, white3, side_out
):
    n = v3.shape[1]
    tok = [v3[w] for w in range(2)]
    core = (acts[...], grads[...])
    fresh = [whiten(tok[w], terms.at[w]) for w in range(2)]
    for w in range(2):
        white3[w] = fresh[w]
    side_out[...] = side[...]
    side_out[0:per, 5 * n : 6 * n] = block(
        seq_len, [white[w, 2 * n : 3 * n] for w in range(2)], tok
    )
    side_out[3 * per : 4 * per, 0 : 3 * n] = block(
        seq_len, fresh, [stack(u1[w], core[w], u2[w]) for w in range(2)]
    )


def return_kernel(
    seq_len, per, terms, white, white3, pick, side, u3, u1, v3, acts, grads, v2, by_z, by_x
):
    n = v2.shape[1]
    tok = [v2[w] for w in range(2)]
    core = (acts[...], grads[...])
    by_row = block(
        seq_len,
        [whiten(tok[w], terms.at[w]) for w in range(2)],
        [stack(u1[w], core[w], u3[w], v3[w]) for w in range(2)],
    )
    by_column = block(
        seq_len, [stack(white[w, 3 * n : 4 * n], white3[w]) for w in range(2)], tok
    )
    zeros = jnp.zeros((per, 2 * n), jnp.float32)
    none = jnp.zeros((per, 6 * n), jnp.float32)
    row = jnp.concatenate([by_row[:, : 2 * n], zeros, by_row[:, 2 * n :]], axis=1)
    lead = jnp.zeros((2 * per, 3 * n), jnp.float32)
    both = jnp.concatenate([lead, by_column, lead[:, : 2 * n]], axis=1)
    picked = pick_columns(side[...] + stack(none, row, both), pick.at[2 * n :])
    by_x[...] = picked[: 2 * per]
    by_z[...] = picked[2 * per :]


def rows_kernel(seq_len, per, white, pick, mine, v3, v2, out):
    n = v2.shape[1]
    left = [white[w, : 2 * n] for w in range(2)]
    got = block(seq_len, left, [stack(v2[w], v3[w]) for w in range(2)])
    zeros = jnp.zeros((2 * per, n), jnp.float32)
    late = jnp.concatenate([zeros] * 5 + [got[:, :n], zeros, got[:, n:]], axis=1)
    out[...] = pick_columns(mine[...] + late, pick)


def call(kernel, name, flops, limit, operands, specs, out_shape, scratch=(), **more):
    vmem = pl.BlockSpec(memory_space=pltpu.VMEM)
    return pl.pallas_call(
        kernel,
        out_shape=out_shape,
        in_specs=specs + [vmem] * (len(operands) - len(specs)),
        out_specs=jax.tree.map(lambda _: vmem, out_shape),
        scratch_shapes=scratch,
        compiler_params=pltpu.CompilerParams(vmem_limit_bytes=int(limit * 1024 * 1024)),
        cost_estimate=pl.CostEstimate(flops=flops, bytes_accessed=10**6, transcendentals=0),
        name=name,
        **more,
    )(*operands)


def paired(activations, out_grads, lengths, layer_ids, flagged, act_factor, grad_factor):
    size = 16
    per = lengths.shape[0]
    tokens, rank = activations.shape[1:]
    seq_len = tokens // per
    f32, bf16 = jnp.float32, jnp.bfloat16

    def send(x, to):
        return lax.ppermute(x, "blk", [(d, to(d)) for d in range(size)])

    def opposite(d):
        return d ^ 8

    ways = (z_near, lambda d: d ^ 2, lambda d: d ^ 1)
    hbm = pl.BlockSpec(memory_space=pltpu.HBM)
    vmem = pl.BlockSpec(memory_space=pltpu.VMEM)
    shape = jax.ShapeDtypeStruct
    columns = flagged.shape[0]
    unit = shape((2, tokens, rank), bf16)
    data = (activations, out_grads)
    lens = lengths.reshape(1, -1)
    copies = [pltpu.SemaphoreType.DMA((2,))]
    away = call(away_kernel, "away", 3 * 10**9, 53.71, data, [hbm, hbm], unit, copies)
    away = call(
        functools.partial(away_mask_kernel, seq_len),
        "away_mask",
        10**4,
        40,
        (lens, away),
        [],
        unit,
        input_output_aliases={1: 0},
    )
    v = send(away, opposite)
    away, ids = lax.optimization_barrier((away, layer_ids))
    terms, pick = call(
        functools.partial(setup_kernel, seq_len, per),
        "factor_terms",
        10**9,
        51,
        (ids, flagged.reshape(1, -1), act_factor, grad_factor),
        [pl.BlockSpec(memory_space=pltpu.SMEM), vmem, hbm, hbm],
        (shape((2, 3, rank, rank), bf16), shape((8 * tokens, columns), bf16)),
        [pltpu.VMEM((2, rank, rank), f32), pltpu.SemaphoreType.DMA((2,))],
    )
    away, terms, lens, *data = lax.optimization_barrier((away, terms, lens, *data))
    own = call(
        functools.partial(own_kernel, seq_len), "own", 10**9, 40, (lens, *data), [], unit
    )
    near = [send(own, to) for to in ways]
    v, terms, pick = lax.optimization_barrier((v, terms, pick))
    v3 = send(v, ways[0])
    v, near[0] = lax.optimization_barrier((v, near[0]))
    v2 = send(v, ways[1])
    whole = shape((2 * per, 8 * tokens), f32)
    sides = shape((4 * per, 6 * tokens), f32)
    rows = shape((2 * per, columns), f32)
    u3, u2, u1 = near

    def kernel(body, name, operands, out_shape, flops=10**9, **more):
        body = functools.partial(body, seq_len, per)
        return call(body, name, flops, 40, operands, [], out_shape, **more)

    white, mine, side = kernel(
        early_kernel,
        "early_pairs",
        (terms, own, v, u1, u2, u3),
        (shape((2, 4 * tokens, rank), bf16), whole, sides),
    )
    v, white = lax.optimization_barrier((v, white))
    v1 = [send(v[w], ways[2]) for w in range(2)]
    mine, side = kernel(
        core_kernel,
        "core_pairs",
        (white, *v1, mine, side),
        (whole, sides),
        flops=10**4,
        input_output_aliases={3: 0, 4: 1},
    )
    white3, side = kernel(
        z_kernel,
        "z_pairs",
        (terms, white, u2, u1, *v1, v3, side),
        (unit, sides),
        flops=10**4,
        input_output_aliases={7: 1},
    )
    by_z, by_x = kernel(
        return_kernel,
        "return_rows",
        (terms, white, white3, pick, side, u3, u1, v3, *v1, v2),
        (rows, rows),
    )
    mine = kernel(rows_kernel, "own_rows", (white, pick, mine, v3, v2), rows)
    half_sum = mine + send(by_z, z_near) + send(by_x, lambda d: d ^ 2)
    return half_sum[:per] + send(half_sum[per:], opposite)


def solution(mesh):
    in_specs = (
        P(None, ("grp", "blk"), None),
        P(None, ("grp", "blk"), None),
        P(("grp", "blk")),
        P("grp"),
        P("grp"),
        P(),
        P(),
    )
    out_specs = P(("grp", "blk"), None)
    shards = paired if mesh.shape["blk"] == 16 else gathered
    return jax.shard_map(shards, mesh=mesh, in_specs=in_specs, out_specs=out_specs, check_vma=False)
```
